32 devices in a mesh: parts: 2 (over y), attn: 8 (over z, x), ffn: 2 (over core).
Axes of the slice: x: 2, y: 2, z: 4, core: 2. Of those that a mesh axis runs over, the one named last changes fastest.
Arguments:
- queries: bfloat16 [128, 64, 128], P(('parts', 'attn'), 'ffn'), parts along dimension 0, may hold values from -10 to 10
- cache_keys: bfloat16 [128, 128, 4, 128], P(('parts', 'attn'), None, 'ffn'), parts along dimension 0, may hold values from -6 to 6
- stored_value_cache: bfloat16 [128, 128, 4, 128], P(('parts', 'attn'), None, 'ffn'), parts along dimension 0, may hold values from -6 to 6
- lengths: int32 [128], P(('parts', 'attn')), parts along dimension 0, may hold values from 2 to 128, as said below
- residual: bfloat16 [128, 8192], P(('parts', 'attn'), 'ffn'), parts along dimension 0, may hold values from -6 to 6
- target: int32 [128, 1], P('parts'), parts along dimension 0, may hold values from 0 to 15; in each aligned block of 64 rows (0 to 63, 64 to 127, ...) at most 8 rows name the same one
- gate_weight: bfloat16 [8192, 26624], P('ffn', 'attn'), may hold values from -0.0625 to 0.0625
- up_weight: bfloat16 [8192, 26624], P('ffn', 'attn'), may hold values from -0.0625 to 0.0625
- down_weight: bfloat16 [26624, 8192], P('attn', 'ffn'), may hold values from -0.0390625 to 0.0390625
Outputs:
- returned: bfloat16 [256, 8192], P(('parts', 'attn'), 'ffn'), parts along dimension 0
The draws below stay inside these ranges and needn't reach their ends.
There are 2 independent parts, one for each index of `parts`. The reference program is written for one: setup_inputs(seed, part) draws one part's arguments, and reference() takes and returns one part's arrays. A program takes and returns all parts, laid end to end along the dimension named above; an argument that names none is the same for every part. Nothing has to cross between parts.
Inputs may be any that keep to these rules, and one draw needn't show every extreme that they name: `lengths`: each device's requests lie in a bucket of 128, 64 or 32 positions, and one request of each device fills its bucket; some device's bucket is 128. `target`: no value is named by more than 8 requests, a bound that some block reaches.
All inputs are finite; a program needn't handle non-finite values.
Results may differ from the reference program's by a relative error of at most 0.006.
Values may be sent and summed in bfloat16 or wider, within the bound.
No kernel may reach another device: no remote copies, remote signals or barrier semaphores. Data moves between devices by JAX's collectives and lax.ppermute only.
A program may use at most 192 MiB of HBM per device.

```python
import math
import jax
import jax.numpy as jnp
import numpy as np
from jax import lax

QUERY_HEADS = 64
KEY_VALUE_HEADS = 4
HEAD_SIZE = 128
D = 8192
FF = 26624
ROWS_DEV = 8
MAX_CACHE_LENGTH = 128
CAP = 8
REQUEST_ROWS = 64
SLOTS = 128
N_ATTN = 8


def draw_cache_keys(key, part):
    key = jax.random.fold_in(key, 3)
    sampled_draw = jnp.clip(jax.random.normal(key, (REQUEST_ROWS, MAX_CACHE_LENGTH, KEY_VALUE_HEADS, HEAD_SIZE), jnp.float32), -6.0, 6.0)
    return sampled_draw.astype(jnp.bfloat16)


def draw_queries(key, part):
    key = jax.random.fold_in(key, 5)
    sampled_draw = jnp.clip(jax.random.normal(key, (REQUEST_ROWS, QUERY_HEADS, HEAD_SIZE), jnp.float32), -6.0, 6.0)
    return sampled_draw.astype(jnp.bfloat16)


def draw_lengths(key, part):
    key = jax.random.fold_in(key, 11)
    device_count = REQUEST_ROWS // ROWS_DEV
    subkeys = jax.random.split(key, 4)
    shrink = jax.random.randint(subkeys[0], (device_count,), 0, 3)
    bucket = jnp.array([MAX_CACHE_LENGTH, MAX_CACHE_LENGTH // 2, MAX_CACHE_LENGTH // 4], jnp.int32)[shrink]
    full_device = jax.random.randint(subkeys[1], (), 0, device_count)
    bucket = jnp.where(jnp.arange(device_count) == full_device, MAX_CACHE_LENGTH, bucket)
    per_row = jnp.repeat(bucket, ROWS_DEV)
    sampled_draw = jax.random.randint(subkeys[2], (REQUEST_ROWS,), 2, per_row + 1)
    longest = jax.random.randint(subkeys[3], (device_count,), 0, ROWS_DEV)
    at_bucket = jnp.arange(REQUEST_ROWS) % ROWS_DEV == jnp.repeat(longest, ROWS_DEV)
    return jnp.where(at_bucket, per_row, sampled_draw).astype(jnp.int32)


def block_scale(stream_key, shape, cuts, low, top_value):
    def one(axis_at, parts):
        heights = jax.random.uniform(jax.random.fold_in(jax.random.fold_in(stream_key, 6), axis_at), (parts,), jnp.float32, low / len(cuts), top_value / len(cuts))
        return jnp.repeat(jnp.exp(heights), shape[axis_at] // parts).reshape((-1,) + (1,) * (len(shape) - axis_at - 1))

    loudness = one(*cuts[0])
    for cut in cuts[1:]:
        loudness = loudness * one(*cut)
    return loudness


def deal_out(key, own, number, rows, count, top, limit, skew):
    sequence = jax.random.permutation(key, count)
    heavy_load, ordinary = portions_of(count, rows * top, limit, skew, True), portions_of(count, rows * top, limit, skew, False)
    places = jnp.arange(count)

    def named(sizes, rotation):
        used = int((sizes > 0).sum())
        fixed = max(1, used // 4)
        passed = fixed + (places - fixed + rotation * (used - fixed)) % max(1, count - fixed)
        return jnp.zeros((count,), jnp.int32).at[sequence[jnp.where(places < fixed, places, passed)]].set(jnp.asarray(sizes, jnp.int32))

    sizes = jnp.where(number % 4 == 0, named(heavy_load, number // 4), named(ordinary, number - number // 4 - 1))
    mixed = jax.random.permutation(jax.random.fold_in(own, 3), count)
    giver, taker = mixed[0:count // 2 * 2:2], mixed[1:count // 2 * 2:2]
    room = jnp.minimum(sizes[giver] - 1, limit - sizes[taker]) // 2
    room = jnp.where((giver == sequence[0]) | (taker == sequence[0]) | (sizes[taker] == 0), 0, jnp.maximum(room, 0))
    passed = jax.random.randint(jax.random.fold_in(own, 4), (count // 2,), 0, 1 << 20) % (room + 1)
    sizes = sizes.at[giver].add(-passed).at[taker].add(passed)
    members = jnp.searchsorted(jnp.cumsum(sizes), jnp.arange(rows * top), side="right").astype(jnp.int32)
    table = members.reshape(top, rows).T
    table = table[jax.random.permutation(jax.random.fold_in(own, 1), rows)]
    rotation = jax.random.randint(jax.random.fold_in(own, 2), (rows, 1), 0, top)
    return jnp.take_along_axis(table, (jnp.arange(top)[None, :] + rotation) % top, axis=1)


def portions_of(amount, total, bound, slope, full):
    weights = [(1 << 20) // math.isqrt(standing ** slope) + 1 for standing in range(1, amount + 1)]
    largest = bound if full else min(bound, max(-(-total // amount), total * weights[0] // sum(weights)))
    least = 1 if total - largest >= amount - 1 else 0
    counts, rest = [largest] + [least] * (amount - 1), total - largest - least * (amount - 1)
    while rest > 0:
        free = [i for i in range(1, amount) if counts[i] < largest] or [i for i in range(1, amount) if counts[i] < bound]
        whole, left = sum([weights[i] for i in free]), rest
        for i in free:
            addition = min(bound - counts[i], max(1, left * weights[i] // whole), rest)
            counts[i] = counts[i] + addition
            rest = rest - addition
    return np.array(counts)


def centred(own_key, shape, width, reach, pieces=(), held_as=jnp.bfloat16):
    loudness = block_scale(own_key, shape, pieces, -0.22, 0.18) if pieces else 1.0
    drawn = jax.random.normal(own_key, shape, jnp.float32) * width * loudness
    return jnp.minimum(jnp.maximum(drawn, -reach), reach).astype(held_as)


def setup_inputs(seed: int = 0, part: int = 0) -> dict:
    key_of = jax.random.split(jax.random.key(seed), 10)
    part_splits = jax.random.split(jax.random.fold_in(key_of[9], part), 10)
    queries = draw_queries(jax.random.fold_in(jax.random.fold_in(key_of[9], part), 71), part)
    cache_keys = draw_cache_keys(jax.random.fold_in(jax.random.fold_in(key_of[9], part), 71), part)
    stored_value_cache = centred(part_splits[2], (REQUEST_ROWS, MAX_CACHE_LENGTH, KEY_VALUE_HEADS, HEAD_SIZE), 1.0, 6.0, ((0, 8), (2, 2)))
    lengths = draw_lengths(jax.random.fold_in(jax.random.fold_in(key_of[9], part), 71), part)
    residual = centred(part_splits[4], (REQUEST_ROWS, D), 1.0, 6.0, ((0, 8), (1, 2)))
    target_keys = jax.random.split(jax.random.fold_in(part_splits[5], 1), REQUEST_ROWS // REQUEST_ROWS)
    target_turns = jax.random.permutation(jax.random.fold_in(part_splits[5], 3), REQUEST_ROWS // REQUEST_ROWS)
    target = jax.vmap(lambda own, number: deal_out(jax.random.fold_in(part_splits[5], 2), own, number, REQUEST_ROWS, 2 * N_ATTN, 1, CAP, 2))(target_keys, target_turns).reshape((REQUEST_ROWS, 1))
    gate_weight = centred(key_of[6], (D, FF), D ** -0.5, 0.0625, ((0, 2), (1, 8)))
    up_weight = centred(key_of[7], (D, FF), D ** -0.5, 0.0625, ((0, 2), (1, 8)))
    down_weight = centred(key_of[8], (FF, D), FF ** -0.5, 0.0390625, ((0, 8), (1, 2)))
    return {"queries": queries, "cache_keys": cache_keys, "stored_value_cache": stored_value_cache, "lengths": lengths, "residual": residual, "target": target, "gate_weight": gate_weight, "up_weight": up_weight, "down_weight": down_weight}


def slot_positions(column, destinations, capacity):
    onehot = (column[:, None] == jnp.arange(destinations, dtype=jnp.int32)[None, :]).astype(jnp.int32)
    before = jnp.cumsum(onehot, axis=0) - onehot
    slot_rank = lax.optimization_barrier(jnp.sum(before * onehot, axis=1))
    return (column * capacity + slot_rank).astype(jnp.int32)

def reference(queries, cache_keys, stored_value_cache, lengths, residual, target, gate_weight, up_weight, down_weight):
    heads_per_group = QUERY_HEADS // KEY_VALUE_HEADS
    score_scale = 1.0 / math.sqrt(HEAD_SIZE)
    grouped_heads = queries.astype(jnp.float32).reshape(REQUEST_ROWS, KEY_VALUE_HEADS, heads_per_group, HEAD_SIZE)
    scores = jnp.einsum('rgqd,rlgd->rgql', grouped_heads, cache_keys.astype(jnp.float32)) * score_scale
    in_cache = (jnp.arange(MAX_CACHE_LENGTH, dtype=jnp.int32)[None, :] < lengths[:, None])[:, None, None, :]
    masked = jnp.where(in_cache, scores, -1e+30)
    row_peak = lax.optimization_barrier(jnp.max(masked, axis=-1, keepdims=True))
    raw_weights = jnp.where(in_cache, jnp.exp(masked - row_peak), 0.0)
    weights_bf = (raw_weights / lax.optimization_barrier(jnp.sum(raw_weights, axis=-1, keepdims=True))).astype(jnp.bfloat16)
    attended = jnp.einsum('rgql,rlgd->rgqd', weights_bf.astype(jnp.float32), stored_value_cache.astype(jnp.float32)).reshape(REQUEST_ROWS, D)
    mixed_rows = (residual.astype(jnp.float32) + attended).astype(jnp.bfloat16)
    gate_sum = jnp.dot(mixed_rows, gate_weight, preferred_element_type=jnp.float32)
    up_sum = jnp.dot(mixed_rows, up_weight, preferred_element_type=jnp.float32)
    hidden = (jax.nn.silu(gate_sum) * up_sum).astype(jnp.bfloat16)
    down = jnp.dot(hidden, down_weight, preferred_element_type=jnp.float32)
    finished = (mixed_rows.astype(jnp.float32) + down).astype(jnp.bfloat16)
    position = slot_positions(target[:, 0], 2 * N_ATTN, CAP)
    return jnp.zeros((SLOTS, D), jnp.bfloat16).at[position].set(finished)
```

```python
import math

import jax
import jax.numpy as jnp
from jax import lax
from jax.sharding import PartitionSpec as P

AXIS = "attn"


def slot_positions(column, destinations, capacity):
    onehot = (column[:, None] == jnp.arange(destinations, dtype=jnp.int32)[None, :]).astype(
        jnp.int32
    )
    before = jnp.cumsum(onehot, axis=0) - onehot
    slot_rank = jnp.sum(before * onehot, axis=1)
    return column * capacity + slot_rank


def grid_of(devices):
    nx = 1
    while 4 * nx * nx < devices:
        nx *= 2
    if devices % nx:
        nx = 1
    return devices // nx, nx


def gather_rows(rows, devices):
    nz, nx = grid_of(devices)
    blocks = [rows]
    for shift in range(1, nz):
        perm = [
            (z * nx + x, ((z + shift) % nz) * nx + x) for z in range(nz) for x in range(nx)
        ]
        blocks.append(lax.ppermute(rows, AXIS, perm))
    column = jnp.stack(blocks)
    planes = [column]
    for shift in range(1, nx):
        perm = [
            (z * nx + x, z * nx + (x + shift) % nx) for z in range(nz) for x in range(nx)
        ]
        planes.append(lax.ppermute(column, AXIS, perm))
    table = jnp.stack(planes).reshape((devices,) + rows.shape)
    me = lax.axis_index(AXIS)
    my_z, my_x = me // nx, me % nx
    owner = jnp.arange(devices, dtype=jnp.int32)
    dz = (my_z - owner // nx) % nz
    dx = (my_x - owner % nx) % nx
    return jnp.take(table, dx * nz + dz, axis=0, mode="clip").reshape(
        (devices * rows.shape[0], rows.shape[1])
    )


def attend(queries, cache_keys, stored_value_cache, lengths, residual):
    rows_dev = cache_keys.shape[0]
    cache_len = cache_keys.shape[1]
    kv_local = cache_keys.shape[2]
    head_dim = cache_keys.shape[3]
    heads_per_group = queries.shape[1] // kv_local
    score_scale = 1.0 / math.sqrt(head_dim)
    grouped_heads = queries.reshape(rows_dev, kv_local, heads_per_group, head_dim)
    scores = (
        jnp.einsum("rgqd,rlgd->rgql", grouped_heads, cache_keys, preferred_element_type=jnp.float32)
        * score_scale
    )
    in_cache = (jnp.arange(cache_len, dtype=jnp.int32)[None, :] < lengths[:, None])[
        :, None, None, :
    ]
    masked = jnp.where(in_cache, scores, -1e30)
    row_peak = jnp.max(masked, axis=-1, keepdims=True)
    raw_weights = jnp.where(in_cache, jnp.exp(masked - row_peak), 0.0)
    weights_bf = (raw_weights / jnp.sum(raw_weights, axis=-1, keepdims=True)).astype(jnp.bfloat16)
    attended = jnp.einsum(
        "rgql,rlgd->rgqd", weights_bf, stored_value_cache, preferred_element_type=jnp.float32
    )
    attended = attended.reshape(rows_dev, kv_local * heads_per_group * head_dim)
    return (residual.astype(jnp.float32) + attended).astype(jnp.bfloat16)


def local(
    queries,
    cache_keys,
    stored_value_cache,
    lengths,
    residual,
    target,
    gate_weight,
    up_weight,
    down_weight,
):
    rows_dev = cache_keys.shape[0]
    devices = lax.axis_size(AXIS)
    me = lax.axis_index(AXIS)
    mixed_rows = attend(queries, cache_keys, stored_value_cache, lengths, residual)
    gathered = gather_rows(mixed_rows, devices)
    total_rows, features = gathered.shape
    gate_part = jnp.dot(gathered, gate_weight, preferred_element_type=jnp.float32)
    up_part = jnp.dot(gathered, up_weight, preferred_element_type=jnp.float32)
    mine = jnp.stack([gate_part, up_part])
    other = lax.ppermute(mine.astype(jnp.bfloat16), "ffn", [(0, 1), (1, 0)])
    gate_sum, up_sum = mine + other.astype(jnp.float32)
    hidden = (jax.nn.silu(gate_sum) * up_sum).astype(jnp.bfloat16)
    down = jnp.dot(hidden, down_weight, preferred_element_type=jnp.float32)
    share = features // devices
    pieces = jnp.moveaxis(
        down.astype(jnp.bfloat16).reshape(total_rows, devices, share), 1, 0
    )
    landed = lax.all_to_all(pieces, AXIS, split_axis=0, concat_axis=0)
    summed = jnp.sum(landed.astype(jnp.float32), axis=0)
    mixed_share = lax.dynamic_slice_in_dim(gathered, me * share, share, axis=1)
    finished = (mixed_share.astype(jnp.float32) + summed).astype(jnp.bfloat16)
    slot_count = 2 * devices * rows_dev
    position = slot_positions(target[:, 0], 2 * devices, rows_dev)
    chosen = (jnp.arange(slot_count, dtype=jnp.int32)[:, None] == position[None, :]).astype(
        jnp.bfloat16
    )
    slots = jnp.dot(chosen, finished, preferred_element_type=jnp.float32).astype(jnp.bfloat16)
    slots = slots.reshape(devices, 2 * rows_dev, share)
    mine_out = lax.all_to_all(slots, AXIS, split_axis=0, concat_axis=0)
    return jnp.moveaxis(mine_out, 0, 1).reshape(2 * rows_dev, features)


def solution(mesh):
    return jax.shard_map(
        local,
        mesh=mesh,
        in_specs=(
            P(("parts", "attn"), "ffn", None),
            P(("parts", "attn"), None, "ffn", None),
            P(("parts", "attn"), None, "ffn", None),
            P(("parts", "attn")),
            P(("parts", "attn"), "ffn"),
            P("parts", None),
            P("ffn", "attn"),
            P("ffn", "attn"),
            P("attn", "ffn"),
        ),
        out_specs=P(("parts", "attn"), "ffn"),
        check_vma=False,
    )
```

```python
import functools
import math

import jax
import jax.numpy as jnp
from jax import lax
from jax.experimental import pallas as pl
from jax.experimental.pallas import tpu as pltpu
from jax.sharding import PartitionSpec as P

AXIS = "attn"
TILE = 256
MIB = 1 << 20
VMEM = pl.BlockSpec(memory_space=pltpu.VMEM)
SMEM = pl.BlockSpec(memory_space=pltpu.SMEM)
ANY = pl.BlockSpec(memory_space=pl.ANY)
F32 = jnp.float32
BF16 = jnp.bfloat16


def params(mib):
    return pltpu.CompilerParams(vmem_limit_bytes=mib * MIB)


def cost(flops, moved):
    return pl.CostEstimate(flops=flops, bytes_accessed=moved, transcendentals=0)


def grid_of(devices):
    nx = 1
    while 4 * nx * nx < devices:
        nx *= 2
    if devices % nx:
        nx = 1
    return devices // nx, nx


def shift_z(devices, shift):
    nz, nx = grid_of(devices)
    return [(z * nx + x, ((z + shift) % nz) * nx + x) for z in range(nz) for x in range(nx)]


def shift_x(devices, shift):
    nz, nx = grid_of(devices)
    return [(z * nx + x, z * nx + (x + shift) % nx) for z in range(nz) for x in range(nx)]


def attend_kernel(kv, lengths, q_ref, k_ref, v_ref, res_ref, out_ref, att_ref):
    rows, heads, dim = q_ref.shape
    span = k_ref.shape[1]
    per_group = heads // kv
    column = lax.broadcasted_iota(jnp.int32, (heads, span), 1)
    head = lax.broadcasted_iota(jnp.int32, (heads, span), 0)
    right_group = (column % kv) == (head // per_group)
    position = column // kv
    for r in range(rows):
        scores = lax.dot_general(
            q_ref[r], k_ref[r], (((1,), (1,)), ((), ())), preferred_element_type=F32
        ) * (1.0 / math.sqrt(dim))
        live = right_group & (position < lengths[r])
        masked = jnp.where(live, scores, -1e30)
        peak = jnp.max(masked, axis=-1, keepdims=True)
        raw = jnp.where(live, jnp.exp(masked - peak), 0.0)
        probs = (raw / jnp.sum(raw, axis=-1, keepdims=True)).astype(BF16)
        att_ref[r * heads : (r + 1) * heads, :] = jnp.dot(
            probs, v_ref[r], preferred_element_type=F32
        )
    for h in range(heads):
        at = slice(h * dim, (h + 1) * dim)
        mine = att_ref[pl.ds(h, rows, stride=heads), :]
        out_ref[:, at] = (res_ref[:, at].astype(F32) + mine).astype(BF16)


def attend(queries, cache_keys, stored_value_cache, lengths, residual):
    rows, heads, dim = queries.shape
    kv = cache_keys.shape[2]
    span = cache_keys.shape[1] * kv
    return pl.pallas_call(
        functools.partial(attend_kernel, kv),
        out_shape=jax.ShapeDtypeStruct((rows, heads * dim), BF16),
        in_specs=[SMEM, VMEM, VMEM, VMEM, VMEM],
        out_specs=VMEM,
        scratch_shapes=[pltpu.VMEM((rows * heads, dim), F32)],
        compiler_params=params(8),
        cost_estimate=cost(rows * heads * span * dim * 4, rows * span * dim * 4),
        name="attention",
    )(
        lengths,
        queries,
        cache_keys.reshape(rows, span, dim),
        stored_value_cache.reshape(rows, span, dim),
        residual,
    )


def tile_at(index):
    return pl.ds(pl.multiple_of(index * TILE, TILE), TILE)


def gate_up_kernel(devices, depth, own_ref, far_ref, g_hbm, u_hbm, part_ref, rows_ref, buf, sems):
    nz, nx = grid_of(devices)
    columns = g_hbm.shape[1]
    tiles = columns // TILE

    def copies(i, slot):
        return (
            pltpu.make_async_copy(g_hbm.at[:, tile_at(i)], buf.at[slot, 0], sems.at[slot, 0]),
            pltpu.make_async_copy(u_hbm.at[:, tile_at(i)], buf.at[slot, 1], sems.at[slot, 1]),
        )

    for i in range(min(depth, tiles)):
        for c in copies(i, i):
            c.start()
    me = lax.axis_index(AXIS)
    my_z, my_x = me // nx, me % nx
    per = own_ref.shape[1]
    for dz in range(nz):
        z = lax.rem(my_z - dz + nz, nz)
        a, b = own_ref[dz].astype(F32), far_ref[dz].astype(F32)
        first = jnp.where(my_x == 0, a, b)
        second = jnp.where(my_x == 0, b, a)
        at = pl.ds(pl.multiple_of(z * (2 * per), 2 * per), 2 * per)
        rows_ref[at, :] = jnp.concatenate([first, second], axis=0).astype(BF16)

    def step(i, _):
        slot = lax.rem(i, depth)
        for kind, c in enumerate(copies(i, slot)):
            c.wait()
            part = jnp.dot(rows_ref[...], buf[slot, kind], preferred_element_type=F32)
            part_ref[kind, :, tile_at(i)] = part.astype(BF16)

        @pl.when(i + depth < tiles)
        def _():
            for c in copies(i + depth, slot):
                c.start()

        return 0

    lax.fori_loop(0, tiles, step, 0)


def gate_up(own, far, gate_weight, up_weight, devices):
    depth = 4
    total = devices * own.shape[1]
    features, columns = gate_weight.shape
    return pl.pallas_call(
        functools.partial(gate_up_kernel, devices, depth),
        out_shape=(
            jax.ShapeDtypeStruct((2, total, columns), BF16),
            jax.ShapeDtypeStruct((total, features), BF16),
        ),
        in_specs=[VMEM, VMEM, ANY, ANY],
        out_specs=(VMEM, VMEM),
        scratch_shapes=[
            pltpu.VMEM((depth, 2, features, TILE), BF16),
            pltpu.SemaphoreType.DMA((depth, 2)),
        ],
        compiler_params=params(24),
        cost_estimate=cost(4 * total * features * columns, 4 * features * columns),
        name="gate_up",
    )(own, far, gate_weight, up_weight)


def down_kernel(devices, mine, depth, hidden_of, w_hbm, out_ref, hidden_ref, buf, sems):
    nx = grid_of(devices)[1]
    half = out_ref.shape[1]
    tiles = half // TILE
    my_x = lax.axis_index(AXIS) % nx
    base = (my_x if mine else 1 - my_x) * tiles

    def copy(i, slot):
        return pltpu.make_async_copy(w_hbm.at[:, tile_at(base + i)], buf.at[slot], sems.at[slot])

    for i in range(min(depth, tiles)):
        copy(i, i).start()
    if len(hidden_of) == 2:
        own, other = hidden_of
        gate = own[0].astype(F32) + other[0].astype(F32)
        up = own[1].astype(F32) + other[1].astype(F32)
        hidden_ref[...] = (gate / (1.0 + jnp.exp(-gate)) * up).astype(BF16)
    else:
        hidden_ref = hidden_of[0]

    def step(i, _):
        slot = lax.rem(i, depth)
        copy(i, slot).wait()
        part = jnp.dot(hidden_ref[...], buf[slot], preferred_element_type=F32)
        out_ref[:, tile_at(i)] = part.astype(out_ref.dtype)

        @pl.when(i + depth < tiles)
        def _():
            copy(i + depth, slot).start()

        return 0

    lax.fori_loop(0, tiles, step, 0)


def down_far(own, other, down_weight, devices):
    depth = 6
    total = own.shape[1]
    columns, features = down_weight.shape

    def kernel(own_ref, other_ref, w_hbm, out_ref, hidden_ref, buf, sems):
        down_kernel(devices, False, depth, (own_ref, other_ref), w_hbm, out_ref, hidden_ref, buf, sems)

    return pl.pallas_call(
        kernel,
        out_shape=(
            jax.ShapeDtypeStruct((total, features // 2), BF16),
            jax.ShapeDtypeStruct((total, columns), BF16),
        ),
        in_specs=[VMEM, VMEM, ANY],
        out_specs=(VMEM, VMEM),
        scratch_shapes=[
            pltpu.VMEM((depth, columns, TILE), BF16),
            pltpu.SemaphoreType.DMA((depth,)),
        ],
        compiler_params=params(24),
        cost_estimate=cost(total * features * columns, features * columns),
        name="down_far_half",
    )(own, other, down_weight)


def down_near(hidden, down_weight, devices):
    depth = 6
    total = hidden.shape[0]
    columns, features = down_weight.shape

    def kernel(hidden_ref, w_hbm, out_ref, buf, sems):
        down_kernel(devices, True, depth, (hidden_ref,), w_hbm, out_ref, None, buf, sems)

    return pl.pallas_call(
        kernel,
        out_shape=jax.ShapeDtypeStruct((total, features // 2), F32),
        in_specs=[VMEM, ANY],
        out_specs=VMEM,
        scratch_shapes=[
            pltpu.VMEM((depth, columns, TILE), BF16),
            pltpu.SemaphoreType.DMA((depth,)),
        ],
        compiler_params=params(24),
        cost_estimate=cost(total * features * columns, features * columns),
        name="down_near_half",
    )(hidden, down_weight)


def pick(column_ref, row_ref, capacity, first_slot, slots):
    total = row_ref.shape[1]
    same = column_ref[...] == row_ref[...]
    earlier = lax.broadcasted_iota(jnp.int32, (total, total), 0) < lax.broadcasted_iota(
        jnp.int32, (total, total), 1
    )
    rank = jnp.sum((same & earlier).astype(F32), axis=0, keepdims=True).astype(jnp.int32)
    position = row_ref[...] * capacity + rank
    slot = first_slot + lax.broadcasted_iota(jnp.int32, (slots, total), 0)
    return (slot == position).astype(F32).astype(BF16)


def to_slots_kernel(devices, capacity, column_ref, row_ref, near_ref, far_ref, own_ref, *sends):
    nz, nx = grid_of(devices)
    my_z = lax.axis_index(AXIS) // nx
    slots = own_ref.shape[0]
    total = near_ref[...] + far_ref[...].astype(F32)
    rounded = total.astype(BF16)
    for dz, send_ref in enumerate((own_ref,) + sends):
        z = lax.rem(my_z + dz, nz)
        chosen = pick(column_ref, row_ref, capacity, z * slots, slots)
        if dz:
            send_ref[...] = jnp.dot(chosen, rounded, preferred_element_type=F32).astype(BF16)
        else:
            high = rounded.astype(F32)
            low = (total - high).astype(BF16)
            own_ref[...] = jnp.dot(chosen, rounded, preferred_element_type=F32) + jnp.dot(
                chosen, low, preferred_element_type=F32
            )


def to_slots(column, row, near, far, devices, capacity):
    nz, nx = grid_of(devices)
    slots = nx * 2 * capacity
    width = near.shape[1]
    return pl.pallas_call(
        functools.partial(to_slots_kernel, devices, capacity),
        out_shape=(jax.ShapeDtypeStruct((slots, width), F32),)
        + (jax.ShapeDtypeStruct((slots, width), BF16),) * (nz - 1),
        in_specs=[VMEM] * 4,
        out_specs=(VMEM,) * nz,
        compiler_params=params(8),
        name="to_slots",
    )(column, row, near, far)


def finish_kernel(devices, capacity, column_ref, row_ref, rows_ref, own_ref, *refs):
    *landed, keep_ref, send_ref = refs
    nz, nx = grid_of(devices)
    me = lax.axis_index(AXIS)
    my_z, my_x = me // nx, me % nx
    slots, width = own_ref.shape
    chosen = pick(column_ref, row_ref, capacity, my_z * slots, slots)
    mixed = rows_ref[:, pl.ds(pl.multiple_of(my_x * width, width), width)]
    total = own_ref[...]
    for ref in landed:
        total = total + ref[...].astype(F32)
    done = jnp.dot(chosen, mixed, preferred_element_type=F32) + total
    half = slots // 2
    first, second = done[:half], done[half:]
    keep_ref[...] = jnp.where(my_x == 0, first, second).astype(BF16)
    send_ref[...] = jnp.where(my_x == 0, second, first).astype(BF16)


def finish(column, row, rows, own, landed, devices, capacity):
    slots, width = own.shape
    shape = jax.ShapeDtypeStruct((slots // 2, width), BF16)
    return pl.pallas_call(
        functools.partial(finish_kernel, devices, capacity),
        out_shape=(shape, shape),
        in_specs=[VMEM] * (4 + len(landed)),
        out_specs=(VMEM, VMEM),
        compiler_params=params(8),
        name="finish",
    )(column, row, rows, own, *landed)


def join_kernel(nx, keep_ref, other_ref, out_ref):
    my_x = lax.axis_index(AXIS) % nx
    width = keep_ref.shape[1]
    out_ref[:, :width] = jnp.where(my_x == 0, keep_ref[...], other_ref[...])
    out_ref[:, width:] = jnp.where(my_x == 0, other_ref[...], keep_ref[...])


def join(keep, other, devices):
    slots, width = keep.shape
    return pl.pallas_call(
        functools.partial(join_kernel, grid_of(devices)[1]),
        out_shape=jax.ShapeDtypeStruct((slots, 2 * width), BF16),
        in_specs=[VMEM, VMEM],
        out_specs=VMEM,
        compiler_params=params(8),
        name="join_halves",
    )(keep, other)


def slot_positions(column, destinations, capacity):
    onehot = (column[:, None] == jnp.arange(destinations, dtype=jnp.int32)[None, :]).astype(
        jnp.int32
    )
    before = jnp.cumsum(onehot, axis=0) - onehot
    slot_rank = jnp.sum(before * onehot, axis=1)
    return column * capacity + slot_rank


def plain(mixed_rows, target, gate_weight, up_weight, down_weight, devices):
    rows_dev, features = mixed_rows.shape
    me = lax.axis_index(AXIS)
    gathered = lax.all_gather(mixed_rows, AXIS, axis=0, tiled=True)
    mine = jnp.stack(
        [
            jnp.dot(gathered, gate_weight, preferred_element_type=F32),
            jnp.dot(gathered, up_weight, preferred_element_type=F32),
        ]
    )
    other = lax.ppermute(mine.astype(BF16), "ffn", [(0, 1), (1, 0)])
    gate_sum, up_sum = mine + other.astype(F32)
    hidden = (jax.nn.silu(gate_sum) * up_sum).astype(BF16)
    down = jnp.dot(hidden, down_weight, preferred_element_type=F32)
    share = features // devices
    landed = lax.all_to_all(
        jnp.moveaxis(down.astype(BF16).reshape(-1, devices, share), 1, 0), AXIS, 0, 0
    )
    summed = jnp.sum(landed.astype(F32), axis=0)
    mixed_share = lax.dynamic_slice_in_dim(gathered, me * share, share, axis=1)
    finished = (mixed_share.astype(F32) + summed).astype(BF16)
    slot_count = 2 * devices * rows_dev
    position = slot_positions(target[:, 0], 2 * devices, rows_dev)
    chosen = (jnp.arange(slot_count, dtype=jnp.int32)[:, None] == position[None, :]).astype(BF16)
    slots = jnp.dot(chosen, finished, preferred_element_type=F32).astype(BF16)
    slots = slots.reshape(devices, 2 * rows_dev, share)
    mine_out = lax.all_to_all(slots, AXIS, split_axis=0, concat_axis=0)
    return jnp.moveaxis(mine_out, 0, 1).reshape(2 * rows_dev, features)


def local(
    queries,
    cache_keys,
    stored_value_cache,
    lengths,
    residual,
    target,
    gate_weight,
    up_weight,
    down_weight,
):
    devices = lax.axis_size(AXIS)
    nz, nx = grid_of(devices)
    capacity = cache_keys.shape[0]
    mixed_rows = attend(queries, cache_keys, stored_value_cache, lengths, residual)
    columns, features = down_weight.shape
    if nx != 2 or columns % TILE or features % (2 * TILE):
        return plain(mixed_rows, target, gate_weight, up_weight, down_weight, devices)

    own = jnp.stack(
        [mixed_rows]
        + [lax.ppermute(mixed_rows, AXIS, shift_z(devices, shift)) for shift in range(1, nz)]
    )
    far = lax.ppermute(own, AXIS, shift_x(devices, 1))
    part, rows = gate_up(own, far, gate_weight, up_weight, devices)
    other = lax.ppermute(part, "ffn", [(0, 1), (1, 0)])
    far_half, hidden = down_far(part, other, down_weight, devices)
    arrived = lax.ppermute(far_half, AXIS, shift_x(devices, 1))
    near_half = down_near(hidden, down_weight, devices)
    row = target.reshape(1, -1)
    own_slots, *sends = to_slots(target, row, near_half, arrived, devices, capacity)
    landed = [
        lax.ppermute(send, AXIS, shift_z(devices, dz + 1)) for dz, send in enumerate(sends)
    ]
    keep, send = finish(target, row, rows, own_slots, landed, devices, capacity)
    return join(keep, lax.ppermute(send, AXIS, shift_x(devices, 1)), devices)


def solution(mesh):
    return jax.shard_map(
        local,
        mesh=mesh,
        in_specs=(
            P(("parts", "attn"), "ffn", None),
            P(("parts", "attn"), None, "ffn", None),
            P(("parts", "attn"), None, "ffn", None),
            P(("parts", "attn")),
            P(("parts", "attn"), "ffn"),
            P("parts", None),
            P("ffn", "attn"),
            P("ffn", "attn"),
            P("attn", "ffn"),
        ),
        out_specs=P(("parts", "attn"), "ffn"),
        check_vma=False,
    )
```

```python
import functools
import math

import jax
import jax.numpy as jnp
from jax import lax
from jax.experimental import pallas as pl
from jax.experimental.pallas import tpu as pltpu
from jax.sharding import PartitionSpec as P

AXIS = "attn"
TILE = 256
MIB = 1 << 20
VMEM = pl.BlockSpec(memory_space=pltpu.VMEM)
SMEM = pl.BlockSpec(memory_space=pltpu.SMEM)
ANY = pl.BlockSpec(memory_space=pl.ANY)
F32 = jnp.float32
BF16 = jnp.bfloat16


def params(mib):
    return pltpu.CompilerParams(vmem_limit_bytes=mib * MIB)


def cost(flops, moved):
    return pl.CostEstimate(flops=flops, bytes_accessed=moved, transcendentals=0)


def grid_of(devices):
    nx = 1
    while 4 * nx * nx < devices:
        nx *= 2
    if devices % nx:
        nx = 1
    return devices // nx, nx


def swap_z(devices, bits):
    nz, nx = grid_of(devices)
    return [(z * nx + x, (z ^ bits) * nx + x) for z in range(nz) for x in range(nx)]


def swap_x(devices):
    nz, nx = grid_of(devices)
    return [(z * nx + x, z * nx + (x ^ 1)) for z in range(nz) for x in range(nx)]


def attend_kernel(
    kv, lengths, q_hbm, k_hbm, v_hbm, res_ref, out_ref, att_ref, q_ref, k_ref, v_ref, sems
):
    rows, heads, dim = q_ref.shape
    span = k_ref.shape[1]
    loads = [
        pltpu.make_async_copy(source, held, sems.at[i])
        for i, (source, held) in enumerate(
            ((q_hbm, q_ref), (k_hbm, k_ref), (v_hbm, v_ref))
        )
    ]
    for load in loads:
        load.start()
    per_group = heads // kv
    column = lax.broadcasted_iota(jnp.int32, (heads, span), 1)
    head = lax.broadcasted_iota(jnp.int32, (heads, span), 0)
    right_group = (column % kv) == (head // per_group)
    position = column // kv
    for load in loads:
        load.wait()
    for r in range(rows):
        scores = lax.dot_general(
            q_ref[r], k_ref[r], (((1,), (1,)), ((), ())), preferred_element_type=F32
        ) * (1.0 / math.sqrt(dim))
        live = right_group & (position < lengths[r])
        masked = jnp.where(live, scores, -1e30)
        peak = jnp.max(masked, axis=-1, keepdims=True)
        raw = jnp.where(live, jnp.exp(masked - peak), 0.0)
        probs = (raw / jnp.sum(raw, axis=-1, keepdims=True)).astype(BF16)
        att_ref[r * heads : (r + 1) * heads, :] = jnp.dot(
            probs, v_ref[r], preferred_element_type=F32
        )
    for h in range(heads):
        at = slice(h * dim, (h + 1) * dim)
        mine = att_ref[pl.ds(h, rows, stride=heads), :]
        out_ref[:, at] = (res_ref[:, at].astype(F32) + mine).astype(BF16)


def attend(queries, cache_keys, stored_value_cache, lengths, residual):
    rows, heads, dim = queries.shape
    kv = cache_keys.shape[2]
    span = cache_keys.shape[1] * kv
    return pl.pallas_call(
        functools.partial(attend_kernel, kv),
        out_shape=jax.ShapeDtypeStruct((rows, heads * dim), BF16),
        in_specs=[SMEM, ANY, ANY, ANY, VMEM],
        out_specs=VMEM,
        scratch_shapes=[
            pltpu.VMEM((rows * heads, dim), F32),
            pltpu.VMEM(queries.shape, BF16),
            pltpu.VMEM((rows, span, dim), BF16),
            pltpu.VMEM((rows, span, dim), BF16),
            pltpu.SemaphoreType.DMA((3,)),
        ],
        compiler_params=params(56),
        cost_estimate=cost(rows * heads * span * dim * 4, rows * span * dim * 4),
        name="attention",
    )(
        lengths,
        queries,
        cache_keys.reshape(rows, span, dim),
        stored_value_cache.reshape(rows, span, dim),
        residual,
    )


def tile_at(index):
    return pl.ds(pl.multiple_of(index * TILE, TILE), TILE)


def gate_up_kernel(
    devices, depth, deep, own_ref, far_ref, g_hbm, u_hbm, part_ref, rows_ref, total_ref, buf, sems
):
    nz, nx = grid_of(devices)
    steps = g_hbm.shape[0] // deep

    def band(i):
        return pl.ds(pl.multiple_of(i * deep, deep), deep)

    def copies(i, slot):
        return (
            pltpu.make_async_copy(g_hbm.at[band(i)], buf.at[slot, 0], sems.at[slot, 0]),
            pltpu.make_async_copy(u_hbm.at[band(i)], buf.at[slot, 1], sems.at[slot, 1]),
        )

    for i in range(min(depth, steps)):
        for c in copies(i, i):
            c.start()
    me = lax.axis_index(AXIS)
    my_z, my_x = me // nx, me % nx
    per = own_ref.shape[1]
    for dz in range(nz):
        z = my_z ^ dz
        a, b = own_ref[dz].astype(F32), far_ref[dz].astype(F32)
        first = jnp.where(my_x == 0, a, b)
        second = jnp.where(my_x == 0, b, a)
        at = pl.ds(pl.multiple_of(z * (2 * per), 2 * per), 2 * per)
        rows_ref[at, :] = jnp.concatenate([first, second], axis=0).astype(BF16)
    total_ref[...] = jnp.zeros_like(total_ref)

    def step(i, _):
        slot = lax.rem(i, depth)
        for kind, c in enumerate(copies(i, slot)):
            c.wait()
            total_ref[kind] += jnp.dot(
                rows_ref[:, band(i)], buf[slot, kind], preferred_element_type=F32
            )

        @pl.when(i + depth < steps)
        def _():
            for c in copies(i + depth, slot):
                c.start()

        return 0

    lax.fori_loop(0, steps, step, 0)
    part_ref[...] = total_ref[...].astype(BF16)


def gate_up(own, far, gate_weight, up_weight, devices):
    depth, deep = 3, 2 * TILE
    total = devices * own.shape[1]
    features, columns = gate_weight.shape
    return pl.pallas_call(
        functools.partial(gate_up_kernel, devices, depth, deep),
        out_shape=(
            jax.ShapeDtypeStruct((2, total, columns), BF16),
            jax.ShapeDtypeStruct((total, features), BF16),
        ),
        in_specs=[VMEM, VMEM, ANY, ANY],
        out_specs=(VMEM, VMEM),
        scratch_shapes=[
            pltpu.VMEM((2, total, columns), F32),
            pltpu.VMEM((depth, 2, deep, columns), BF16),
            pltpu.SemaphoreType.DMA((depth, 2)),
        ],
        compiler_params=params(44),
        cost_estimate=cost(4 * total * features * columns, 4 * features * columns),
        name="gate_up",
    )(own, far, gate_weight, up_weight)


def down_far_kernel(
    devices, depth, own_ref, other_ref, w_hbm, out_ref, hidden_ref, total_ref, buf, sems
):
    nx = grid_of(devices)[1]
    half = out_ref.shape[1]
    steps = w_hbm.shape[0] // TILE
    base = pl.multiple_of((1 - lax.axis_index(AXIS) % nx) * half, half)

    def copy(i, slot):
        return pltpu.make_async_copy(
            w_hbm.at[tile_at(i), pl.ds(base, half)], buf.at[slot], sems.at[slot]
        )

    for i in range(min(depth, steps)):
        copy(i, i).start()
    gate = own_ref[0].astype(F32) + other_ref[0].astype(F32)
    up = own_ref[1].astype(F32) + other_ref[1].astype(F32)
    hidden_ref[...] = (gate / (1.0 + jnp.exp(-gate)) * up).astype(BF16)
    total_ref[...] = jnp.zeros_like(total_ref)

    def step(i, _):
        slot = lax.rem(i, depth)
        copy(i, slot).wait()
        total_ref[...] += jnp.dot(
            hidden_ref[:, tile_at(i)], buf[slot], preferred_element_type=F32
        )

        @pl.when(i + depth < steps)
        def _():
            copy(i + depth, slot).start()

        return 0

    lax.fori_loop(0, steps, step, 0)
    out_ref[...] = total_ref[...].astype(BF16)


def down_far(own, other, down_weight, devices):
    depth = 10
    total = own.shape[1]
    columns, features = down_weight.shape
    return pl.pallas_call(
        functools.partial(down_far_kernel, devices, depth),
        out_shape=(
            jax.ShapeDtypeStruct((total, features // 2), BF16),
            jax.ShapeDtypeStruct((total, columns), BF16),
        ),
        in_specs=[VMEM, VMEM, ANY],
        out_specs=(VMEM, VMEM),
        scratch_shapes=[
            pltpu.VMEM((total, features // 2), F32),
            pltpu.VMEM((depth, TILE, features // 2), BF16),
            pltpu.SemaphoreType.DMA((depth,)),
        ],
        compiler_params=params(44),
        cost_estimate=cost(total * features * columns, features * columns),
        name="down_far_half",
    )(own, other, down_weight)


def down_near_kernel(devices, hidden_ref, w_hbm, out_ref, buf, sems):
    nx = grid_of(devices)[1]
    half = out_ref.shape[1]
    wide = buf.shape[2]
    base = (lax.axis_index(AXIS) % nx) * half
    copies = [
        pltpu.make_async_copy(
            w_hbm.at[:, pl.ds(pl.multiple_of(base + i * wide, wide), wide)],
            buf.at[i],
            sems.at[i],
        )
        for i in range(half // wide)
    ]
    for c in copies:
        c.start()
    for i, c in enumerate(copies):
        c.wait()
        out_ref[:, i * wide : (i + 1) * wide] = jnp.dot(
            hidden_ref[...], buf[i], preferred_element_type=F32
        )


def down_near(hidden, down_weight, devices):
    total = hidden.shape[0]
    columns, features = down_weight.shape
    wide = 2 * TILE
    tiles = features // 2 // wide
    return pl.pallas_call(
        functools.partial(down_near_kernel, devices),
        out_shape=jax.ShapeDtypeStruct((total, features // 2), F32),
        in_specs=[VMEM, ANY],
        out_specs=VMEM,
        scratch_shapes=[
            pltpu.VMEM((tiles, columns, wide), BF16),
            pltpu.SemaphoreType.DMA((tiles,)),
        ],
        compiler_params=params(44),
        cost_estimate=cost(total * features * columns, features * columns),
        name="down_near_half",
    )(hidden, down_weight)


def pick(column_ref, row_ref, capacity, first_slot, slots):
    total = row_ref.shape[1]
    same = column_ref[...] == row_ref[...]
    earlier = lax.broadcasted_iota(jnp.int32, (total, total), 0) < lax.broadcasted_iota(
        jnp.int32, (total, total), 1
    )
    rank = jnp.sum((same & earlier).astype(F32), axis=0, keepdims=True).astype(jnp.int32)
    position = row_ref[...] * capacity + rank
    slot = first_slot + lax.broadcasted_iota(jnp.int32, (slots, total), 0)
    return (slot == position).astype(F32).astype(BF16)


def to_slots_kernel(devices, capacity, column_ref, row_ref, near_ref, far_ref, own_ref, *sends):
    nz, nx = grid_of(devices)
    my_z = lax.axis_index(AXIS) // nx
    slots = own_ref.shape[0]
    total = near_ref[...] + far_ref[...].astype(F32)
    rounded = total.astype(BF16)
    for dz, send_ref in enumerate((own_ref,) + sends):
        z = my_z ^ dz
        chosen = pick(column_ref, row_ref, capacity, z * slots, slots)
        if dz:
            send_ref[...] = jnp.dot(chosen, rounded, preferred_element_type=F32).astype(BF16)
        else:
            high = rounded.astype(F32)
            low = (total - high).astype(BF16)
            own_ref[...] = jnp.dot(chosen, rounded, preferred_element_type=F32) + jnp.dot(
                chosen, low, preferred_element_type=F32
            )


def to_slots(column, row, near, far, devices, capacity):
    nz, nx = grid_of(devices)
    slots = nx * 2 * capacity
    width = near.shape[1]
    return pl.pallas_call(
        functools.partial(to_slots_kernel, devices, capacity),
        out_shape=(jax.ShapeDtypeStruct((slots, width), F32),)
        + (jax.ShapeDtypeStruct((slots, width), BF16),) * (nz - 1),
        in_specs=[VMEM] * 4,
        out_specs=(VMEM,) * nz,
        compiler_params=params(8),
        name="to_slots",
    )(column, row, near, far)


def finish_kernel(devices, capacity, column_ref, row_ref, rows_ref, own_ref, *refs):
    *landed, keep_ref, send_ref = refs
    nz, nx = grid_of(devices)
    me = lax.axis_index(AXIS)
    my_z, my_x = me // nx, me % nx
    slots, width = own_ref.shape
    chosen = pick(column_ref, row_ref, capacity, my_z * slots, slots)
    mixed = rows_ref[:, pl.ds(pl.multiple_of(my_x * width, width), width)]
    total = own_ref[...]
    for ref in landed:
        total = total + ref[...].astype(F32)
    done = jnp.dot(chosen, mixed, preferred_element_type=F32) + total
    half = slots // 2
    first, second = done[:half], done[half:]
    keep_ref[...] = jnp.where(my_x == 0, first, second).astype(BF16)
    send_ref[...] = jnp.where(my_x == 0, second, first).astype(BF16)


def finish(column, row, rows, own, landed, devices, capacity):
    slots, width = own.shape
    shape = jax.ShapeDtypeStruct((slots // 2, width), BF16)
    return pl.pallas_call(
        functools.partial(finish_kernel, devices, capacity),
        out_shape=(shape, shape),
        in_specs=[VMEM] * (4 + len(landed)),
        out_specs=(VMEM, VMEM),
        compiler_params=params(8),
        name="finish",
    )(column, row, rows, own, *landed)


def join_kernel(nx, keep_ref, other_ref, out_ref):
    my_x = lax.axis_index(AXIS) % nx
    width = keep_ref.shape[1]
    out_ref[:, :width] = jnp.where(my_x == 0, keep_ref[...], other_ref[...])
    out_ref[:, width:] = jnp.where(my_x == 0, other_ref[...], keep_ref[...])


def join(keep, other, devices):
    slots, width = keep.shape
    return pl.pallas_call(
        functools.partial(join_kernel, grid_of(devices)[1]),
        out_shape=jax.ShapeDtypeStruct((slots, 2 * width), BF16),
        in_specs=[VMEM, VMEM],
        out_specs=VMEM,
        compiler_params=params(8),
        name="join_halves",
    )(keep, other)


def slot_positions(column, destinations, capacity):
    onehot = (column[:, None] == jnp.arange(destinations, dtype=jnp.int32)[None, :]).astype(
        jnp.int32
    )
    before = jnp.cumsum(onehot, axis=0) - onehot
    slot_rank = jnp.sum(before * onehot, axis=1)
    return column * capacity + slot_rank


def plain(mixed_rows, target, gate_weight, up_weight, down_weight, devices):
    rows_dev, features = mixed_rows.shape
    me = lax.axis_index(AXIS)
    gathered = lax.all_gather(mixed_rows, AXIS, axis=0, tiled=True)
    mine = jnp.stack(
        [
            jnp.dot(gathered, gate_weight, preferred_element_type=F32),
            jnp.dot(gathered, up_weight, preferred_element_type=F32),
        ]
    )
    other = lax.ppermute(mine.astype(BF16), "ffn", [(0, 1), (1, 0)])
    gate_sum, up_sum = mine + other.astype(F32)
    hidden = (jax.nn.silu(gate_sum) * up_sum).astype(BF16)
    down = jnp.dot(hidden, down_weight, preferred_element_type=F32)
    share = features // devices
    landed = lax.all_to_all(
        jnp.moveaxis(down.astype(BF16).reshape(-1, devices, share), 1, 0), AXIS, 0, 0
    )
    summed = jnp.sum(landed.astype(F32), axis=0)
    mixed_share = lax.dynamic_slice_in_dim(gathered, me * share, share, axis=1)
    finished = (mixed_share.astype(F32) + summed).astype(BF16)
    slot_count = 2 * devices * rows_dev
    position = slot_positions(target[:, 0], 2 * devices, rows_dev)
    chosen = (jnp.arange(slot_count, dtype=jnp.int32)[:, None] == position[None, :]).astype(BF16)
    slots = jnp.dot(chosen, finished, preferred_element_type=F32).astype(BF16)
    slots = slots.reshape(devices, 2 * rows_dev, share)
    mine_out = lax.all_to_all(slots, AXIS, split_axis=0, concat_axis=0)
    return jnp.moveaxis(mine_out, 0, 1).reshape(2 * rows_dev, features)


def local(
    queries,
    cache_keys,
    stored_value_cache,
    lengths,
    residual,
    target,
    gate_weight,
    up_weight,
    down_weight,
):
    devices = lax.axis_size(AXIS)
    nz, nx = grid_of(devices)
    capacity = cache_keys.shape[0]
    mixed_rows = attend(queries, cache_keys, stored_value_cache, lengths, residual)
    columns, features = down_weight.shape
    if nx != 2 or nz & (nz - 1) or columns % TILE or features % (4 * TILE):
        return plain(mixed_rows, target, gate_weight, up_weight, down_weight, devices)

    own = jnp.stack(
        [mixed_rows]
        + [lax.ppermute(mixed_rows, AXIS, swap_z(devices, bits)) for bits in range(1, nz)]
    )
    far = lax.ppermute(own, AXIS, swap_x(devices))
    part, rows = gate_up(own, far, gate_weight, up_weight, devices)
    other = lax.ppermute(part, "ffn", [(0, 1), (1, 0)])
    far_half, hidden = down_far(part, other, down_weight, devices)
    arrived = lax.ppermute(far_half, AXIS, swap_x(devices))
    near_half = down_near(hidden, down_weight, devices)
    row = target.reshape(1, -1)
    own_slots, *sends = to_slots(target, row, near_half, arrived, devices, capacity)
    landed = [
        lax.ppermute(send, AXIS, swap_z(devices, bits + 1)) for bits, send in enumerate(sends)
    ]
    keep, send = finish(target, row, rows, own_slots, landed, devices, capacity)
    return join(keep, lax.ppermute(send, AXIS, swap_x(devices)), devices)


def solution(mesh):
    return jax.shard_map(
        local,
        mesh=mesh,
        in_specs=(
            P(("parts", "attn"), "ffn", None),
            P(("parts", "attn"), None, "ffn", None),
            P(("parts", "attn"), None, "ffn", None),
            P(("parts", "attn")),
            P(("parts", "attn"), "ffn"),
            P("parts", None),
            P("ffn", "attn"),
            P("ffn", "attn"),
            P("attn", "ffn"),
        ),
        out_specs=P(("parts", "attn"), "ffn"),
        check_vma=False,
    )
```

```python
import functools
import math

import jax
import jax.numpy as jnp
from jax import lax
from jax.experimental import pallas as pl
from jax.experimental.pallas import tpu as pltpu
from jax.sharding import PartitionSpec as P

AXIS = "attn"
TILE = 256
BAND = 256
MIB = 1 << 20
VMEM = pl.BlockSpec(memory_space=pltpu.VMEM)
SMEM = pl.BlockSpec(memory_space=pltpu.SMEM)
ANY = pl.BlockSpec(memory_space=pl.ANY)
HBM = pl.BlockSpec(memory_space=pltpu.HBM)
F32 = jnp.float32
BF16 = jnp.bfloat16


def params(mib):
    return pltpu.CompilerParams(vmem_limit_bytes=mib * MIB)


def in_vmem(array):
    return pltpu.with_memory_space_constraint(array, pltpu.VMEM)


def in_hbm(array):
    return pltpu.with_memory_space_constraint(array, pltpu.HBM)


def cost(flops, moved):
    return pl.CostEstimate(flops=flops, bytes_accessed=moved, transcendentals=0)


def grid_of(devices):
    nx = 1
    while 4 * nx * nx < devices:
        nx *= 2
    if devices % nx:
        nx = 1
    return devices // nx, nx


def swap_z(devices, bits):
    nz, nx = grid_of(devices)
    return [(z * nx + x, (z ^ bits) * nx + x) for z in range(nz) for x in range(nx)]


def swap_x(devices):
    nz, nx = grid_of(devices)
    return [(z * nx + x, z * nx + (x ^ 1)) for z in range(nz) for x in range(nx)]


def attend_kernel(kv, bands, lengths, q_hbm, k_hbm, v_hbm, res_ref, *refs):
    weights = ()
    if bands:
        g_hbm, u_hbm, out_ref, held_ref, *refs, band_sems = refs
        weights = band_copies(g_hbm, u_hbm, held_ref, band_sems, 0)
    else:
        out_ref, *refs = refs
    att_ref, scores_ref, probs_ref, q_ref, k_ref, v_ref, sems = refs
    rows, heads, dim = q_ref.shape
    span = k_ref.shape[1]
    per_group = heads // kv
    loads = [
        pltpu.make_async_copy(source, held, sems.at[i])
        for i, (source, held) in enumerate(((q_hbm, q_ref), (k_hbm, k_ref), (v_hbm, v_ref)))
    ]
    for load in loads:
        load.start()
    for c in weights:
        c.start()
    column = lax.broadcasted_iota(jnp.int32, (heads, span), 1)
    head = lax.broadcasted_iota(jnp.int32, (heads, span), 0)
    right_group = (column % kv) == (head // per_group)
    position = column // kv

    def at(r):
        return slice(r * heads, (r + 1) * heads)

    loads[0].wait()
    loads[1].wait()
    for r in range(rows):
        scores = lax.dot_general(
            q_ref[r], k_ref[r], (((1,), (1,)), ((), ())), preferred_element_type=F32
        ) * (1.0 / math.sqrt(dim))
        scores_ref[at(r), :] = jnp.where(right_group & (position < lengths[r]), scores, -1e30)
    for r in range(rows):
        scores = scores_ref[at(r), :]
        raw = jnp.exp(scores - jnp.max(scores, axis=-1, keepdims=True))
        probs_ref[at(r), :] = (raw / jnp.sum(raw, axis=-1, keepdims=True)).astype(BF16)
    loads[2].wait()
    for r in range(rows):
        att_ref[at(r), :] = jnp.dot(probs_ref[at(r), :], v_ref[r], preferred_element_type=F32)
    for h in range(heads):
        lanes = slice(h * dim, (h + 1) * dim)
        mine = att_ref[pl.ds(h, rows, stride=heads), :]
        out_ref[:, lanes] = (res_ref[:, lanes].astype(F32) + mine).astype(BF16)
    for c in weights:
        c.wait()


def attend(queries, cache_keys, stored_value_cache, lengths, residual, weights, bands):
    rows, heads, dim = queries.shape
    kv = cache_keys.shape[2]
    span = cache_keys.shape[1] * kv
    held = [pltpu.VMEM((bands, 2, BAND, w.shape[1]), BF16) for w in weights[:1]]
    band_sems = [pltpu.SemaphoreType.DMA((bands, 2)) for _ in held]
    return pl.pallas_call(
        functools.partial(attend_kernel, kv, bands),
        out_shape=(jax.ShapeDtypeStruct((rows, heads * dim), BF16), *held),
        in_specs=[SMEM, HBM, HBM, HBM, VMEM] + [HBM for _ in weights],
        out_specs=(VMEM,) + tuple(VMEM for _ in held),
        scratch_shapes=[
            pltpu.VMEM((rows * heads, dim), F32),
            pltpu.VMEM((rows * heads, span), F32),
            pltpu.VMEM((rows * heads, span), BF16),
            pltpu.VMEM(queries.shape, BF16),
            pltpu.VMEM((rows, span, dim), BF16),
            pltpu.VMEM((rows, span, dim), BF16),
            pltpu.SemaphoreType.DMA((3,)),
        ]
        + band_sems,
        compiler_params=params(8),
        cost_estimate=cost(rows * heads * span * dim * 4, rows * span * dim * 4),
        name="attention",
    )(
        in_hbm(lengths),
        in_hbm(queries),
        in_hbm(cache_keys.reshape(rows, span, dim)),
        in_hbm(stored_value_cache.reshape(rows, span, dim)),
        in_hbm(residual),
        *(in_hbm(w) for w in weights),
    )


def band_copies(g_hbm, u_hbm, held_ref, sems, first):
    return [
        pltpu.make_async_copy(
            w.at[pl.ds((first + i) * BAND, BAND)], held_ref.at[i, kind], sems.at[i, kind]
        )
        for i in range(held_ref.shape[0])
        for kind, w in enumerate((g_hbm, u_hbm))
    ]


def load_kernel(first, after_ref, g_hbm, u_hbm, held_ref, sems):
    copies = band_copies(g_hbm, u_hbm, held_ref, sems, first)
    for c in copies:
        c.start()
    for c in copies:
        c.wait()


def load_bands(after, gate_weight, up_weight, first, bands):
    columns = gate_weight.shape[1]
    return pl.pallas_call(
        functools.partial(load_kernel, first),
        out_shape=pltpu.VMEM((bands, 2, BAND, columns), BF16),
        in_specs=[ANY, HBM, HBM],
        out_specs=VMEM,
        scratch_shapes=[pltpu.SemaphoreType.DMA((bands, 2))],
        compiler_params=params(2),
        cost_estimate=cost(0, bands * 2 * BAND * columns * 2),
        name="load_bands",
    )(after, in_hbm(gate_weight), in_hbm(up_weight))


def hold(array, after):
    return pl.pallas_call(
        lambda array_ref, after_ref, out_ref: None,
        out_shape=jax.ShapeDtypeStruct(array.shape, array.dtype),
        in_specs=[ANY, ANY],
        out_specs=ANY,
        input_output_aliases={0: 0},
        compiler_params=params(2),
        name="hold",
    )(array, after)


def pack_kernel(a_ref, b_ref, after_ref, out_ref):
    out_ref[0] = a_ref[...]
    out_ref[1] = b_ref[...]


def pack(a, b, after):
    return pl.pallas_call(
        pack_kernel,
        out_shape=jax.ShapeDtypeStruct((2,) + a.shape, a.dtype),
        in_specs=[VMEM, VMEM, ANY],
        out_specs=VMEM,
        compiler_params=params(4),
        name="pack",
    )(a, b, after)


def tile_at(index):
    return pl.ds(pl.multiple_of(index * TILE, TILE), TILE)


def gate_up_kernel(devices, holders, first, *refs):
    a_ref, b_ref, c_ref, d_ref, g_hbm, u_hbm = refs[:6]
    held_refs = refs[6 : 6 + holders]
    part_ref, rows_ref, total_ref, buf, sems = refs[6 + holders :]
    nx = grid_of(devices)[1]
    slots = buf.shape[0]
    streamed = band_copies(g_hbm, u_hbm, buf, sems, first)
    late = band_copies(g_hbm, u_hbm, buf.at[0:1], sems, first + slots)
    for c in streamed:
        c.start()
    me = lax.axis_index(AXIS)
    my_z, my_x = me // nx, me % nx
    per = a_ref.shape[1]
    for near, far, flip in ((a_ref, b_ref, 0), (c_ref, d_ref, 1)):
        for i in range(2):
            z = my_z ^ (flip + 2 * i)
            here, there = near[i].astype(F32), far[i].astype(F32)
            pair = [jnp.where(my_x == 0, here, there), jnp.where(my_x == 0, there, here)]
            at = pl.ds(pl.multiple_of(z * (2 * per), 2 * per), 2 * per)
            rows_ref[at, :] = jnp.concatenate(pair, axis=0).astype(BF16)

    def band(i):
        if isinstance(i, int):
            return slice(i * BAND, (i + 1) * BAND)
        return pl.ds(pl.multiple_of(i * BAND, BAND), BAND)

    def add(i, weight, kind):
        total_ref[kind] += jnp.dot(rows_ref[:, band(i)], weight, preferred_element_type=F32)

    def add_streamed(index, slot, copies):
        for kind, c in enumerate(copies):
            c.wait()
            add(index, buf[slot, kind], kind)

    total_ref[...] = jnp.zeros_like(total_ref)
    start = 0
    for number, held in enumerate(held_refs):

        def step(i, _, held=held, start=start):
            for kind in range(2):
                add(start + i, held[i, kind], kind)
            return 0

        lax.fori_loop(0, held.shape[0], step, 0)
        start += held.shape[0]
        if number == 1:
            add_streamed(first, 0, streamed[:2])
            for c in late:
                c.start()
    for slot in range(1, slots):
        add_streamed(first + slot, slot, streamed[2 * slot : 2 * slot + 2])
    add_streamed(first + slots, 0, late)
    part_ref[...] = total_ref[...].astype(BF16)


def gate_up(blocks, gate_weight, up_weight, held, devices):
    total = devices * blocks[0].shape[1]
    features, columns = gate_weight.shape
    first = sum(h.shape[0] for h in held)
    slots = features // BAND - first - 1
    return pl.pallas_call(
        functools.partial(gate_up_kernel, devices, len(held), first),
        out_shape=(
            jax.ShapeDtypeStruct((2, total, columns), BF16),
            jax.ShapeDtypeStruct((total, features), BF16),
        ),
        in_specs=[VMEM] * 4 + [HBM, HBM] + [VMEM] * len(held),
        out_specs=(VMEM, VMEM),
        scratch_shapes=[
            pltpu.VMEM((2, total, columns), F32),
            pltpu.VMEM((slots, 2, BAND, columns), BF16),
            pltpu.SemaphoreType.DMA((slots, 2)),
        ],
        compiler_params=params(13),
        cost_estimate=cost(4 * total * features * columns, 4 * features * columns),
        name="gate_up",
    )(*blocks, in_hbm(gate_weight), in_hbm(up_weight), *(in_vmem(h) for h in held))


def half_copies(w_hbm, base, held_ref, sems, first):
    half = held_ref.shape[2]
    return [
        pltpu.make_async_copy(
            w_hbm.at[pl.ds((first + i) * TILE, TILE), pl.ds(base, half)],
            held_ref.at[i],
            sems.at[i],
        )
        for i in range(held_ref.shape[0])
    ]


def half_base(devices, mine, half):
    my_x = lax.axis_index(AXIS) % grid_of(devices)[1]
    return pl.multiple_of((my_x if mine else 1 - my_x) * half, half)


def down_load_kernel(devices, after_ref, w_hbm, held_ref, sems):
    base = half_base(devices, False, held_ref.shape[2])
    copies = half_copies(w_hbm, base, held_ref, sems, 0)
    for c in copies:
        c.start()
    for c in copies:
        c.wait()


def load_down(after, down_weight, devices, tiles):
    half = down_weight.shape[1] // 2
    return pl.pallas_call(
        functools.partial(down_load_kernel, devices),
        out_shape=pltpu.VMEM((tiles, TILE, half), BF16),
        in_specs=[ANY, HBM],
        out_specs=VMEM,
        scratch_shapes=[pltpu.SemaphoreType.DMA((tiles,))],
        compiler_params=params(2),
        cost_estimate=cost(0, tiles * TILE * half * 2),
        name="load_down",
    )(after, in_hbm(down_weight))


def add_half(hidden_ref, held_ref, buf, copies, total_ref):
    held = held_ref.shape[0]
    total_ref[...] = jnp.zeros_like(total_ref)

    def step(i, _):
        total_ref[...] += jnp.dot(
            hidden_ref[:, tile_at(i)], held_ref[i], preferred_element_type=F32
        )
        return 0

    lax.fori_loop(0, held, step, 0)
    for i, c in enumerate(copies):
        c.wait()
        at = slice((held + i) * TILE, (held + i + 1) * TILE)
        total_ref[...] += jnp.dot(hidden_ref[:, at], buf[i], preferred_element_type=F32)


def down_far_kernel(
    devices,
    own_ref,
    other_ref,
    held_ref,
    w_hbm,
    out_ref,
    hidden_ref,
    next_ref,
    total_ref,
    buf,
    sems,
    next_sems,
):
    half = out_ref.shape[1]
    copies = half_copies(w_hbm, half_base(devices, False, half), buf, sems, held_ref.shape[0])
    ahead = half_copies(w_hbm, half_base(devices, True, half), next_ref, next_sems, 0)
    for c in copies + ahead:
        c.start()
    gate = own_ref[0].astype(F32) + other_ref[0].astype(F32)
    up = own_ref[1].astype(F32) + other_ref[1].astype(F32)
    hidden_ref[...] = (gate / (1.0 + jnp.exp(-gate)) * up).astype(BF16)
    add_half(hidden_ref, held_ref, buf, copies, total_ref)
    out_ref[...] = total_ref[...].astype(BF16)
    for c in ahead:
        c.wait()


def down_far(own, other, held, down_weight, devices, ahead):
    total = own.shape[1]
    columns, features = down_weight.shape
    half = features // 2
    left = columns // TILE - held.shape[0]
    return pl.pallas_call(
        functools.partial(down_far_kernel, devices),
        out_shape=(
            jax.ShapeDtypeStruct((total, half), BF16),
            jax.ShapeDtypeStruct((total, columns), BF16),
            pltpu.VMEM((ahead, TILE, half), BF16),
        ),
        in_specs=[VMEM, VMEM, VMEM, HBM],
        out_specs=(VMEM, VMEM, VMEM),
        scratch_shapes=[
            pltpu.VMEM((total, half), F32),
            pltpu.VMEM((left, TILE, half), BF16),
            pltpu.SemaphoreType.DMA((left,)),
            pltpu.SemaphoreType.DMA((ahead,)),
        ],
        compiler_params=params(20),
        cost_estimate=cost(total * features * columns, features * columns),
        name="down_far_half",
    )(own, other, in_vmem(held), in_hbm(down_weight))


def down_near_kernel(devices, hidden_ref, held_ref, w_hbm, out_ref, buf, sems):
    half = out_ref.shape[1]
    copies = half_copies(w_hbm, half_base(devices, True, half), buf, sems, held_ref.shape[0])
    for c in copies:
        c.start()
    add_half(hidden_ref, held_ref, buf, copies, out_ref)


def down_near(hidden, held, down_weight, devices):
    total = hidden.shape[0]
    columns, features = down_weight.shape
    half = features // 2
    left = columns // TILE - held.shape[0]
    return pl.pallas_call(
        functools.partial(down_near_kernel, devices),
        out_shape=jax.ShapeDtypeStruct((total, half), F32),
        in_specs=[VMEM, VMEM, HBM],
        out_specs=VMEM,
        scratch_shapes=[
            pltpu.VMEM((left, TILE, half), BF16),
            pltpu.SemaphoreType.DMA((left,)),
        ],
        compiler_params=params(20),
        cost_estimate=cost(total * features * columns, features * columns),
        name="down_near_half",
    )(hidden, in_vmem(held), in_hbm(down_weight))


def pick(row_ref, capacity, first_slot, slots):
    row = row_ref[...]
    total = row.shape[1]
    down = lax.broadcasted_iota(jnp.int32, (total, total), 0)
    across = lax.broadcasted_iota(jnp.int32, (total, total), 1)
    diagonal = jnp.where(down == across, row, 0).astype(F32).astype(BF16)
    column = jnp.dot(diagonal, jnp.ones((total, total), BF16), preferred_element_type=F32)
    earlier = (column == row.astype(F32)) & (down < across)
    rank = jnp.sum(earlier.astype(F32), axis=0, keepdims=True).astype(jnp.int32)
    slot = first_slot + lax.broadcasted_iota(jnp.int32, (slots, total), 0)
    return (slot == row * capacity + rank).astype(F32).astype(BF16)


def to_slots_kernel(devices, capacity, row_ref, near_ref, far_ref, own_ref, *sends):
    nz, nx = grid_of(devices)
    my_z = lax.axis_index(AXIS) // nx
    slots = own_ref.shape[0]
    total = near_ref[...] + far_ref[...].astype(F32)
    rounded = total.astype(BF16)
    for dz, send_ref in enumerate((own_ref,) + sends):
        z = my_z ^ dz
        chosen = pick(row_ref, capacity, z * slots, slots)
        if dz:
            send_ref[...] = jnp.dot(chosen, rounded, preferred_element_type=F32).astype(BF16)
        else:
            high = rounded.astype(F32)
            low = (total - high).astype(BF16)
            own_ref[...] = jnp.dot(chosen, rounded, preferred_element_type=F32) + jnp.dot(
                chosen, low, preferred_element_type=F32
            )


def to_slots(row, near, far, devices, capacity):
    nz, nx = grid_of(devices)
    slots = nx * 2 * capacity
    width = near.shape[1]
    return pl.pallas_call(
        functools.partial(to_slots_kernel, devices, capacity),
        out_shape=(jax.ShapeDtypeStruct((slots, width), F32),)
        + (jax.ShapeDtypeStruct((slots, width), BF16),) * (nz - 1),
        in_specs=[VMEM] * 3,
        out_specs=(VMEM,) * nz,
        compiler_params=params(8),
        name="to_slots",
    )(row, near, far)


def finish_kernel(devices, capacity, row_ref, rows_ref, own_ref, *refs):
    *landed, keep_ref, send_ref = refs
    nz, nx = grid_of(devices)
    me = lax.axis_index(AXIS)
    my_z, my_x = me // nx, me % nx
    slots, width = own_ref.shape
    chosen = pick(row_ref, capacity, my_z * slots, slots)
    mixed = rows_ref[:, pl.ds(pl.multiple_of(my_x * width, width), width)]
    total = own_ref[...]
    for ref in landed:
        total = total + ref[...].astype(F32)
    done = jnp.dot(chosen, mixed, preferred_element_type=F32) + total
    half = slots // 2
    first, second = done[:half], done[half:]
    keep_ref[...] = jnp.where(my_x == 0, first, second).astype(BF16)
    send_ref[...] = jnp.where(my_x == 0, second, first).astype(BF16)


def finish(row, rows, own, landed, devices, capacity):
    slots, width = own.shape
    shape = jax.ShapeDtypeStruct((slots // 2, width), BF16)
    return pl.pallas_call(
        functools.partial(finish_kernel, devices, capacity),
        out_shape=(shape, shape),
        in_specs=[VMEM] * (3 + len(landed)),
        out_specs=(VMEM, VMEM),
        compiler_params=params(8),
        name="finish",
    )(row, rows, own, *landed)


def join_kernel(nx, keep_ref, other_ref, out_ref):
    my_x = lax.axis_index(AXIS) % nx
    width = keep_ref.shape[1]
    out_ref[:, :width] = jnp.where(my_x == 0, keep_ref[...], other_ref[...])
    out_ref[:, width:] = jnp.where(my_x == 0, other_ref[...], keep_ref[...])


def join(keep, other, devices):
    slots, width = keep.shape
    return pl.pallas_call(
        functools.partial(join_kernel, grid_of(devices)[1]),
        out_shape=jax.ShapeDtypeStruct((slots, 2 * width), BF16),
        in_specs=[VMEM, VMEM],
        out_specs=VMEM,
        compiler_params=params(8),
        name="join_halves",
    )(keep, other)


def slot_positions(column, destinations, capacity):
    onehot = (column[:, None] == jnp.arange(destinations, dtype=jnp.int32)[None, :]).astype(
        jnp.int32
    )
    before = jnp.cumsum(onehot, axis=0) - onehot
    slot_rank = jnp.sum(before * onehot, axis=1)
    return column * capacity + slot_rank


def plain(mixed_rows, target, gate_weight, up_weight, down_weight, devices):
    rows_dev, features = mixed_rows.shape
    me = lax.axis_index(AXIS)
    gathered = lax.all_gather(mixed_rows, AXIS, axis=0, tiled=True)
    mine = jnp.stack(
        [
            jnp.dot(gathered, gate_weight, preferred_element_type=F32),
            jnp.dot(gathered, up_weight, preferred_element_type=F32),
        ]
    )
    other = lax.ppermute(mine.astype(BF16), "ffn", [(0, 1), (1, 0)])
    gate_sum, up_sum = mine + other.astype(F32)
    hidden = (jax.nn.silu(gate_sum) * up_sum).astype(BF16)
    down = jnp.dot(hidden, down_weight, preferred_element_type=F32)
    share = features // devices
    landed = lax.all_to_all(
        jnp.moveaxis(down.astype(BF16).reshape(-1, devices, share), 1, 0), AXIS, 0, 0
    )
    summed = jnp.sum(landed.astype(F32), axis=0)
    mixed_share = lax.dynamic_slice_in_dim(gathered, me * share, share, axis=1)
    finished = (mixed_share.astype(F32) + summed).astype(BF16)
    slot_count = 2 * devices * rows_dev
    position = slot_positions(target[:, 0], 2 * devices, rows_dev)
    chosen = (jnp.arange(slot_count, dtype=jnp.int32)[:, None] == position[None, :]).astype(BF16)
    slots = jnp.dot(chosen, finished, preferred_element_type=F32).astype(BF16)
    slots = slots.reshape(devices, 2 * rows_dev, share)
    mine_out = lax.all_to_all(slots, AXIS, split_axis=0, concat_axis=0)
    return jnp.moveaxis(mine_out, 0, 1).reshape(2 * rows_dev, features)


def local(
    queries,
    cache_keys,
    stored_value_cache,
    lengths,
    residual,
    target,
    gate_weight,
    up_weight,
    down_weight,
):
    devices = lax.axis_size(AXIS)
    nz, nx = grid_of(devices)
    capacity = cache_keys.shape[0]
    columns, features = down_weight.shape
    fits = nz == 4 and nx == 2 and columns % TILE == 0 and features % (16 * TILE) == 0
    share = 3 * (gate_weight.shape[0] // BAND) // 16 if fits else 0
    mixed_rows, *held = attend(
        queries,
        cache_keys,
        stored_value_cache,
        lengths,
        residual,
        (gate_weight, up_weight) if fits else (),
        share,
    )
    if not fits:
        return plain(mixed_rows, target, gate_weight, up_weight, down_weight, devices)

    two = lax.ppermute(mixed_rows, AXIS, swap_z(devices, 2))
    held.append(load_bands(mixed_rows, gate_weight, up_weight, share, share))
    a = pack(mixed_rows, two, held[-1])
    b = lax.ppermute(a, AXIS, swap_x(devices))
    c = lax.ppermute(a, AXIS, swap_z(devices, 1))
    held.append(load_bands(a, gate_weight, up_weight, 2 * share, share))
    c = hold(c, held[-1])
    d = lax.ppermute(c, AXIS, swap_x(devices))
    held.append(load_bands(c, gate_weight, up_weight, 3 * share, share))
    part, rows = gate_up((a, b, c, d), gate_weight, up_weight, held, devices)
    other = lax.ppermute(part, "ffn", [(0, 1), (1, 0)])
    tiles = columns // TILE
    held_down = load_down(part, down_weight, devices, 6 * tiles // 13)
    far_half, hidden, held_near = down_far(
        part, other, held_down, down_weight, devices, 4 * tiles // 13
    )
    arrived = lax.ppermute(far_half, AXIS, swap_x(devices))
    near_half = down_near(hidden, held_near, down_weight, devices)
    row = target.reshape(1, -1)
    own_slots, *sends = to_slots(row, near_half, arrived, devices, capacity)
    landed = [
        lax.ppermute(send, AXIS, swap_z(devices, bits + 1)) for bits, send in enumerate(sends)
    ]
    keep, send = finish(row, rows, own_slots, landed, devices, capacity)
    return join(keep, lax.ppermute(send, AXIS, swap_x(devices)), devices)


def solution(mesh):
    return jax.shard_map(
        local,
        mesh=mesh,
        in_specs=(
            P(("parts", "attn"), "ffn", None),
            P(("parts", "attn"), None, "ffn", None),
            P(("parts", "attn"), None, "ffn", None),
            P(("parts", "attn")),
            P(("parts", "attn"), "ffn"),
            P("parts", None),
            P("ffn", "attn"),
            P("ffn", "attn"),
            P("attn", "ffn"),
        ),
        out_specs=P(("parts", "attn"), "ffn"),
        check_vma=False,
    )
```

```python
import functools
import math

import jax
import jax.numpy as jnp
from jax import lax
from jax.experimental import pallas as pl
from jax.experimental.pallas import tpu as pltpu
from jax.sharding import PartitionSpec as P

AXIS = "attn"
TILE = 256
BAND = 256
ORDER = (0, 2, 1, 3)
MIB = 1 << 20
VMEM = pl.BlockSpec(memory_space=pltpu.VMEM)
SMEM = pl.BlockSpec(memory_space=pltpu.SMEM)
ANY = pl.BlockSpec(memory_space=pl.ANY)
HBM = pl.BlockSpec(memory_space=pltpu.HBM)
F32 = jnp.float32
BF16 = jnp.bfloat16


def params(mib):
    return pltpu.CompilerParams(vmem_limit_bytes=mib * MIB)


def in_vmem(array):
    return pltpu.with_memory_space_constraint(array, pltpu.VMEM)


def in_hbm(array):
    return pltpu.with_memory_space_constraint(array, pltpu.HBM)


def cost(flops, moved):
    return pl.CostEstimate(flops=flops, bytes_accessed=moved, transcendentals=0)


def grid_of(devices):
    nx = 1
    while 4 * nx * nx < devices:
        nx *= 2
    if devices % nx:
        nx = 1
    return devices // nx, nx


def swap_z(devices, bits):
    nz, nx = grid_of(devices)
    return [(z * nx + x, (z ^ bits) * nx + x) for z in range(nz) for x in range(nx)]


def swap_x(devices):
    nz, nx = grid_of(devices)
    return [(z * nx + x, z * nx + (x ^ 1)) for z in range(nz) for x in range(nx)]


COST = cost(0, 1024)


def attend_kernel(kv, bands, lengths, q_hbm, k_hbm, v_hbm, res_ref, *refs):
    weights = ()
    if bands:
        g_hbm, u_hbm, out_ref, held_ref, *refs, band_sems = refs
        weights = band_copies(g_hbm, u_hbm, held_ref, band_sems, 0)
    else:
        out_ref, *refs = refs
    att_ref, scores_ref, probs_ref, q_ref, k_ref, v_ref, sems = refs
    rows, heads, dim = q_ref.shape
    span = k_ref.shape[1]
    per_group = heads // kv
    loads = [
        pltpu.make_async_copy(source, held, sems.at[i])
        for i, (source, held) in enumerate(((q_hbm, q_ref), (k_hbm, k_ref), (v_hbm, v_ref)))
    ]
    for load in loads:
        load.start()
    for c in weights:
        c.start()
    column = lax.broadcasted_iota(jnp.int32, (heads, span), 1)
    head = lax.broadcasted_iota(jnp.int32, (heads, span), 0)
    right_group = (column % kv) == (head // per_group)
    position = column // kv

    def at(r):
        return slice(r * heads, (r + 1) * heads)

    loads[0].wait()
    loads[1].wait()
    for r in range(rows):
        scores = lax.dot_general(
            q_ref[r], k_ref[r], (((1,), (1,)), ((), ())), preferred_element_type=F32
        ) * (1.0 / math.sqrt(dim))
        scores_ref[at(r), :] = jnp.where(right_group & (position < lengths[r]), scores, -1e30)
    for r in range(rows):
        scores = scores_ref[at(r), :]
        raw = jnp.exp(scores - jnp.max(scores, axis=-1, keepdims=True))
        probs_ref[at(r), :] = (raw * (1.0 / jnp.sum(raw, axis=-1, keepdims=True))).astype(BF16)
    loads[2].wait()
    for r in range(rows):
        att_ref[at(r), :] = jnp.dot(probs_ref[at(r), :], v_ref[r], preferred_element_type=F32)
    for h in range(heads):
        lanes = slice(h * dim, (h + 1) * dim)
        mine = att_ref[pl.ds(h, rows, stride=heads), :]
        out_ref[:, lanes] = (res_ref[:, lanes].astype(F32) + mine).astype(BF16)
    for c in weights:
        c.wait()


def attend(queries, cache_keys, stored_value_cache, lengths, residual, weights, bands):
    rows, heads, dim = queries.shape
    kv = cache_keys.shape[2]
    span = cache_keys.shape[1] * kv
    held = [pltpu.VMEM((bands, 2, BAND, w.shape[1]), BF16) for w in weights[:1]]
    band_sems = [pltpu.SemaphoreType.DMA((bands, 2)) for _ in held]
    return pl.pallas_call(
        functools.partial(attend_kernel, kv, bands),
        out_shape=(jax.ShapeDtypeStruct((rows, heads * dim), BF16), *held),
        in_specs=[SMEM, HBM, HBM, HBM, VMEM] + [HBM for _ in weights],
        out_specs=(VMEM,) + tuple(VMEM for _ in held),
        scratch_shapes=[
            pltpu.VMEM((rows * heads, dim), F32),
            pltpu.VMEM((rows * heads, span), F32),
            pltpu.VMEM((rows * heads, span), BF16),
            pltpu.VMEM(queries.shape, BF16),
            pltpu.VMEM((rows, span, dim), BF16),
            pltpu.VMEM((rows, span, dim), BF16),
            pltpu.SemaphoreType.DMA((3,)),
        ]
        + band_sems,
        compiler_params=params(8),
        cost_estimate=cost(rows * heads * span * dim * 4, rows * span * dim * 4),
        name="attention",
    )(
        in_hbm(lengths),
        in_hbm(queries),
        in_hbm(cache_keys.reshape(rows, span, dim)),
        in_hbm(stored_value_cache.reshape(rows, span, dim)),
        in_hbm(residual),
        *(in_hbm(w) for w in weights),
    )


def band_copies(g_hbm, u_hbm, held_ref, sems, first):
    return [
        pltpu.make_async_copy(
            w.at[pl.ds((first + i) * BAND, BAND)], held_ref.at[i, kind], sems.at[i, kind]
        )
        for i in range(held_ref.shape[0])
        for kind, w in enumerate((g_hbm, u_hbm))
    ]


def load_kernel(first, after_ref, g_hbm, u_hbm, held_ref, sems):
    copies = band_copies(g_hbm, u_hbm, held_ref, sems, first)
    for c in copies:
        c.start()
    for c in copies:
        c.wait()


def load_bands(after, gate_weight, up_weight, first, bands):
    columns = gate_weight.shape[1]
    return pl.pallas_call(
        functools.partial(load_kernel, first),
        out_shape=pltpu.VMEM((bands, 2, BAND, columns), BF16),
        in_specs=[ANY, HBM, HBM],
        out_specs=VMEM,
        scratch_shapes=[pltpu.SemaphoreType.DMA((bands, 2))],
        compiler_params=params(2),
        cost_estimate=cost(0, bands * 2 * BAND * columns * 2),
        name="load_bands",
    )(after, in_hbm(gate_weight), in_hbm(up_weight))


def hold(array, after):
    return pl.pallas_call(
        lambda array_ref, after_ref, out_ref: None,
        out_shape=jax.ShapeDtypeStruct(array.shape, array.dtype),
        in_specs=[ANY, ANY],
        out_specs=ANY,
        input_output_aliases={0: 0},
        compiler_params=params(2),
        name="hold",
    )(array, after)


def pack_kernel(a_ref, b_ref, after_ref, out_ref):
    out_ref[0] = a_ref[...]
    out_ref[1] = b_ref[...]


def pack(a, b, after):
    return pl.pallas_call(
        pack_kernel,
        out_shape=jax.ShapeDtypeStruct((2,) + a.shape, a.dtype),
        in_specs=[VMEM, VMEM, ANY],
        out_specs=VMEM,
        compiler_params=params(4),
        name="pack",
    )(a, b, after)


def tile_at(index):
    return pl.ds(pl.multiple_of(index * TILE, TILE), TILE)


def gate_up_kernel(devices, holders, first, *refs):
    a_ref, b_ref, c_ref, d_ref, g_hbm, u_hbm, w_hbm = refs[:7]
    held_refs = refs[7 : 7 + holders]
    part_ref, rows_ref, far_ref, total_ref, buf, sems, far_sems = refs[7 + holders :]
    nx = grid_of(devices)[1]
    slots = buf.shape[0]
    left = g_hbm.shape[0] // BAND - first

    def streamed(j):
        slot = lax.rem(j, slots)
        at = pl.ds(pl.multiple_of((first + j) * BAND, BAND), BAND)
        return [
            pltpu.make_async_copy(w.at[at], buf.at[slot, kind], sems.at[slot, kind])
            for kind, w in enumerate((g_hbm, u_hbm))
        ]

    for j in range(min(slots, left)):
        for c in streamed(j):
            c.start()
    half = far_ref.shape[2]
    ahead = down_copies(w_hbm, half_base(devices, False, half), far_ref, far_sems, 0)
    for c in ahead:
        c.start()
    me = lax.axis_index(AXIS)
    my_z, my_x = me // nx, me % nx
    per = a_ref.shape[1]
    for near, far, flip in ((a_ref, b_ref, 0), (c_ref, d_ref, 1)):
        for i in range(2):
            z = my_z ^ (flip + 2 * i)
            here, there = near[i].astype(F32), far[i].astype(F32)
            pair = [jnp.where(my_x == 0, here, there), jnp.where(my_x == 0, there, here)]
            at = pl.ds(pl.multiple_of(z * (2 * per), 2 * per), 2 * per)
            rows_ref[at, :] = jnp.concatenate(pair, axis=0).astype(BF16)

    def add(i, weight, kind):
        at = pl.ds(pl.multiple_of(i * BAND, BAND), BAND)
        total_ref[kind] += jnp.dot(rows_ref[:, at], weight, preferred_element_type=F32)

    def add_streamed(j):
        slot = lax.rem(j, slots)
        for kind, c in enumerate(streamed(j)):
            c.wait()
            add(first + j, buf[slot, kind], kind)

        @pl.when(j + slots < left)
        def _():
            for c in streamed(j + slots):
                c.start()

    total_ref[...] = jnp.zeros_like(total_ref)
    start, came = 0, 0
    for held in held_refs:

        def step(i, _, held=held, start=start, came=came):
            for kind in range(2):
                add(start + i, held[i, kind], kind)
            if start:
                add_streamed(came + i)
            return 0

        lax.fori_loop(0, held.shape[0], step, 0)
        came += held.shape[0] if start else 0
        start += held.shape[0]

    def rest(j, _):
        add_streamed(j)
        return 0

    lax.fori_loop(came, left, rest, 0)
    part_ref[...] = total_ref[...].astype(BF16)
    for c in ahead:
        c.wait()


def gate_up(blocks, gate_weight, up_weight, down_weight, held, devices, tiles):
    total = devices * blocks[0].shape[1]
    features, columns = gate_weight.shape
    first = sum(h.shape[0] for h in held)
    slots = 2
    far = (tiles, TILE, features // 2)
    return pl.pallas_call(
        functools.partial(gate_up_kernel, devices, len(held), first),
        out_shape=(
            jax.ShapeDtypeStruct((2, total, columns), BF16),
            jax.ShapeDtypeStruct((total, features), BF16),
            pltpu.VMEM(far, BF16),
        ),
        in_specs=[VMEM] * 4 + [HBM] * 3 + [VMEM] * len(held),
        out_specs=(VMEM, VMEM, VMEM),
        scratch_shapes=[
            pltpu.VMEM((2, total, columns), F32),
            pltpu.VMEM((slots, 2, BAND, columns), BF16),
            pltpu.SemaphoreType.DMA((slots, 2)),
            pltpu.SemaphoreType.DMA((far[0],)),
        ],
        compiler_params=params(10),
        cost_estimate=cost(4 * total * features * columns, 4 * features * columns),
        name="gate_up",
    )(
        *blocks,
        in_hbm(gate_weight),
        in_hbm(up_weight),
        in_hbm(down_weight),
        *(in_vmem(h) for h in held),
    )


def down_copies(w_hbm, base, held_ref, sems, first):
    wide = held_ref.shape[2]
    return [
        pltpu.make_async_copy(
            w_hbm.at[pl.ds((first + i) * TILE, TILE), pl.ds(base, wide)],
            held_ref.at[i],
            sems.at[i],
        )
        for i in range(held_ref.shape[0])
    ]


def half_base(devices, mine, half):
    my_x = lax.axis_index(AXIS) % grid_of(devices)[1]
    return pl.multiple_of((my_x if mine else 1 - my_x) * half, half)


def quarter_base(devices, quarter, wide):
    my_x = lax.axis_index(AXIS) % grid_of(devices)[1]
    return pl.multiple_of((2 * my_x + quarter) * wide, wide)


def pick(row_ref, capacity, first_slot, slots):
    row = row_ref[...]
    total = row.shape[1]
    down = lax.broadcasted_iota(jnp.int32, (total, total), 0)
    across = lax.broadcasted_iota(jnp.int32, (total, total), 1)
    diagonal = jnp.where(down == across, row, 0).astype(F32).astype(BF16)
    column = jnp.dot(diagonal, jnp.ones((total, total), BF16), preferred_element_type=F32)
    earlier = (column == row.astype(F32)) & (down < across)
    rank = jnp.sum(earlier.astype(F32), axis=0, keepdims=True).astype(jnp.int32)
    slot = first_slot + lax.broadcasted_iota(jnp.int32, (slots, total), 0)
    return (slot == row * capacity + rank).astype(F32).astype(BF16)


def prepare_kernel(devices, capacity, first, after_ref, row_ref, w_hbm, held_ref, chosen_ref, sems):
    base = half_base(devices, False, held_ref.shape[2])
    copies = down_copies(w_hbm, base, held_ref, sems, first)
    for c in copies:
        c.start()
    nz, nx = grid_of(devices)
    my_z = lax.axis_index(AXIS) // nx
    slots = chosen_ref.shape[0] // nz
    for i, bits in enumerate(ORDER):
        chosen_ref[i * slots : (i + 1) * slots, :] = pick(
            row_ref, capacity, (my_z ^ bits) * slots, slots
        )
    for c in copies:
        c.wait()


def prepare(after, row, down_weight, devices, capacity, first, tiles):
    wide = down_weight.shape[1] // 2
    total = row.shape[1]
    return pl.pallas_call(
        functools.partial(prepare_kernel, devices, capacity, first),
        out_shape=(
            pltpu.VMEM((tiles, TILE, wide), BF16),
            jax.ShapeDtypeStruct((devices * 2 * capacity, total), BF16),
        ),
        in_specs=[ANY, VMEM, HBM],
        out_specs=(VMEM, VMEM),
        scratch_shapes=[pltpu.SemaphoreType.DMA((tiles,))],
        compiler_params=params(2),
        cost_estimate=cost(0, tiles * TILE * wide * 2),
        name="prepare",
    )(after, row, in_hbm(down_weight))


def add_held(hidden_ref, held_refs, at, total_ref):
    start = 0
    for held_ref in held_refs:

        def step(i, _, held_ref=held_ref, start=start):
            total_ref[...] += jnp.dot(
                hidden_ref[:, tile_at(start + i)],
                held_ref[i, :, at],
                preferred_element_type=F32,
            )
            return 0

        lax.fori_loop(0, held_ref.shape[0], step, 0)
        start += held_ref.shape[0]


def down_far_kernel(devices, quarter, *refs):
    if quarter == 0:
        own_ref, other_ref, *refs = refs
        *held_refs, w_hbm, out_ref, next_ref, hidden_ref, total_ref, sems = refs
    else:
        hidden_ref, *held_refs, w_hbm, out_ref, next_ref, total_ref, sems = refs
    wide = out_ref.shape[1]
    ahead = down_copies(w_hbm, quarter_base(devices, quarter, wide), next_ref, sems, 0)
    for c in ahead:
        c.start()
    if quarter == 0:
        gate = own_ref[0].astype(F32) + other_ref[0].astype(F32)
        up = own_ref[1].astype(F32) + other_ref[1].astype(F32)
        hidden_ref[...] = (gate / (1.0 + jnp.exp(-gate)) * up).astype(BF16)
    total_ref[...] = jnp.zeros_like(total_ref)
    add_held(hidden_ref, held_refs, slice(quarter * wide, (quarter + 1) * wide), total_ref)
    out_ref[...] = total_ref[...].astype(BF16)
    for c in ahead:
        c.wait()


def down_far(inputs, held, down_weight, devices, quarter, ahead):
    total = inputs[0].shape[-2]
    columns, features = down_weight.shape
    wide = features // 4
    hidden = [jax.ShapeDtypeStruct((total, columns), BF16)] if quarter == 0 else []
    return pl.pallas_call(
        functools.partial(down_far_kernel, devices, quarter),
        out_shape=(
            jax.ShapeDtypeStruct((total, wide), BF16),
            pltpu.VMEM((ahead, TILE, wide), BF16),
            *hidden,
        ),
        in_specs=[VMEM] * (len(inputs) + len(held)) + [HBM],
        out_specs=(VMEM, VMEM) + tuple(VMEM for _ in hidden),
        scratch_shapes=[
            pltpu.VMEM((total, wide), F32),
            pltpu.SemaphoreType.DMA((ahead,)),
        ],
        compiler_params=params(6),
        cost_estimate=COST,
        name="down_far",
    )(*inputs, *(in_vmem(h) for h in held), in_hbm(down_weight))


def down_near_kernel(devices, quarter, *refs):
    hidden_ref, arrived_ref, chosen_ref, held_ref, w_hbm, keep_ref, send_ref, total_ref, buf, sems = refs
    held = held_ref.shape[0]
    copies = down_copies(w_hbm, quarter_base(devices, quarter, buf.shape[2]), buf, sems, held)
    for c in copies:
        c.start()
    total_ref[...] = arrived_ref[...].astype(F32)
    add_held(hidden_ref, (held_ref,), slice(None), total_ref)
    for i, c in enumerate(copies):
        c.wait()
        at = slice((held + i) * TILE, (held + i + 1) * TILE)
        total_ref[...] += jnp.dot(hidden_ref[:, at], buf[i], preferred_element_type=F32)
    slots = keep_ref.shape[0]
    rounded = total_ref[...].astype(BF16)
    keep_ref[...] = jnp.dot(chosen_ref[:slots], rounded, preferred_element_type=F32).astype(BF16)
    send_ref[...] = jnp.dot(chosen_ref[slots:], rounded, preferred_element_type=F32).astype(BF16)


def down_near(hidden, arrived, chosen, down_weight, held, devices, quarter):
    total, wide = arrived.shape
    left = down_weight.shape[0] // TILE - held.shape[0]
    shape = jax.ShapeDtypeStruct((chosen.shape[0] // 2, wide), BF16)
    return pl.pallas_call(
        functools.partial(down_near_kernel, devices, quarter),
        out_shape=(shape, shape),
        in_specs=[VMEM] * 4 + [HBM],
        out_specs=(VMEM, VMEM),
        scratch_shapes=[
            pltpu.VMEM((total, wide), F32),
            pltpu.VMEM((left, TILE, wide), BF16),
            pltpu.SemaphoreType.DMA((left,)),
        ],
        compiler_params=params(8),
        cost_estimate=COST,
        name="down_near",
    )(hidden, arrived, chosen, in_vmem(held), in_hbm(down_weight))


def add_kernel(keep_ref, came_ref, own_ref, send_ref):
    slots = own_ref.shape[0]
    total = keep_ref[...].astype(F32) + came_ref[...].astype(F32)
    own_ref[...] = total[:slots]
    send_ref[...] = total[slots:].astype(BF16)


def add(keep, came):
    slots, wide = keep.shape
    return pl.pallas_call(
        add_kernel,
        out_shape=(
            jax.ShapeDtypeStruct((slots // 2, wide), F32),
            jax.ShapeDtypeStruct((slots // 2, wide), BF16),
        ),
        in_specs=[VMEM, VMEM],
        out_specs=(VMEM, VMEM),
        compiler_params=params(4),
        name="add",
    )(keep, came)


def finish_kernel(devices, chosen_ref, rows_ref, *refs):
    own_refs, came_refs, (keep_ref, send_ref) = refs[:2], refs[2:4], refs[4:]
    my_x = lax.axis_index(AXIS) % grid_of(devices)[1]
    slots, wide = own_refs[0].shape
    half = slots // 2
    for quarter, (own_ref, came_ref) in enumerate(zip(own_refs, came_refs)):
        mixed = rows_ref[:, pl.ds(quarter_base(devices, quarter, wide), wide)]
        done = jnp.dot(chosen_ref[:slots], mixed, preferred_element_type=F32)
        done = done + (own_ref[...] + came_ref[...].astype(F32))
        first, second = done[:half], done[half:]
        at = slice(quarter * wide, (quarter + 1) * wide)
        keep_ref[:, at] = jnp.where(my_x == 0, first, second).astype(BF16)
        send_ref[:, at] = jnp.where(my_x == 0, second, first).astype(BF16)


def finish(chosen, rows, own, came, devices):
    slots, wide = own[0].shape
    shape = jax.ShapeDtypeStruct((slots // 2, 2 * wide), BF16)
    return pl.pallas_call(
        functools.partial(finish_kernel, devices),
        out_shape=(shape, shape),
        in_specs=[VMEM] * 6,
        out_specs=(VMEM, VMEM),
        compiler_params=params(6),
        name="finish",
    )(chosen, rows, *own, *came)


def join_kernel(nx, keep_ref, other_ref, out_ref):
    my_x = lax.axis_index(AXIS) % nx
    width = keep_ref.shape[1]
    out_ref[:, :width] = jnp.where(my_x == 0, keep_ref[...], other_ref[...])
    out_ref[:, width:] = jnp.where(my_x == 0, other_ref[...], keep_ref[...])


def join(keep, other, devices):
    slots, width = keep.shape
    return pl.pallas_call(
        functools.partial(join_kernel, grid_of(devices)[1]),
        out_shape=jax.ShapeDtypeStruct((slots, 2 * width), BF16),
        in_specs=[VMEM, VMEM],
        out_specs=VMEM,
        compiler_params=params(8),
        name="join_halves",
    )(keep, other)


def slot_positions(column, destinations, capacity):
    onehot = (column[:, None] == jnp.arange(destinations, dtype=jnp.int32)[None, :]).astype(
        jnp.int32
    )
    before = jnp.cumsum(onehot, axis=0) - onehot
    slot_rank = jnp.sum(before * onehot, axis=1)
    return column * capacity + slot_rank


def plain(mixed_rows, target, gate_weight, up_weight, down_weight, devices):
    rows_dev, features = mixed_rows.shape
    me = lax.axis_index(AXIS)
    gathered = lax.all_gather(mixed_rows, AXIS, axis=0, tiled=True)
    mine = jnp.stack(
        [
            jnp.dot(gathered, gate_weight, preferred_element_type=F32),
            jnp.dot(gathered, up_weight, preferred_element_type=F32),
        ]
    )
    other = lax.ppermute(mine.astype(BF16), "ffn", [(0, 1), (1, 0)])
    gate_sum, up_sum = mine + other.astype(F32)
    hidden = (jax.nn.silu(gate_sum) * up_sum).astype(BF16)
    down = jnp.dot(hidden, down_weight, preferred_element_type=F32)
    share = features // devices
    landed = lax.all_to_all(
        jnp.moveaxis(down.astype(BF16).reshape(-1, devices, share), 1, 0), AXIS, 0, 0
    )
    summed = jnp.sum(landed.astype(F32), axis=0)
    mixed_share = lax.dynamic_slice_in_dim(gathered, me * share, share, axis=1)
    finished = (mixed_share.astype(F32) + summed).astype(BF16)
    slot_count = 2 * devices * rows_dev
    position = slot_positions(target[:, 0], 2 * devices, rows_dev)
    chosen = (jnp.arange(slot_count, dtype=jnp.int32)[:, None] == position[None, :]).astype(BF16)
    slots = jnp.dot(chosen, finished, preferred_element_type=F32).astype(BF16)
    slots = slots.reshape(devices, 2 * rows_dev, share)
    mine_out = lax.all_to_all(slots, AXIS, split_axis=0, concat_axis=0)
    return jnp.moveaxis(mine_out, 0, 1).reshape(2 * rows_dev, features)


def local(
    queries,
    cache_keys,
    stored_value_cache,
    lengths,
    residual,
    target,
    gate_weight,
    up_weight,
    down_weight,
):
    devices = lax.axis_size(AXIS)
    nz, nx = grid_of(devices)
    capacity = cache_keys.shape[0]
    columns, features = down_weight.shape
    fits = nz == 4 and nx == 2 and columns % TILE == 0 and features % (16 * TILE) == 0
    share = gate_weight.shape[0] // BAND // 8 if fits else 0
    mixed_rows, *held = attend(
        queries,
        cache_keys,
        stored_value_cache,
        lengths,
        residual,
        (gate_weight, up_weight) if fits else (),
        share,
    )
    if not fits:
        return plain(mixed_rows, target, gate_weight, up_weight, down_weight, devices)

    two = lax.ppermute(mixed_rows, AXIS, swap_z(devices, 2))
    held.append(load_bands(mixed_rows, gate_weight, up_weight, share, share))
    a = pack(mixed_rows, two, held[-1])
    b = lax.ppermute(a, AXIS, swap_x(devices))
    c = lax.ppermute(a, AXIS, swap_z(devices, 1))
    held.append(load_bands(a, gate_weight, up_weight, 2 * share, share))
    c = hold(c, held[-1])
    d = lax.ppermute(c, AXIS, swap_x(devices))
    held.append(load_bands(c, gate_weight, up_weight, 3 * share, share))
    tiles = columns // TILE
    most = 8 * tiles // 13
    part, rows, *held_far = gate_up(
        (a, b, c, d), gate_weight, up_weight, down_weight, held, devices, most
    )
    other = lax.ppermute(part, "ffn", [(0, 1), (1, 0)])
    rest, chosen = prepare(
        part, target.reshape(1, -1), down_weight, devices, capacity, most, tiles - most
    )
    held_far.append(rest)

    far, near_first, hidden = down_far((part, other), held_far, down_weight, devices, 0, 9 * tiles // 13)
    arrived = [lax.ppermute(far, AXIS, swap_x(devices))]
    far, near_second = down_far((hidden,), held_far, down_weight, devices, 1, 8 * tiles // 13)
    arrived.append(lax.ppermute(far, AXIS, swap_x(devices)))
    own, came = [], []
    for quarter, held_near in enumerate((near_first, near_second)):
        keep, send = down_near(
            hidden, arrived[quarter], chosen, down_weight, held_near, devices, quarter
        )
        mine, send = add(keep, lax.ppermute(send, AXIS, swap_z(devices, 1)))
        own.append(mine)
        came.append(lax.ppermute(send, AXIS, swap_z(devices, 2)))
    keep, send = finish(chosen, rows, own, came, devices)
    return join(keep, lax.ppermute(send, AXIS, swap_x(devices)), devices)


def solution(mesh):
    return jax.shard_map(
        local,
        mesh=mesh,
        in_specs=(
            P(("parts", "attn"), "ffn", None),
            P(("parts", "attn"), None, "ffn", None),
            P(("parts", "attn"), None, "ffn", None),
            P(("parts", "attn")),
            P(("parts", "attn"), "ffn"),
            P("parts", None),
            P("ffn", "attn"),
            P("ffn", "attn"),
            P("attn", "ffn"),
        ),
        out_specs=P(("parts", "attn"), "ffn"),
        check_vma=False,
    )
```

```python
import functools
import math

import jax
import jax.numpy as jnp
from jax import lax
from jax.experimental import pallas as pl
from jax.experimental.pallas import tpu as pltpu
from jax.sharding import PartitionSpec as P

AXIS = "attn"
TILE = 256
BAND = 512
PIECES = 2
ORDER = (0, 2, 1, 3)
MIB = 1 << 20
VMEM = pl.BlockSpec(memory_space=pltpu.VMEM)
SMEM = pl.BlockSpec(memory_space=pltpu.SMEM)
ANY = pl.BlockSpec(memory_space=pl.ANY)
HBM = pl.BlockSpec(memory_space=pltpu.HBM)
F32 = jnp.float32
BF16 = jnp.bfloat16


def params(mib):
    return pltpu.CompilerParams(vmem_limit_bytes=mib * MIB)


def in_vmem(array):
    return pltpu.with_memory_space_constraint(array, pltpu.VMEM)


def in_hbm(array):
    return pltpu.with_memory_space_constraint(array, pltpu.HBM)


def cost(flops, moved):
    return pl.CostEstimate(flops=flops, bytes_accessed=moved, transcendentals=0)


def grid_of(devices):
    nx = 1
    while 4 * nx * nx < devices:
        nx *= 2
    if devices % nx:
        nx = 1
    return devices // nx, nx


def swap_z(devices, bits):
    nz, nx = grid_of(devices)
    return [(z * nx + x, (z ^ bits) * nx + x) for z in range(nz) for x in range(nx)]


def swap_x(devices):
    nz, nx = grid_of(devices)
    return [(z * nx + x, z * nx + (x ^ 1)) for z in range(nz) for x in range(nx)]


COST = cost(0, 1024)


def attend_kernel(kv, bands, lengths, q_hbm, k_hbm, v_hbm, res_ref, *refs):
    weights = ()
    if bands:
        g_hbm, u_hbm, out_ref, held_ref, *refs, band_sems = refs
        weights = band_copies(g_hbm, u_hbm, held_ref, band_sems, 0, 0)
    else:
        out_ref, *refs = refs
    att_ref, scores_ref, probs_ref, q_ref, k_ref, v_ref, sems = refs
    rows, heads, dim = q_ref.shape
    span = k_ref.shape[1]
    per_group = heads // kv
    loads = [
        pltpu.make_async_copy(source, held, sems.at[i])
        for i, (source, held) in enumerate(((q_hbm, q_ref), (k_hbm, k_ref), (v_hbm, v_ref)))
    ]
    for load in loads:
        load.start()
    for c in weights:
        c.start()
    column = lax.broadcasted_iota(jnp.int32, (heads, span), 1)
    head = lax.broadcasted_iota(jnp.int32, (heads, span), 0)
    right_group = (column % kv) == (head // per_group)
    position = column // kv

    def at(r):
        return slice(r * heads, (r + 1) * heads)

    loads[0].wait()
    loads[1].wait()
    for r in range(rows):
        scores = lax.dot_general(
            q_ref[r], k_ref[r], (((1,), (1,)), ((), ())), preferred_element_type=F32
        ) * (1.0 / math.sqrt(dim))
        scores_ref[at(r), :] = jnp.where(right_group & (position < lengths[r]), scores, -1e30)
    for r in range(rows):
        scores = scores_ref[at(r), :]
        raw = jnp.exp(scores - jnp.max(scores, axis=-1, keepdims=True))
        probs_ref[at(r), :] = (raw * (1.0 / jnp.sum(raw, axis=-1, keepdims=True))).astype(BF16)
    loads[2].wait()
    for r in range(rows):
        att_ref[at(r), :] = jnp.dot(probs_ref[at(r), :], v_ref[r], preferred_element_type=F32)
    for h in range(heads):
        lanes = slice(h * dim, (h + 1) * dim)
        mine = att_ref[pl.ds(h, rows, stride=heads), :]
        out_ref[:, lanes] = (res_ref[:, lanes].astype(F32) + mine).astype(BF16)
    for c in weights:
        c.wait()


def attend(queries, cache_keys, stored_value_cache, lengths, residual, weights, bands):
    rows, heads, dim = queries.shape
    kv = cache_keys.shape[2]
    span = cache_keys.shape[1] * kv
    held = [pltpu.VMEM((bands, 2, BAND, w.shape[1]), BF16) for w in weights[:1]]
    band_sems = [pltpu.SemaphoreType.DMA((2, PIECES)) for _ in held]
    return pl.pallas_call(
        functools.partial(attend_kernel, kv, bands),
        out_shape=(jax.ShapeDtypeStruct((rows, heads * dim), BF16), *held),
        in_specs=[SMEM, HBM, HBM, HBM, VMEM] + [HBM for _ in weights],
        out_specs=(VMEM,) + tuple(VMEM for _ in held),
        scratch_shapes=[
            pltpu.VMEM((rows * heads, dim), F32),
            pltpu.VMEM((rows * heads, span), F32),
            pltpu.VMEM((rows * heads, span), BF16),
            pltpu.VMEM(queries.shape, BF16),
            pltpu.VMEM((rows, span, dim), BF16),
            pltpu.VMEM((rows, span, dim), BF16),
            pltpu.SemaphoreType.DMA((3,)),
        ]
        + band_sems,
        compiler_params=params(8),
        cost_estimate=cost(rows * heads * span * dim * 4, rows * span * dim * 4),
        name="attention",
    )(
        in_hbm(lengths),
        in_hbm(queries),
        in_hbm(cache_keys.reshape(rows, span, dim)),
        in_hbm(stored_value_cache.reshape(rows, span, dim)),
        in_hbm(residual),
        *(in_hbm(w) for w in weights),
    )


def band_copies(g_hbm, u_hbm, held_ref, sems, place, band):
    rows = BAND // PIECES
    return [
        pltpu.make_async_copy(
            w.at[pl.ds(pl.multiple_of(band * BAND + i * rows, rows), rows)],
            held_ref.at[place, kind, pl.ds(i * rows, rows)],
            sems.at[kind, i],
        )
        for kind, w in enumerate((g_hbm, u_hbm))
        for i in range(PIECES)
    ]


def load_kernel(band, after_ref, g_hbm, u_hbm, held_ref, sems):
    copies = band_copies(g_hbm, u_hbm, held_ref, sems, 0, band)
    for c in copies:
        c.start()
    for c in copies:
        c.wait()


def load_band(after, gate_weight, up_weight, band):
    columns = gate_weight.shape[1]
    return pl.pallas_call(
        functools.partial(load_kernel, band),
        out_shape=pltpu.VMEM((1, 2, BAND, columns), BF16),
        in_specs=[ANY, HBM, HBM],
        out_specs=VMEM,
        scratch_shapes=[pltpu.SemaphoreType.DMA((2, PIECES))],
        compiler_params=params(2),
        cost_estimate=cost(0, 4 * BAND * columns),
        name="load_band",
    )(after, in_hbm(gate_weight), in_hbm(up_weight))


def hold(array, after):
    return pl.pallas_call(
        lambda array_ref, after_ref, out_ref: None,
        out_shape=jax.ShapeDtypeStruct(array.shape, array.dtype),
        in_specs=[ANY, ANY],
        out_specs=ANY,
        input_output_aliases={0: 0},
        compiler_params=params(2),
        name="hold",
    )(array, after)


def pack_kernel(a_ref, b_ref, after_ref, out_ref):
    out_ref[0] = a_ref[...]
    out_ref[1] = b_ref[...]


def pack(a, b, after):
    return pl.pallas_call(
        pack_kernel,
        out_shape=jax.ShapeDtypeStruct((2,) + a.shape, a.dtype),
        in_specs=[VMEM, VMEM, ANY],
        out_specs=VMEM,
        compiler_params=params(4),
        name="pack",
    )(a, b, after)


def tile_at(index):
    return pl.ds(pl.multiple_of(index * TILE, TILE), TILE)


def gate_up_kernel(
    devices,
    held,
    *refs,
):
    a_ref, b_ref, c_ref, d_ref, g_hbm, u_hbm, w_hbm = refs[:7]
    held_refs = refs[7 : 7 + held]
    part_ref, rows_ref, far_ref, total_ref, buf, sems, far_sems = refs[7 + held :]
    nx = grid_of(devices)[1]
    slots = buf.shape[0]
    left = g_hbm.shape[0] // BAND - held

    def streamed(j):
        slot = lax.rem(j, slots)
        return band_copies(g_hbm, u_hbm, buf, sems.at[slot], slot, held + j)

    for j in range(min(slots, left)):
        for c in streamed(j):
            c.start()
    ahead = down_copies(
        w_hbm, half_base(devices, False, far_ref.shape[1]), far_ref, far_sems, 0
    )
    for c in ahead:
        c.start()
    me = lax.axis_index(AXIS)
    my_z, my_x = me // nx, me % nx
    per = a_ref.shape[1]
    for near, far, flip in ((a_ref, b_ref, 0), (c_ref, d_ref, 1)):
        for i in range(2):
            z = my_z ^ (flip + 2 * i)
            here, there = near[i].astype(F32), far[i].astype(F32)
            pair = [jnp.where(my_x == 0, here, there), jnp.where(my_x == 0, there, here)]
            at = pl.ds(pl.multiple_of(z * (2 * per), 2 * per), 2 * per)
            rows_ref[at, :] = jnp.concatenate(pair, axis=0).astype(BF16)

    def add(i, weight, kind):
        at = pl.ds(pl.multiple_of(i * BAND, BAND), BAND)
        total_ref[kind] += jnp.dot(rows_ref[:, at], weight, preferred_element_type=F32)

    total_ref[...] = jnp.zeros_like(total_ref)

    def step(i, _):
        for number, held_ref in enumerate(held_refs):

            @pl.when(i == number)
            def _():
                for kind in range(2):
                    add(number, held_ref[0, kind], kind)

        slot = lax.rem(i, slots)
        copies = streamed(i)
        for kind in range(2):
            for c in copies[kind * PIECES : (kind + 1) * PIECES]:
                c.wait()
            add(held + i, buf[slot, kind], kind)

        @pl.when(i + slots < left)
        def _():
            for c in streamed(i + slots):
                c.start()

        return 0

    lax.fori_loop(0, held, step, 0)
    part_ref[...] = total_ref[...].astype(BF16)
    for c in ahead:
        c.wait()


def gate_up(blocks, gate_weight, up_weight, down_weight, held, devices, ahead):
    total = devices * blocks[0].shape[1]
    features, columns = gate_weight.shape
    slots = 2
    return pl.pallas_call(
        functools.partial(gate_up_kernel, devices, len(held)),
        out_shape=(
            jax.ShapeDtypeStruct((2, total, columns), BF16),
            jax.ShapeDtypeStruct((total, features), BF16),
            pltpu.VMEM((ahead, features // 2), BF16),
        ),
        in_specs=[VMEM] * 4 + [HBM] * 3 + [VMEM] * len(held),
        out_specs=(VMEM, VMEM, VMEM),
        scratch_shapes=[
            pltpu.VMEM((2, total, columns), F32),
            pltpu.VMEM((slots, 2, BAND, columns), BF16),
            pltpu.SemaphoreType.DMA((slots, 2, PIECES)),
            pltpu.SemaphoreType.DMA((ahead // TILE,)),
        ],
        compiler_params=params(18),
        cost_estimate=cost(4 * total * features * columns, 4 * features * columns),
        name="gate_up",
    )(
        *blocks,
        in_hbm(gate_weight),
        in_hbm(up_weight),
        in_hbm(down_weight),
        *(in_vmem(h) for h in held),
    )


def down_copies(w_hbm, base, held_ref, sems, first):
    rows, wide = held_ref.shape
    return [
        pltpu.make_async_copy(
            w_hbm.at[pl.ds(first + i * TILE, TILE), pl.ds(base, wide)],
            held_ref.at[pl.ds(i * TILE, TILE)],
            sems.at[i],
        )
        for i in range(rows // TILE)
    ]


def half_base(devices, mine, half):
    my_x = lax.axis_index(AXIS) % grid_of(devices)[1]
    return pl.multiple_of((my_x if mine else 1 - my_x) * half, half)


def quarter_base(devices, far, quarter, wide):
    my_x = lax.axis_index(AXIS) % grid_of(devices)[1]
    half = 1 - my_x if far else my_x
    return pl.multiple_of((2 * half + quarter) * wide, wide)


def pick(row_ref, capacity, first_slot, slots):
    row = row_ref[...]
    total = row.shape[1]
    down = lax.broadcasted_iota(jnp.int32, (total, total), 0)
    across = lax.broadcasted_iota(jnp.int32, (total, total), 1)
    diagonal = jnp.where(down == across, row, 0).astype(F32).astype(BF16)
    column = jnp.dot(diagonal, jnp.ones((total, total), BF16), preferred_element_type=F32)
    earlier = (column == row.astype(F32)) & (down < across)
    rank = jnp.sum(earlier.astype(F32), axis=0, keepdims=True).astype(jnp.int32)
    slot = first_slot + lax.broadcasted_iota(jnp.int32, (slots, total), 0)
    return (slot == row * capacity + rank).astype(F32).astype(BF16)


def prepare_kernel(devices, capacity, first, after_ref, row_ref, w_hbm, held_ref, chosen_ref, sems):
    base = half_base(devices, False, held_ref.shape[1])
    copies = down_copies(w_hbm, base, held_ref, sems, first)
    for c in copies:
        c.start()
    nz, nx = grid_of(devices)
    my_z = lax.axis_index(AXIS) // nx
    slots = chosen_ref.shape[0] // nz
    for i, bits in enumerate(ORDER):
        chosen_ref[i * slots : (i + 1) * slots, :] = pick(
            row_ref, capacity, (my_z ^ bits) * slots, slots
        )
    for c in copies:
        c.wait()


def prepare(after, row, down_weight, devices, capacity, first, rows):
    wide = down_weight.shape[1] // 2
    total = row.shape[1]
    return pl.pallas_call(
        functools.partial(prepare_kernel, devices, capacity, first),
        out_shape=(
            pltpu.VMEM((rows, wide), BF16),
            jax.ShapeDtypeStruct((devices * 2 * capacity, total), BF16),
        ),
        in_specs=[ANY, VMEM, HBM],
        out_specs=(VMEM, VMEM),
        scratch_shapes=[pltpu.SemaphoreType.DMA((rows // TILE,))],
        compiler_params=params(2),
        cost_estimate=cost(0, rows * wide * 2),
        name="prepare",
    )(after, row, in_hbm(down_weight))


def multiply(hidden_ref, held_refs, quarter, total_ref, buf, copies):
    wide = total_ref.shape[1]
    start = 0
    for held_ref in held_refs:
        rows = held_ref.shape[0]
        at = slice(quarter * wide, (quarter + 1) * wide)
        weight = held_ref[...] if held_ref.shape[1] == wide else held_ref[:, at]
        total_ref[...] += jnp.dot(
            hidden_ref[:, start : start + rows], weight, preferred_element_type=F32
        )
        start += rows
    if copies:
        cut = (len(copies) + 1) // 2
        for some in (slice(0, cut), slice(cut, len(copies))):
            if not copies[some]:
                continue
            for c in copies[some]:
                c.wait()
            at = slice(some.start * TILE, some.stop * TILE)
            total_ref[...] += jnp.dot(
                hidden_ref[:, start + at.start : start + at.stop],
                buf[at],
                preferred_element_type=F32,
            )


def down_kernel(devices, far, quarter, held_count, next_base, next_first, streams, aheads, *refs):
    refs = list(refs)
    take = lambda count: [refs.pop(0) for _ in range(count)]
    first_call = far and quarter == 0
    sources = take(2 if first_call else 1)
    arrived_ref, chosen_ref = take(2) if not far else (None, None)
    held_refs = take(held_count)
    (w_hbm,) = take(1)
    out_refs = take(1 if far else 2)
    next_refs = take(1 if aheads else 0)
    (hidden_ref,) = take(1) if first_call else sources
    (total_ref,) = take(1)
    wide = total_ref.shape[1]
    copies, ahead, buf = [], [], None
    base = quarter_base(devices, far, quarter, wide)
    if streams:
        buf, sems = take(2)
        copies = down_copies(w_hbm, base, buf, sems, sum(h.shape[0] for h in held_refs))
    if aheads:
        (next_sems,) = take(1)
        ahead = down_copies(
            w_hbm, quarter_base(devices, *next_base, wide), next_refs[0], next_sems, next_first
        )
    for c in copies + ahead:
        c.start()
    if first_call:
        own_ref, other_ref = sources
        gate = own_ref[0].astype(F32) + other_ref[0].astype(F32)
        up = own_ref[1].astype(F32) + other_ref[1].astype(F32)
        hidden_ref[...] = (gate / (1.0 + jnp.exp(-gate)) * up).astype(BF16)
    if far:
        total_ref[...] = jnp.zeros_like(total_ref)
    else:
        total_ref[...] = arrived_ref[...].astype(F32)
    multiply(hidden_ref, held_refs, quarter, total_ref, buf, copies)
    rounded = total_ref[...].astype(BF16)
    if far:
        out_refs[0][...] = rounded
    else:
        slots = out_refs[0].shape[0]
        for i, ref in enumerate(out_refs):
            chosen = chosen_ref[i * slots : (i + 1) * slots]
            ref[...] = jnp.dot(chosen, rounded, preferred_element_type=F32).astype(BF16)
    for c in ahead:
        c.wait()


def down(sources, held, down_weight, devices, far, quarter, ahead=None):
    total = sources[0].shape[-2]
    columns, features = down_weight.shape
    wide = features // 4
    streams = columns - sum(h.shape[0] for h in held)
    next_base, next_first, aheads = ahead or (None, 0, 0)
    first_call = far and quarter == 0
    if far:
        out_shape = [jax.ShapeDtypeStruct((total, wide), BF16)]
    else:
        out_shape = [jax.ShapeDtypeStruct((sources[2].shape[0] // 2, wide), BF16)] * 2
    if aheads:
        out_shape.append(pltpu.VMEM((aheads, wide), BF16))
    if first_call:
        out_shape.append(jax.ShapeDtypeStruct((total, columns), BF16))
    scratch = [pltpu.VMEM((total, wide), F32)]
    if streams:
        scratch += [
            pltpu.VMEM((streams, wide), BF16),
            pltpu.SemaphoreType.DMA((streams // TILE,)),
        ]
    if aheads:
        scratch.append(pltpu.SemaphoreType.DMA((aheads // TILE,)))
    return pl.pallas_call(
        functools.partial(
            down_kernel, devices, far, quarter, len(held), next_base, next_first, streams, aheads
        ),
        out_shape=tuple(out_shape),
        in_specs=[VMEM] * (len(sources) + len(held)) + [HBM],
        out_specs=tuple(VMEM for _ in out_shape),
        scratch_shapes=scratch,
        compiler_params=params(10),
        cost_estimate=COST,
        name="down_far" if far else "down_near",
    )(*sources, *(in_vmem(h) for h in held), in_hbm(down_weight))


def add_kernel(keep_ref, came_ref, own_ref, send_ref):
    slots = own_ref.shape[0]
    total = keep_ref[...].astype(F32) + came_ref[...].astype(F32)
    own_ref[...] = total[:slots]
    send_ref[...] = total[slots:].astype(BF16)


def add(keep, came):
    slots, wide = keep.shape
    return pl.pallas_call(
        add_kernel,
        out_shape=(
            jax.ShapeDtypeStruct((slots // 2, wide), F32),
            jax.ShapeDtypeStruct((slots // 2, wide), BF16),
        ),
        in_specs=[VMEM, VMEM],
        out_specs=(VMEM, VMEM),
        compiler_params=params(4),
        name="add",
    )(keep, came)


def finish_kernel(devices, chosen_ref, rows_ref, *refs):
    own_refs, came_refs, (keep_ref, send_ref) = refs[:2], refs[2:4], refs[4:]
    my_x = lax.axis_index(AXIS) % grid_of(devices)[1]
    slots, wide = own_refs[0].shape
    half = slots // 2
    for quarter, (own_ref, came_ref) in enumerate(zip(own_refs, came_refs)):
        mixed = rows_ref[:, pl.ds(quarter_base(devices, False, quarter, wide), wide)]
        done = jnp.dot(chosen_ref[:slots], mixed, preferred_element_type=F32)
        done = done + (own_ref[...] + came_ref[...].astype(F32))
        first, second = done[:half], done[half:]
        at = slice(quarter * wide, (quarter + 1) * wide)
        keep_ref[:, at] = jnp.where(my_x == 0, first, second).astype(BF16)
        send_ref[:, at] = jnp.where(my_x == 0, second, first).astype(BF16)


def finish(chosen, rows, own, came, devices):
    slots, wide = own[0].shape
    shape = jax.ShapeDtypeStruct((slots // 2, 2 * wide), BF16)
    return pl.pallas_call(
        functools.partial(finish_kernel, devices),
        out_shape=(shape, shape),
        in_specs=[VMEM] * 6,
        out_specs=(VMEM, VMEM),
        compiler_params=params(6),
        name="finish",
    )(chosen, rows, *own, *came)


def join_kernel(nx, keep_ref, other_ref, out_ref):
    my_x = lax.axis_index(AXIS) % nx
    width = keep_ref.shape[1]
    out_ref[:, :width] = jnp.where(my_x == 0, keep_ref[...], other_ref[...])
    out_ref[:, width:] = jnp.where(my_x == 0, other_ref[...], keep_ref[...])


def join(keep, other, devices):
    slots, width = keep.shape
    return pl.pallas_call(
        functools.partial(join_kernel, grid_of(devices)[1]),
        out_shape=jax.ShapeDtypeStruct((slots, 2 * width), BF16),
        in_specs=[VMEM, VMEM],
        out_specs=VMEM,
        compiler_params=params(8),
        name="join_halves",
    )(keep, other)


def slot_positions(column, destinations, capacity):
    onehot = (column[:, None] == jnp.arange(destinations, dtype=jnp.int32)[None, :]).astype(
        jnp.int32
    )
    before = jnp.cumsum(onehot, axis=0) - onehot
    slot_rank = jnp.sum(before * onehot, axis=1)
    return column * capacity + slot_rank


def plain(mixed_rows, target, gate_weight, up_weight, down_weight, devices):
    rows_dev, features = mixed_rows.shape
    me = lax.axis_index(AXIS)
    gathered = lax.all_gather(mixed_rows, AXIS, axis=0, tiled=True)
    mine = jnp.stack(
        [
            jnp.dot(gathered, gate_weight, preferred_element_type=F32),
            jnp.dot(gathered, up_weight, preferred_element_type=F32),
        ]
    )
    other = lax.ppermute(mine.astype(BF16), "ffn", [(0, 1), (1, 0)])
    gate_sum, up_sum = mine + other.astype(F32)
    hidden = (jax.nn.silu(gate_sum) * up_sum).astype(BF16)
    down = jnp.dot(hidden, down_weight, preferred_element_type=F32)
    share = features // devices
    landed = lax.all_to_all(
        jnp.moveaxis(down.astype(BF16).reshape(-1, devices, share), 1, 0), AXIS, 0, 0
    )
    summed = jnp.sum(landed.astype(F32), axis=0)
    mixed_share = lax.dynamic_slice_in_dim(gathered, me * share, share, axis=1)
    finished = (mixed_share.astype(F32) + summed).astype(BF16)
    slot_count = 2 * devices * rows_dev
    position = slot_positions(target[:, 0], 2 * devices, rows_dev)
    chosen = (jnp.arange(slot_count, dtype=jnp.int32)[:, None] == position[None, :]).astype(BF16)
    slots = jnp.dot(chosen, finished, preferred_element_type=F32).astype(BF16)
    slots = slots.reshape(devices, 2 * rows_dev, share)
    mine_out = lax.all_to_all(slots, AXIS, split_axis=0, concat_axis=0)
    return jnp.moveaxis(mine_out, 0, 1).reshape(2 * rows_dev, features)


def local(
    queries,
    cache_keys,
    stored_value_cache,
    lengths,
    residual,
    target,
    gate_weight,
    up_weight,
    down_weight,
):
    devices = lax.axis_size(AXIS)
    nz, nx = grid_of(devices)
    capacity = cache_keys.shape[0]
    columns, features = down_weight.shape
    fits = nz == 4 and nx == 2 and columns % TILE == 0 and features % (8 * BAND) == 0
    mixed_rows, *held = attend(
        queries,
        cache_keys,
        stored_value_cache,
        lengths,
        residual,
        (gate_weight, up_weight) if fits else (),
        1 if fits else 0,
    )
    if not fits:
        return plain(mixed_rows, target, gate_weight, up_weight, down_weight, devices)

    two = lax.ppermute(mixed_rows, AXIS, swap_z(devices, 2))
    held.append(load_band(mixed_rows, gate_weight, up_weight, 1))
    a = pack(mixed_rows, two, held[-1])
    b = lax.ppermute(a, AXIS, swap_x(devices))
    c = lax.ppermute(a, AXIS, swap_z(devices, 1))
    held.append(load_band(a, gate_weight, up_weight, 2))
    c = hold(c, held[-1])
    d = lax.ppermute(c, AXIS, swap_x(devices))
    held.append(load_band(c, gate_weight, up_weight, 3))
    tiles = columns // TILE
    early, middle = 3 * tiles // 13 * TILE, 5 * tiles // 13 * TILE
    part, rows, far_a = gate_up(
        (a, b, c, d), gate_weight, up_weight, down_weight, held, devices, early
    )
    other = lax.ppermute(part, "ffn", [(0, 1), (1, 0)])
    far_b, chosen = prepare(
        part, target.reshape(1, -1), down_weight, devices, capacity, early, middle
    )

    first = early + middle
    far, far_c, hidden = down(
        (part, other),
        (far_a, far_b),
        down_weight,
        devices,
        True,
        0,
        ((True, 1), first, columns - first),
    )
    arrived = [lax.ppermute(far, AXIS, swap_x(devices))]
    far, near_a = down(
        (hidden,),
        (far_a, far_b, far_c),
        down_weight,
        devices,
        True,
        1,
        ((False, 0), 0, 9 * tiles // 13 * TILE),
    )
    arrived.append(lax.ppermute(far, AXIS, swap_x(devices)))
    own, came = [], []
    for quarter in range(2):
        sources = (hidden, arrived[quarter], chosen)
        if quarter == 0:
            ahead = ((False, 1), 0, 5 * tiles // 13 * TILE)
            keep, send, near_b = down(
                sources, (near_a,), down_weight, devices, False, 0, ahead
            )
        else:
            keep, send = down(sources, (near_b,), down_weight, devices, False, 1)
        mine, send = add(keep, lax.ppermute(send, AXIS, swap_z(devices, 1)))
        own.append(mine)
        came.append(lax.ppermute(send, AXIS, swap_z(devices, 2)))
    keep, send = finish(chosen, rows, own, came, devices)
    return join(keep, lax.ppermute(send, AXIS, swap_x(devices)), devices)


def solution(mesh):
    return jax.shard_map(
        local,
        mesh=mesh,
        in_specs=(
            P(("parts", "attn"), "ffn", None),
            P(("parts", "attn"), None, "ffn", None),
            P(("parts", "attn"), None, "ffn", None),
            P(("parts", "attn")),
            P(("parts", "attn"), "ffn"),
            P("parts", None),
            P("ffn", "attn"),
            P("ffn", "attn"),
            P("attn", "ffn"),
        ),
        out_specs=P(("parts", "attn"), "ffn"),
        check_vma=False,
    )
```

```python
import functools
import math

import jax
import jax.numpy as jnp
from jax import lax
from jax.experimental import pallas as pl
from jax.experimental.pallas import tpu as pltpu
from jax.sharding import PartitionSpec as P

AXIS = "attn"
TILE = 256
BAND = 256
GATE_MIB = 11
ORDER = (0, 2, 1, 3)
MIB = 1 << 20
VMEM = pl.BlockSpec(memory_space=pltpu.VMEM)
SMEM = pl.BlockSpec(memory_space=pltpu.SMEM)
ANY = pl.BlockSpec(memory_space=pl.ANY)
HBM = pl.BlockSpec(memory_space=pltpu.HBM)
F32 = jnp.float32
BF16 = jnp.bfloat16


def params(mib):
    return pltpu.CompilerParams(vmem_limit_bytes=mib * MIB)


def in_vmem(array):
    return pltpu.with_memory_space_constraint(array, pltpu.VMEM)


def in_hbm(array):
    return pltpu.with_memory_space_constraint(array, pltpu.HBM)


def cost(flops, moved):
    return pl.CostEstimate(flops=flops, bytes_accessed=moved, transcendentals=0)


def grid_of(devices):
    nx = 1
    while 4 * nx * nx < devices:
        nx *= 2
    if devices % nx:
        nx = 1
    return devices // nx, nx


def swap_z(devices, bits):
    nz, nx = grid_of(devices)
    return [(z * nx + x, (z ^ bits) * nx + x) for z in range(nz) for x in range(nx)]


def swap_x(devices):
    nz, nx = grid_of(devices)
    return [(z * nx + x, z * nx + (x ^ 1)) for z in range(nz) for x in range(nx)]


COST = cost(0, 1024)


def attend_kernel(kv, ahead, lengths, q_hbm, k_hbm, v_hbm, res_ref, *refs):
    weights = ()
    if ahead:
        g_hbm, u_hbm, out_ref, held_ref, *refs, band_sems = refs
        weights = band_copies(g_hbm, u_hbm, held_ref, band_sems, 0)
    else:
        out_ref, *refs = refs
    att_ref, scores_ref, probs_ref, q_ref, k_ref, v_ref, sems = refs
    rows, heads, dim = q_ref.shape
    span = k_ref.shape[1]
    per_group = heads // kv
    loads = [
        pltpu.make_async_copy(source, held, sems.at[i])
        for i, (source, held) in enumerate(((q_hbm, q_ref), (k_hbm, k_ref), (v_hbm, v_ref)))
    ]
    for load in loads:
        load.start()
    for c in weights:
        c.start()
    column = lax.broadcasted_iota(jnp.int32, (heads, span), 1)
    head = lax.broadcasted_iota(jnp.int32, (heads, span), 0)
    right_group = (column % kv) == (head // per_group)
    position = column // kv

    def at(r):
        return slice(r * heads, (r + 1) * heads)

    loads[0].wait()
    loads[1].wait()
    for r in range(rows):
        scores = lax.dot_general(
            q_ref[r], k_ref[r], (((1,), (1,)), ((), ())), preferred_element_type=F32
        ) * (1.0 / math.sqrt(dim))
        scores_ref[at(r), :] = jnp.where(right_group & (position < lengths[r]), scores, -1e30)
    for r in range(rows):
        scores = scores_ref[at(r), :]
        raw = jnp.exp(scores - jnp.max(scores, axis=-1, keepdims=True))
        probs_ref[at(r), :] = (raw * (1.0 / jnp.sum(raw, axis=-1, keepdims=True))).astype(BF16)
    loads[2].wait()
    for r in range(rows):
        att_ref[at(r), :] = jnp.dot(probs_ref[at(r), :], v_ref[r], preferred_element_type=F32)
    for h in range(heads):
        lanes = slice(h * dim, (h + 1) * dim)
        mine = att_ref[pl.ds(h, rows, stride=heads), :]
        out_ref[:, lanes] = (res_ref[:, lanes].astype(F32) + mine).astype(BF16)
    for c in weights:
        c.wait()


def attend(queries, cache_keys, stored_value_cache, lengths, residual, weights, ahead):
    rows, heads, dim = queries.shape
    kv = cache_keys.shape[2]
    span = cache_keys.shape[1] * kv
    held = [pltpu.VMEM((2, ahead, w.shape[1]), BF16) for w in weights[:1]]
    band_sems = [pltpu.SemaphoreType.DMA((2, ahead // BAND)) for _ in held]
    return pl.pallas_call(
        functools.partial(attend_kernel, kv, ahead),
        out_shape=(jax.ShapeDtypeStruct((rows, heads * dim), BF16), *held),
        in_specs=[SMEM, HBM, HBM, HBM, VMEM] + [HBM for _ in weights],
        out_specs=(VMEM,) + tuple(VMEM for _ in held),
        scratch_shapes=[
            pltpu.VMEM((rows * heads, dim), F32),
            pltpu.VMEM((rows * heads, span), F32),
            pltpu.VMEM((rows * heads, span), BF16),
            pltpu.VMEM(queries.shape, BF16),
            pltpu.VMEM((rows, span, dim), BF16),
            pltpu.VMEM((rows, span, dim), BF16),
            pltpu.SemaphoreType.DMA((3,)),
        ]
        + band_sems,
        compiler_params=params(8),
        cost_estimate=cost(rows * heads * span * dim * 4, rows * span * dim * 4),
        name="attention",
    )(
        in_hbm(lengths),
        in_hbm(queries),
        in_hbm(cache_keys.reshape(rows, span, dim)),
        in_hbm(stored_value_cache.reshape(rows, span, dim)),
        in_hbm(residual),
        *(in_hbm(w) for w in weights),
    )


def band_copies(g_hbm, u_hbm, held_ref, sems, first):
    return [
        pltpu.make_async_copy(
            w.at[pl.ds(pl.multiple_of(first + i * BAND, BAND), BAND)],
            held_ref.at[kind, pl.ds(i * BAND, BAND)],
            sems.at[kind, i],
        )
        for kind, w in enumerate((g_hbm, u_hbm))
        for i in range(held_ref.shape[1] // BAND)
    ]


def load_kernel(first, after_ref, g_hbm, u_hbm, held_ref, sems):
    copies = band_copies(g_hbm, u_hbm, held_ref, sems, first)
    for c in copies:
        c.start()
    for c in copies:
        c.wait()


def load_rows(after, gate_weight, up_weight, first, rows):
    columns = gate_weight.shape[1]
    return pl.pallas_call(
        functools.partial(load_kernel, first),
        out_shape=pltpu.VMEM((2, rows, columns), BF16),
        in_specs=[ANY, HBM, HBM],
        out_specs=VMEM,
        scratch_shapes=[pltpu.SemaphoreType.DMA((2, rows // BAND))],
        compiler_params=params(2),
        cost_estimate=cost(0, 4 * rows * columns),
        name="load_rows",
    )(after, in_hbm(gate_weight), in_hbm(up_weight))


def hold(array, after):
    return pl.pallas_call(
        lambda array_ref, after_ref, out_ref: None,
        out_shape=jax.ShapeDtypeStruct(array.shape, array.dtype),
        in_specs=[ANY, ANY],
        out_specs=ANY,
        input_output_aliases={0: 0},
        compiler_params=params(2),
        name="hold",
    )(array, after)


def pack_kernel(a_ref, b_ref, after_ref, out_ref):
    out_ref[0] = a_ref[...]
    out_ref[1] = b_ref[...]


def pack(a, b, after):
    return pl.pallas_call(
        pack_kernel,
        out_shape=jax.ShapeDtypeStruct((2,) + a.shape, a.dtype),
        in_specs=[VMEM, VMEM, ANY],
        out_specs=VMEM,
        compiler_params=params(4),
        name="pack",
    )(a, b, after)


def tile_at(index):
    return pl.ds(pl.multiple_of(index * TILE, TILE), TILE)


def gate_up_kernel(
    devices,
    held,
    *refs,
):
    a_ref, b_ref, c_ref, d_ref, g_hbm, u_hbm, w_hbm = refs[:7]
    held_refs = refs[7 : 7 + held]
    part_ref, rows_ref, far_ref, total_ref, buf, sems, far_sems = refs[7 + held :]
    nx = grid_of(devices)[1]
    slots = buf.shape[0]
    first = sum(ref.shape[1] for ref in held_refs)
    left = (g_hbm.shape[0] - first) // BAND

    def streamed(j):
        slot = lax.rem(j, slots)
        return band_copies(g_hbm, u_hbm, buf.at[slot], sems.at[slot], first + j * BAND)

    for j in range(min(slots, left)):
        for c in streamed(j):
            c.start()
    ahead = down_copies(
        w_hbm, half_base(devices, False, far_ref.shape[1]), far_ref, far_sems, 0
    )
    for c in ahead:
        c.start()
    me = lax.axis_index(AXIS)
    my_z, my_x = me // nx, me % nx
    per = a_ref.shape[1]
    for near, far, flip in ((a_ref, b_ref, 0), (c_ref, d_ref, 1)):
        for i in range(2):
            z = my_z ^ (flip + 2 * i)
            here, there = near[i].astype(F32), far[i].astype(F32)
            pair = [jnp.where(my_x == 0, here, there), jnp.where(my_x == 0, there, here)]
            at = pl.ds(pl.multiple_of(z * (2 * per), 2 * per), 2 * per)
            rows_ref[at, :] = jnp.concatenate(pair, axis=0).astype(BF16)

    def add(at, weight, kind):
        total_ref[kind] += jnp.dot(rows_ref[:, at], weight, preferred_element_type=F32)

    total_ref[...] = jnp.zeros_like(total_ref)

    def step(j, _):
        start = 0
        for number, held_ref in enumerate(held_refs):
            stop = start + held_ref.shape[1]

            @pl.when(j == number * left // held)
            def _(start=start, stop=stop, held_ref=held_ref):
                for kind in range(2):
                    add(slice(start, stop), held_ref[kind], kind)

            start = stop
        slot = lax.rem(j, slots)
        for kind, c in enumerate(streamed(j)):
            c.wait()
            at = pl.ds(pl.multiple_of(first + j * BAND, BAND), BAND)
            add(at, buf[slot, kind], kind)

        @pl.when(j + slots < left)
        def _():
            for c in streamed(j + slots):
                c.start()

        return 0

    lax.fori_loop(0, left, step, 0)
    part_ref[...] = total_ref[...].astype(BF16)
    for c in ahead:
        c.wait()


def gate_up(blocks, gate_weight, up_weight, down_weight, held, devices, ahead):
    total = devices * blocks[0].shape[1]
    features, columns = gate_weight.shape
    slots = 2
    return pl.pallas_call(
        functools.partial(gate_up_kernel, devices, len(held)),
        out_shape=(
            jax.ShapeDtypeStruct((2, total, columns), BF16),
            jax.ShapeDtypeStruct((total, features), BF16),
            pltpu.VMEM((ahead, features // 2), BF16),
        ),
        in_specs=[VMEM] * 4 + [HBM] * 3 + [VMEM] * len(held),
        out_specs=(VMEM, VMEM, VMEM),
        scratch_shapes=[
            pltpu.VMEM((2, total, columns), F32),
            pltpu.VMEM((slots, 2, BAND, columns), BF16),
            pltpu.SemaphoreType.DMA((slots, 2, 1)),
            pltpu.SemaphoreType.DMA((ahead // TILE,)),
        ],
        compiler_params=params(GATE_MIB),
        cost_estimate=cost(4 * total * features * columns, 4 * features * columns),
        name="gate_up",
    )(
        *blocks,
        in_hbm(gate_weight),
        in_hbm(up_weight),
        in_hbm(down_weight),
        *(in_vmem(h) for h in held),
    )


def down_copies(w_hbm, base, held_ref, sems, first):
    rows, wide = held_ref.shape
    return [
        pltpu.make_async_copy(
            w_hbm.at[pl.ds(first + i * TILE, TILE), pl.ds(base, wide)],
            held_ref.at[pl.ds(i * TILE, TILE)],
            sems.at[i],
        )
        for i in range(rows // TILE)
    ]


def half_base(devices, mine, half):
    my_x = lax.axis_index(AXIS) % grid_of(devices)[1]
    return pl.multiple_of((my_x if mine else 1 - my_x) * half, half)


def quarter_base(devices, far, quarter, wide):
    my_x = lax.axis_index(AXIS) % grid_of(devices)[1]
    half = 1 - my_x if far else my_x
    return pl.multiple_of((2 * half + quarter) * wide, wide)


def pick(row_ref, capacity, first_slot, slots):
    row = row_ref[...]
    total = row.shape[1]
    down = lax.broadcasted_iota(jnp.int32, (total, total), 0)
    across = lax.broadcasted_iota(jnp.int32, (total, total), 1)
    diagonal = jnp.where(down == across, row, 0).astype(F32).astype(BF16)
    column = jnp.dot(diagonal, jnp.ones((total, total), BF16), preferred_element_type=F32)
    earlier = (column == row.astype(F32)) & (down < across)
    rank = jnp.sum(earlier.astype(F32), axis=0, keepdims=True).astype(jnp.int32)
    slot = first_slot + lax.broadcasted_iota(jnp.int32, (slots, total), 0)
    return (slot == row * capacity + rank).astype(F32).astype(BF16)


def prepare_kernel(
    devices, capacity, first, after_ref, row_ref, w_hbm, far_ref, near_ref, chosen_ref, far_sems, sems
):
    base = half_base(devices, False, far_ref.shape[1])
    copies = down_copies(w_hbm, base, far_ref, far_sems, first)
    base = quarter_base(devices, False, 0, near_ref.shape[1])
    copies += down_copies(w_hbm, base, near_ref, sems, 0)
    for c in copies:
        c.start()
    nz, nx = grid_of(devices)
    my_z = lax.axis_index(AXIS) // nx
    slots = chosen_ref.shape[0] // nz
    for i, bits in enumerate(ORDER):
        chosen_ref[i * slots : (i + 1) * slots, :] = pick(
            row_ref, capacity, (my_z ^ bits) * slots, slots
        )
    for c in copies:
        c.wait()


def prepare(after, row, down_weight, devices, capacity, first, near_rows):
    columns, features = down_weight.shape
    total = row.shape[1]
    far_rows = columns - first
    return pl.pallas_call(
        functools.partial(prepare_kernel, devices, capacity, first),
        out_shape=(
            pltpu.VMEM((far_rows, features // 2), BF16),
            pltpu.VMEM((near_rows, features // 4), BF16),
            jax.ShapeDtypeStruct((devices * 2 * capacity, total), BF16),
        ),
        in_specs=[ANY, VMEM, HBM],
        out_specs=(VMEM, VMEM, VMEM),
        scratch_shapes=[
            pltpu.SemaphoreType.DMA((far_rows // TILE,)),
            pltpu.SemaphoreType.DMA((near_rows // TILE,)),
        ],
        compiler_params=params(2),
        cost_estimate=cost(0, (2 * far_rows + near_rows) * features // 2),
        name="prepare",
    )(after, row, in_hbm(down_weight))


def down_kernel(devices, far, quarter, held_count, aheads, *refs):
    refs = list(refs)

    def take(count):
        return [refs.pop(0) for _ in range(count)]

    first_call = far and quarter == 0
    sources = take(2 if first_call else 1)
    arrived_ref, chosen_ref = (None, None) if far else take(2)
    held_refs = take(held_count)
    (w_hbm,) = take(1)
    out_refs = take(1 if far else 2)
    next_refs = take(len(aheads))
    (hidden_ref,) = take(1) if first_call else sources
    (total_ref,) = take(1)
    wide = total_ref.shape[1]
    ahead = []
    for (their, start, _), ref, sems in zip(aheads, next_refs, take(len(aheads))):
        ahead += down_copies(w_hbm, quarter_base(devices, False, their, wide), ref, sems, start)
    for c in ahead:
        c.start()
    if first_call:
        own_ref, other_ref = sources
        gate = own_ref[0].astype(F32) + other_ref[0].astype(F32)
        up = own_ref[1].astype(F32) + other_ref[1].astype(F32)
        hidden_ref[...] = (gate / (1.0 + jnp.exp(-gate)) * up).astype(BF16)
    if far:
        total_ref[...] = jnp.zeros_like(total_ref)
    else:
        total_ref[...] = arrived_ref[...].astype(F32)
    start = 0
    for held_ref in held_refs:
        stop = start + held_ref.shape[0]
        at = slice(quarter * wide, (quarter + 1) * wide) if far else slice(None)
        total_ref[...] += jnp.dot(
            hidden_ref[:, start:stop], held_ref[:, at], preferred_element_type=F32
        )
        start = stop
    rounded = total_ref[...].astype(BF16)
    if far:
        out_refs[0][...] = rounded
    else:
        slots = out_refs[0].shape[0]
        for i, ref in enumerate(out_refs):
            chosen = chosen_ref[i * slots : (i + 1) * slots]
            ref[...] = jnp.dot(chosen, rounded, preferred_element_type=F32).astype(BF16)
    for c in ahead:
        c.wait()


def down(sources, held, down_weight, devices, far, quarter, aheads=()):
    total = sources[0].shape[-2]
    columns, features = down_weight.shape
    wide = features // 4
    if far:
        out_shape = [jax.ShapeDtypeStruct((total, wide), BF16)]
    else:
        out_shape = [jax.ShapeDtypeStruct((sources[2].shape[0] // 2, wide), BF16)] * 2
    out_shape += [pltpu.VMEM((rows, wide), BF16) for _, _, rows in aheads]
    if far and quarter == 0:
        out_shape.append(jax.ShapeDtypeStruct((total, columns), BF16))
    return pl.pallas_call(
        functools.partial(down_kernel, devices, far, quarter, len(held), aheads),
        out_shape=tuple(out_shape),
        in_specs=[VMEM] * (len(sources) + len(held)) + [HBM],
        out_specs=tuple(VMEM for _ in out_shape),
        scratch_shapes=[pltpu.VMEM((total, wide), F32)]
        + [pltpu.SemaphoreType.DMA((rows // TILE,)) for _, _, rows in aheads],
        compiler_params=params(6),
        cost_estimate=COST,
        name="down_far" if far else "down_near",
    )(*sources, *(in_vmem(h) for h in held), in_hbm(down_weight))


def add_kernel(keep_ref, came_ref, own_ref, send_ref):
    slots = own_ref.shape[0]
    total = keep_ref[...].astype(F32) + came_ref[...].astype(F32)
    own_ref[...] = total[:slots]
    send_ref[...] = total[slots:].astype(BF16)


def add(keep, came):
    slots, wide = keep.shape
    return pl.pallas_call(
        add_kernel,
        out_shape=(
            jax.ShapeDtypeStruct((slots // 2, wide), F32),
            jax.ShapeDtypeStruct((slots // 2, wide), BF16),
        ),
        in_specs=[VMEM, VMEM],
        out_specs=(VMEM, VMEM),
        compiler_params=params(4),
        name="add",
    )(keep, came)


def finish_kernel(devices, chosen_ref, rows_ref, *refs):
    own_refs, came_refs, (keep_ref, send_ref) = refs[:2], refs[2:4], refs[4:]
    my_x = lax.axis_index(AXIS) % grid_of(devices)[1]
    slots, wide = own_refs[0].shape
    half = slots // 2
    for quarter, (own_ref, came_ref) in enumerate(zip(own_refs, came_refs)):
        mixed = rows_ref[:, pl.ds(quarter_base(devices, False, quarter, wide), wide)]
        done = jnp.dot(chosen_ref[:slots], mixed, preferred_element_type=F32)
        done = done + (own_ref[...] + came_ref[...].astype(F32))
        first, second = done[:half], done[half:]
        at = slice(quarter * wide, (quarter + 1) * wide)
        keep_ref[:, at] = jnp.where(my_x == 0, first, second).astype(BF16)
        send_ref[:, at] = jnp.where(my_x == 0, second, first).astype(BF16)


def finish(chosen, rows, own, came, devices):
    slots, wide = own[0].shape
    shape = jax.ShapeDtypeStruct((slots // 2, 2 * wide), BF16)
    return pl.pallas_call(
        functools.partial(finish_kernel, devices),
        out_shape=(shape, shape),
        in_specs=[VMEM] * 6,
        out_specs=(VMEM, VMEM),
        compiler_params=params(6),
        name="finish",
    )(chosen, rows, *own, *came)


def join_kernel(nx, keep_ref, other_ref, out_ref):
    my_x = lax.axis_index(AXIS) % nx
    width = keep_ref.shape[1]
    out_ref[:, :width] = jnp.where(my_x == 0, keep_ref[...], other_ref[...])
    out_ref[:, width:] = jnp.where(my_x == 0, other_ref[...], keep_ref[...])


def join(keep, other, devices):
    slots, width = keep.shape
    return pl.pallas_call(
        functools.partial(join_kernel, grid_of(devices)[1]),
        out_shape=jax.ShapeDtypeStruct((slots, 2 * width), BF16),
        in_specs=[VMEM, VMEM],
        out_specs=VMEM,
        compiler_params=params(8),
        name="join_halves",
    )(keep, other)


def slot_positions(column, destinations, capacity):
    onehot = (column[:, None] == jnp.arange(destinations, dtype=jnp.int32)[None, :]).astype(
        jnp.int32
    )
    before = jnp.cumsum(onehot, axis=0) - onehot
    slot_rank = jnp.sum(before * onehot, axis=1)
    return column * capacity + slot_rank


def plain(mixed_rows, target, gate_weight, up_weight, down_weight, devices):
    rows_dev, features = mixed_rows.shape
    me = lax.axis_index(AXIS)
    gathered = lax.all_gather(mixed_rows, AXIS, axis=0, tiled=True)
    mine = jnp.stack(
        [
            jnp.dot(gathered, gate_weight, preferred_element_type=F32),
            jnp.dot(gathered, up_weight, preferred_element_type=F32),
        ]
    )
    other = lax.ppermute(mine.astype(BF16), "ffn", [(0, 1), (1, 0)])
    gate_sum, up_sum = mine + other.astype(F32)
    hidden = (jax.nn.silu(gate_sum) * up_sum).astype(BF16)
    down = jnp.dot(hidden, down_weight, preferred_element_type=F32)
    share = features // devices
    landed = lax.all_to_all(
        jnp.moveaxis(down.astype(BF16).reshape(-1, devices, share), 1, 0), AXIS, 0, 0
    )
    summed = jnp.sum(landed.astype(F32), axis=0)
    mixed_share = lax.dynamic_slice_in_dim(gathered, me * share, share, axis=1)
    finished = (mixed_share.astype(F32) + summed).astype(BF16)
    slot_count = 2 * devices * rows_dev
    position = slot_positions(target[:, 0], 2 * devices, rows_dev)
    chosen = (jnp.arange(slot_count, dtype=jnp.int32)[:, None] == position[None, :]).astype(BF16)
    slots = jnp.dot(chosen, finished, preferred_element_type=F32).astype(BF16)
    slots = slots.reshape(devices, 2 * rows_dev, share)
    mine_out = lax.all_to_all(slots, AXIS, split_axis=0, concat_axis=0)
    return jnp.moveaxis(mine_out, 0, 1).reshape(2 * rows_dev, features)


def local(
    queries,
    cache_keys,
    stored_value_cache,
    lengths,
    residual,
    target,
    gate_weight,
    up_weight,
    down_weight,
):
    devices = lax.axis_size(AXIS)
    nz, nx = grid_of(devices)
    capacity = cache_keys.shape[0]
    columns, features = down_weight.shape
    fits = nz == 4 and nx == 2 and columns % TILE == 0 and features == 16 * BAND
    mixed_rows, *held = attend(
        queries,
        cache_keys,
        stored_value_cache,
        lengths,
        residual,
        (gate_weight, up_weight) if fits else (),
        3 * BAND if fits else 0,
    )
    if not fits:
        return plain(mixed_rows, target, gate_weight, up_weight, down_weight, devices)

    two = lax.ppermute(mixed_rows, AXIS, swap_z(devices, 2))
    held.append(load_rows(mixed_rows, gate_weight, up_weight, 3 * BAND, 2 * BAND))
    a = pack(mixed_rows, two, held[-1])
    b = lax.ppermute(a, AXIS, swap_x(devices))
    c = lax.ppermute(a, AXIS, swap_z(devices, 1))
    held.append(load_rows(a, gate_weight, up_weight, 5 * BAND, 2 * BAND))
    c = hold(c, held[-1])
    d = lax.ppermute(c, AXIS, swap_x(devices))
    held.append(load_rows(c, gate_weight, up_weight, 7 * BAND, 2 * BAND))
    tiles = columns // TILE
    far_cut = 11 * tiles // 13 * TILE
    first = 6 * tiles // 13 * TILE
    cut = 2 * tiles // 13 * TILE, 8 * tiles // 13 * TILE
    part, rows, far_a = gate_up(
        (a, b, c, d), gate_weight, up_weight, down_weight, held, devices, far_cut
    )
    other = lax.ppermute(part, "ffn", [(0, 1), (1, 0)])
    far_b, near_a, chosen = prepare(
        part, target.reshape(1, -1), down_weight, devices, capacity, far_cut, first
    )
    held_far = far_a, far_b

    far, near_b, near_c, hidden = down(
        (part, other),
        held_far,
        down_weight,
        devices,
        True,
        0,
        ((0, first, columns - first), (1, 0, cut[0])),
    )
    arrived = [lax.ppermute(far, AXIS, swap_x(devices))]
    far, near_d = down(
        (hidden,), held_far, down_weight, devices, True, 1, ((1, cut[0], cut[1] - cut[0]),)
    )
    arrived.append(lax.ppermute(far, AXIS, swap_x(devices)))
    keep_a, send_a, near_e = down(
        (hidden, arrived[0], chosen),
        (near_a, near_b),
        down_weight,
        devices,
        False,
        0,
        ((1, cut[1], columns - cut[1]),),
    )
    came_a = lax.ppermute(send_a, AXIS, swap_z(devices, 1))
    keep_b, send_b = down(
        (hidden, arrived[1], chosen), (near_c, near_d, near_e), down_weight, devices, False, 1
    )
    came_b = lax.ppermute(send_b, AXIS, swap_z(devices, 1))
    own, came = [], []
    for keep, arrived in ((keep_a, came_a), (keep_b, came_b)):
        mine, send = add(keep, arrived)
        own.append(mine)
        came.append(lax.ppermute(send, AXIS, swap_z(devices, 2)))
    keep, send = finish(chosen, rows, own, came, devices)
    return join(keep, lax.ppermute(send, AXIS, swap_x(devices)), devices)


def solution(mesh):
    return jax.shard_map(
        local,
        mesh=mesh,
        in_specs=(
            P(("parts", "attn"), "ffn", None),
            P(("parts", "attn"), None, "ffn", None),
            P(("parts", "attn"), None, "ffn", None),
            P(("parts", "attn")),
            P(("parts", "attn"), "ffn"),
            P("parts", None),
            P("ffn", "attn"),
            P("ffn", "attn"),
            P("attn", "ffn"),
        ),
        out_specs=P(("parts", "attn"), "ffn"),
        check_vma=False,
    )
```

```python
import functools
import math

import jax
import jax.numpy as jnp
from jax import lax
from jax.experimental import pallas as pl
from jax.experimental.pallas import tpu as pltpu
from jax.sharding import PartitionSpec as P

AXIS = "attn"
TILE = 256
BAND = 256
GATE_MIB = 11
ORDER = (0, 2, 1, 3)
MIB = 1 << 20
VMEM = pl.BlockSpec(memory_space=pltpu.VMEM)
SMEM = pl.BlockSpec(memory_space=pltpu.SMEM)
ANY = pl.BlockSpec(memory_space=pl.ANY)
HBM = pl.BlockSpec(memory_space=pltpu.HBM)
F32 = jnp.float32
BF16 = jnp.bfloat16


def params(mib):
    return pltpu.CompilerParams(vmem_limit_bytes=mib * MIB)


def in_vmem(array):
    return pltpu.with_memory_space_constraint(array, pltpu.VMEM)


def in_hbm(array):
    return pltpu.with_memory_space_constraint(array, pltpu.HBM)


def cost(flops, moved):
    return pl.CostEstimate(flops=flops, bytes_accessed=moved, transcendentals=0)


def grid_of(devices):
    nx = 1
    while 4 * nx * nx < devices:
        nx *= 2
    if devices % nx:
        nx = 1
    return devices // nx, nx


def swap_z(devices, bits):
    nz, nx = grid_of(devices)
    return [(z * nx + x, (z ^ bits) * nx + x) for z in range(nz) for x in range(nx)]


def swap_x(devices):
    nz, nx = grid_of(devices)
    return [(z * nx + x, z * nx + (x ^ 1)) for z in range(nz) for x in range(nx)]


COST = cost(0, 1024)


def attend_kernel(kv, ahead, lengths, q_hbm, k_hbm, v_hbm, res_ref, *refs):
    weights = ()
    if ahead:
        g_hbm, u_hbm, out_ref, held_ref, *refs, band_sems = refs
        weights = band_copies(g_hbm, u_hbm, held_ref, band_sems, 0)
    else:
        out_ref, *refs = refs
    att_ref, scores_ref, probs_ref, q_ref, k_ref, v_ref, sems = refs
    rows, heads, dim = q_ref.shape
    span = k_ref.shape[1]
    per_group = heads // kv
    loads = [
        pltpu.make_async_copy(source, held, sems.at[i])
        for i, (source, held) in enumerate(((q_hbm, q_ref), (k_hbm, k_ref), (v_hbm, v_ref)))
    ]
    for load in loads:
        load.start()
    for c in weights:
        c.start()
    column = lax.broadcasted_iota(jnp.int32, (heads, span), 1)
    head = lax.broadcasted_iota(jnp.int32, (heads, span), 0)
    right_group = (column % kv) == (head // per_group)
    position = column // kv

    def at(r):
        return slice(r * heads, (r + 1) * heads)

    loads[0].wait()
    loads[1].wait()
    for r in range(rows):
        scores = lax.dot_general(
            q_ref[r], k_ref[r], (((1,), (1,)), ((), ())), preferred_element_type=F32
        ) * (1.0 / math.sqrt(dim))
        scores_ref[at(r), :] = jnp.where(right_group & (position < lengths[r]), scores, -1e30)
    for r in range(rows):
        scores = scores_ref[at(r), :]
        raw = jnp.exp(scores - jnp.max(scores, axis=-1, keepdims=True))
        probs_ref[at(r), :] = (raw * (1.0 / jnp.sum(raw, axis=-1, keepdims=True))).astype(BF16)
    loads[2].wait()
    for r in range(rows):
        att_ref[at(r), :] = jnp.dot(probs_ref[at(r), :], v_ref[r], preferred_element_type=F32)
    for h in range(heads):
        lanes = slice(h * dim, (h + 1) * dim)
        mine = att_ref[pl.ds(h, rows, stride=heads), :]
        out_ref[:, lanes] = (res_ref[:, lanes].astype(F32) + mine).astype(BF16)
    for c in weights:
        c.wait()


def attend(queries, cache_keys, stored_value_cache, lengths, residual, weights, ahead):
    rows, heads, dim = queries.shape
    kv = cache_keys.shape[2]
    span = cache_keys.shape[1] * kv
    held = [pltpu.VMEM((2, ahead, w.shape[1]), BF16) for w in weights[:1]]
    band_sems = [pltpu.SemaphoreType.DMA((2, ahead // BAND)) for _ in held]
    return pl.pallas_call(
        functools.partial(attend_kernel, kv, ahead),
        out_shape=(jax.ShapeDtypeStruct((rows, heads * dim), BF16), *held),
        in_specs=[SMEM, HBM, HBM, HBM, VMEM] + [HBM for _ in weights],
        out_specs=(VMEM,) + tuple(VMEM for _ in held),
        scratch_shapes=[
            pltpu.VMEM((rows * heads, dim), F32),
            pltpu.VMEM((rows * heads, span), F32),
            pltpu.VMEM((rows * heads, span), BF16),
            pltpu.VMEM(queries.shape, BF16),
            pltpu.VMEM((rows, span, dim), BF16),
            pltpu.VMEM((rows, span, dim), BF16),
            pltpu.SemaphoreType.DMA((3,)),
        ]
        + band_sems,
        compiler_params=params(8),
        cost_estimate=cost(rows * heads * span * dim * 4, rows * span * dim * 4),
        name="attention",
    )(
        in_hbm(lengths),
        in_hbm(queries),
        in_hbm(cache_keys.reshape(rows, span, dim)),
        in_hbm(stored_value_cache.reshape(rows, span, dim)),
        in_hbm(residual),
        *(in_hbm(w) for w in weights),
    )


def band_copies(g_hbm, u_hbm, held_ref, sems, first):
    return [
        pltpu.make_async_copy(
            w.at[pl.ds(pl.multiple_of(first + i * BAND, BAND), BAND)],
            held_ref.at[kind, pl.ds(i * BAND, BAND)],
            sems.at[kind, i],
        )
        for kind, w in enumerate((g_hbm, u_hbm))
        for i in range(held_ref.shape[1] // BAND)
    ]


def load_kernel(first, after_ref, g_hbm, u_hbm, held_ref, sems):
    copies = band_copies(g_hbm, u_hbm, held_ref, sems, first)
    for c in copies:
        c.start()
    for c in copies:
        c.wait()


def load_rows(after, gate_weight, up_weight, first, rows):
    columns = gate_weight.shape[1]
    return pl.pallas_call(
        functools.partial(load_kernel, first),
        out_shape=pltpu.VMEM((2, rows, columns), BF16),
        in_specs=[ANY, HBM, HBM],
        out_specs=VMEM,
        scratch_shapes=[pltpu.SemaphoreType.DMA((2, rows // BAND))],
        compiler_params=params(2),
        cost_estimate=cost(0, 4 * rows * columns),
        name="load_rows",
    )(after, in_hbm(gate_weight), in_hbm(up_weight))


def hold(array, after):
    return pl.pallas_call(
        lambda array_ref, after_ref, out_ref: None,
        out_shape=jax.ShapeDtypeStruct(array.shape, array.dtype),
        in_specs=[ANY, ANY],
        out_specs=ANY,
        input_output_aliases={0: 0},
        compiler_params=params(2),
        name="hold",
    )(array, after)


def pack_kernel(a_ref, b_ref, after_ref, out_ref):
    out_ref[0] = a_ref[...]
    out_ref[1] = b_ref[...]


def pack(a, b, after):
    return pl.pallas_call(
        pack_kernel,
        out_shape=jax.ShapeDtypeStruct((2,) + a.shape, a.dtype),
        in_specs=[VMEM, VMEM, ANY],
        out_specs=VMEM,
        compiler_params=params(4),
        name="pack",
    )(a, b, after)


def tile_at(index):
    return pl.ds(pl.multiple_of(index * TILE, TILE), TILE)


def gate_up_kernel(
    devices,
    held,
    *refs,
):
    a_ref, b_ref, c_ref, d_ref, g_hbm, u_hbm, w_hbm = refs[:7]
    held_refs = refs[7 : 7 + held]
    part_ref, rows_ref, far_ref, total_ref, buf, sems, far_sems = refs[7 + held :]
    nx = grid_of(devices)[1]
    slots = buf.shape[0]
    first = sum(ref.shape[1] for ref in held_refs)
    left = (g_hbm.shape[0] - first) // BAND

    def streamed(j):
        slot = lax.rem(j, slots)
        return band_copies(g_hbm, u_hbm, buf.at[slot], sems.at[slot], first + j * BAND)

    for j in range(min(slots, left)):
        for c in streamed(j):
            c.start()
    far_tiles = far_ref.shape[0] // TILE
    per_step = -(-far_tiles // left)
    far_base = half_base(devices, False, far_ref.shape[1])

    def far_copy(i):
        at = tile_at(i)
        return pltpu.make_async_copy(
            w_hbm.at[at, pl.ds(far_base, far_ref.shape[1])], far_ref.at[at], far_sems.at[i]
        )

    me = lax.axis_index(AXIS)
    my_z, my_x = me // nx, me % nx
    per = a_ref.shape[1]
    for near, far, flip in ((a_ref, b_ref, 0), (c_ref, d_ref, 1)):
        for i in range(2):
            z = my_z ^ (flip + 2 * i)
            here, there = near[i].astype(F32), far[i].astype(F32)
            pair = [jnp.where(my_x == 0, here, there), jnp.where(my_x == 0, there, here)]
            at = pl.ds(pl.multiple_of(z * (2 * per), 2 * per), 2 * per)
            rows_ref[at, :] = jnp.concatenate(pair, axis=0).astype(BF16)

    def add(at, weight, kind):
        total_ref[kind] += jnp.dot(rows_ref[:, at], weight, preferred_element_type=F32)

    total_ref[...] = jnp.zeros_like(total_ref)

    def step(j, _):
        start = 0
        for number, held_ref in enumerate(held_refs):
            stop = start + held_ref.shape[1]

            @pl.when(j == number * left // held)
            def _(start=start, stop=stop, held_ref=held_ref):
                for kind in range(2):
                    add(slice(start, stop), held_ref[kind], kind)

            start = stop
        slot = lax.rem(j, slots)
        for kind, c in enumerate(streamed(j)):
            c.wait()
            at = pl.ds(pl.multiple_of(first + j * BAND, BAND), BAND)
            add(at, buf[slot, kind], kind)

        @pl.when(j + slots < left)
        def _():
            for c in streamed(j + slots):
                c.start()

        for k in range(per_step):

            @pl.when(j * per_step + k < far_tiles)
            def _(k=k):
                far_copy(j * per_step + k).start()

        return 0

    lax.fori_loop(0, left, step, 0)
    part_ref[...] = total_ref[...].astype(BF16)
    for i in range(far_tiles):
        far_copy(i).wait()


def gate_up(blocks, gate_weight, up_weight, down_weight, held, devices, ahead):
    total = devices * blocks[0].shape[1]
    features, columns = gate_weight.shape
    slots = 2
    return pl.pallas_call(
        functools.partial(gate_up_kernel, devices, len(held)),
        out_shape=(
            jax.ShapeDtypeStruct((2, total, columns), BF16),
            jax.ShapeDtypeStruct((total, features), BF16),
            pltpu.VMEM((ahead, features // 2), BF16),
        ),
        in_specs=[VMEM] * 4 + [HBM] * 3 + [VMEM] * len(held),
        out_specs=(VMEM, VMEM, VMEM),
        scratch_shapes=[
            pltpu.VMEM((2, total, columns), F32),
            pltpu.VMEM((slots, 2, BAND, columns), BF16),
            pltpu.SemaphoreType.DMA((slots, 2, 1)),
            pltpu.SemaphoreType.DMA((ahead // TILE,)),
        ],
        compiler_params=params(GATE_MIB),
        cost_estimate=cost(4 * total * features * columns, 4 * features * columns),
        name="gate_up",
    )(
        *blocks,
        in_hbm(gate_weight),
        in_hbm(up_weight),
        in_hbm(down_weight),
        *(in_vmem(h) for h in held),
    )


def down_copies(w_hbm, base, held_ref, sems, first):
    rows, wide = held_ref.shape
    return [
        pltpu.make_async_copy(
            w_hbm.at[pl.ds(first + i * TILE, TILE), pl.ds(base, wide)],
            held_ref.at[pl.ds(i * TILE, TILE)],
            sems.at[i],
        )
        for i in range(rows // TILE)
    ]


def half_base(devices, mine, half):
    my_x = lax.axis_index(AXIS) % grid_of(devices)[1]
    return pl.multiple_of((my_x if mine else 1 - my_x) * half, half)


def quarter_base(devices, far, quarter, wide):
    my_x = lax.axis_index(AXIS) % grid_of(devices)[1]
    half = 1 - my_x if far else my_x
    return pl.multiple_of((2 * half + quarter) * wide, wide)


def pick(row_ref, capacity, first_slot, slots):
    row = row_ref[...]
    total = row.shape[1]
    down = lax.broadcasted_iota(jnp.int32, (total, total), 0)
    across = lax.broadcasted_iota(jnp.int32, (total, total), 1)
    diagonal = jnp.where(down == across, row, 0).astype(F32).astype(BF16)
    column = jnp.dot(diagonal, jnp.ones((total, total), BF16), preferred_element_type=F32)
    earlier = (column == row.astype(F32)) & (down < across)
    rank = jnp.sum(earlier.astype(F32), axis=0, keepdims=True).astype(jnp.int32)
    slot = first_slot + lax.broadcasted_iota(jnp.int32, (slots, total), 0)
    return (slot == row * capacity + rank).astype(F32).astype(BF16)


def prepare_kernel(
    devices, capacity, first, after_ref, row_ref, w_hbm, far_ref, near_ref, chosen_ref, far_sems, sems
):
    base = half_base(devices, False, far_ref.shape[1])
    copies = down_copies(w_hbm, base, far_ref, far_sems, first)
    base = quarter_base(devices, False, 0, near_ref.shape[1])
    copies += down_copies(w_hbm, base, near_ref, sems, 0)
    for c in copies:
        c.start()
    nz, nx = grid_of(devices)
    my_z = lax.axis_index(AXIS) // nx
    slots = chosen_ref.shape[0] // nz
    for i, bits in enumerate(ORDER):
        chosen_ref[i * slots : (i + 1) * slots, :] = pick(
            row_ref, capacity, (my_z ^ bits) * slots, slots
        )
    for c in copies:
        c.wait()


def prepare(after, row, down_weight, devices, capacity, first, near_rows):
    columns, features = down_weight.shape
    total = row.shape[1]
    far_rows = columns - first
    return pl.pallas_call(
        functools.partial(prepare_kernel, devices, capacity, first),
        out_shape=(
            pltpu.VMEM((far_rows, features // 2), BF16),
            pltpu.VMEM((near_rows, features // 4), BF16),
            jax.ShapeDtypeStruct((devices * 2 * capacity, total), BF16),
        ),
        in_specs=[ANY, VMEM, HBM],
        out_specs=(VMEM, VMEM, VMEM),
        scratch_shapes=[
            pltpu.SemaphoreType.DMA((far_rows // TILE,)),
            pltpu.SemaphoreType.DMA((near_rows // TILE,)),
        ],
        compiler_params=params(2),
        cost_estimate=cost(0, (2 * far_rows + near_rows) * features // 2),
        name="prepare",
    )(after, row, in_hbm(down_weight))


def down_kernel(devices, far, quarter, held_count, aheads, *refs):
    refs = list(refs)

    def take(count):
        return [refs.pop(0) for _ in range(count)]

    first_call = far and quarter == 0
    sources = take(2 if first_call else 1)
    arrived_ref, chosen_ref = (None, None) if far else take(2)
    held_refs = take(held_count)
    (w_hbm,) = take(1)
    out_refs = take(1 if far else 2)
    next_refs = take(len(aheads))
    (hidden_ref,) = take(1) if first_call else sources
    (total_ref,) = take(1)
    wide = total_ref.shape[1]
    ahead = []
    for (their, start, _), ref, sems in zip(aheads, next_refs, take(len(aheads))):
        ahead += down_copies(w_hbm, quarter_base(devices, False, their, wide), ref, sems, start)
    for c in ahead:
        c.start()
    if first_call:
        own_ref, other_ref = sources

        @pl.when(lax.axis_index(AXIS) >= 0)
        def _():
            gate = own_ref[0].astype(F32) + other_ref[0].astype(F32)
            up = own_ref[1].astype(F32) + other_ref[1].astype(F32)
            hidden_ref[...] = (gate / (1.0 + jnp.exp(-gate)) * up).astype(BF16)

    if far:
        total_ref[...] = jnp.zeros_like(total_ref)
    else:
        total_ref[...] = arrived_ref[...].astype(F32)
    @pl.when(lax.axis_index(AXIS) >= 0)
    def _():
        start = 0
        for held_ref in held_refs:
            stop = start + held_ref.shape[0]
            at = slice(quarter * wide, (quarter + 1) * wide) if far else slice(None)
            total_ref[...] += jnp.dot(
                hidden_ref[:, start:stop], held_ref[:, at], preferred_element_type=F32
            )
            start = stop

    rounded = total_ref[...].astype(BF16)
    if far:
        out_refs[0][...] = rounded
    else:
        slots = out_refs[0].shape[0]
        for i, ref in enumerate(out_refs):
            chosen = chosen_ref[i * slots : (i + 1) * slots]
            ref[...] = jnp.dot(chosen, rounded, preferred_element_type=F32).astype(BF16)
    for c in ahead:
        c.wait()


def down(sources, held, down_weight, devices, far, quarter, aheads=()):
    total = sources[0].shape[-2]
    columns, features = down_weight.shape
    wide = features // 4
    if far:
        out_shape = [jax.ShapeDtypeStruct((total, wide), BF16)]
    else:
        out_shape = [jax.ShapeDtypeStruct((sources[2].shape[0] // 2, wide), BF16)] * 2
    out_shape += [pltpu.VMEM((rows, wide), BF16) for _, _, rows in aheads]
    if far and quarter == 0:
        out_shape.append(jax.ShapeDtypeStruct((total, columns), BF16))
    return pl.pallas_call(
        functools.partial(down_kernel, devices, far, quarter, len(held), aheads),
        out_shape=tuple(out_shape),
        in_specs=[VMEM] * (len(sources) + len(held)) + [HBM],
        out_specs=tuple(VMEM for _ in out_shape),
        scratch_shapes=[pltpu.VMEM((total, wide), F32)]
        + [pltpu.SemaphoreType.DMA((rows // TILE,)) for _, _, rows in aheads],
        compiler_params=params(6),
        cost_estimate=COST,
        name="down_far" if far else "down_near",
    )(*sources, *(in_vmem(h) for h in held), in_hbm(down_weight))


def add_kernel(keep_ref, came_ref, own_ref, send_ref):
    slots = own_ref.shape[0]
    total = keep_ref[...].astype(F32) + came_ref[...].astype(F32)
    own_ref[...] = total[:slots]
    send_ref[...] = total[slots:].astype(BF16)


def add(keep, came):
    slots, wide = keep.shape
    return pl.pallas_call(
        add_kernel,
        out_shape=(
            jax.ShapeDtypeStruct((slots // 2, wide), F32),
            jax.ShapeDtypeStruct((slots // 2, wide), BF16),
        ),
        in_specs=[VMEM, VMEM],
        out_specs=(VMEM, VMEM),
        compiler_params=params(4),
        name="add",
    )(keep, came)


def finish_kernel(devices, chosen_ref, rows_ref, *refs):
    own_refs, came_refs, (keep_ref, send_ref) = refs[:2], refs[2:4], refs[4:]
    my_x = lax.axis_index(AXIS) % grid_of(devices)[1]
    slots, wide = own_refs[0].shape
    half = slots // 2
    for quarter, (own_ref, came_ref) in enumerate(zip(own_refs, came_refs)):
        mixed = rows_ref[:, pl.ds(quarter_base(devices, False, quarter, wide), wide)]
        done = jnp.dot(chosen_ref[:slots], mixed, preferred_element_type=F32)
        done = done + (own_ref[...] + came_ref[...].astype(F32))
        first, second = done[:half], done[half:]
        at = slice(quarter * wide, (quarter + 1) * wide)
        keep_ref[:, at] = jnp.where(my_x == 0, first, second).astype(BF16)
        send_ref[:, at] = jnp.where(my_x == 0, second, first).astype(BF16)


def finish(chosen, rows, own, came, devices):
    slots, wide = own[0].shape
    shape = jax.ShapeDtypeStruct((slots // 2, 2 * wide), BF16)
    return pl.pallas_call(
        functools.partial(finish_kernel, devices),
        out_shape=(shape, shape),
        in_specs=[VMEM] * 6,
        out_specs=(VMEM, VMEM),
        compiler_params=params(6),
        name="finish",
    )(chosen, rows, *own, *came)


def join_kernel(nx, keep_ref, other_ref, out_ref):
    my_x = lax.axis_index(AXIS) % nx
    width = keep_ref.shape[1]
    out_ref[:, :width] = jnp.where(my_x == 0, keep_ref[...], other_ref[...])
    out_ref[:, width:] = jnp.where(my_x == 0, other_ref[...], keep_ref[...])


def join(keep, other, devices):
    slots, width = keep.shape
    return pl.pallas_call(
        functools.partial(join_kernel, grid_of(devices)[1]),
        out_shape=jax.ShapeDtypeStruct((slots, 2 * width), BF16),
        in_specs=[VMEM, VMEM],
        out_specs=VMEM,
        compiler_params=params(8),
        name="join_halves",
    )(keep, other)


def slot_positions(column, destinations, capacity):
    onehot = (column[:, None] == jnp.arange(destinations, dtype=jnp.int32)[None, :]).astype(
        jnp.int32
    )
    before = jnp.cumsum(onehot, axis=0) - onehot
    slot_rank = jnp.sum(before * onehot, axis=1)
    return column * capacity + slot_rank


def plain(mixed_rows, target, gate_weight, up_weight, down_weight, devices):
    rows_dev, features = mixed_rows.shape
    me = lax.axis_index(AXIS)
    gathered = lax.all_gather(mixed_rows, AXIS, axis=0, tiled=True)
    mine = jnp.stack(
        [
            jnp.dot(gathered, gate_weight, preferred_element_type=F32),
            jnp.dot(gathered, up_weight, preferred_element_type=F32),
        ]
    )
    other = lax.ppermute(mine.astype(BF16), "ffn", [(0, 1), (1, 0)])
    gate_sum, up_sum = mine + other.astype(F32)
    hidden = (jax.nn.silu(gate_sum) * up_sum).astype(BF16)
    down = jnp.dot(hidden, down_weight, preferred_element_type=F32)
    share = features // devices
    landed = lax.all_to_all(
        jnp.moveaxis(down.astype(BF16).reshape(-1, devices, share), 1, 0), AXIS, 0, 0
    )
    summed = jnp.sum(landed.astype(F32), axis=0)
    mixed_share = lax.dynamic_slice_in_dim(gathered, me * share, share, axis=1)
    finished = (mixed_share.astype(F32) + summed).astype(BF16)
    slot_count = 2 * devices * rows_dev
    position = slot_positions(target[:, 0], 2 * devices, rows_dev)
    chosen = (jnp.arange(slot_count, dtype=jnp.int32)[:, None] == position[None, :]).astype(BF16)
    slots = jnp.dot(chosen, finished, preferred_element_type=F32).astype(BF16)
    slots = slots.reshape(devices, 2 * rows_dev, share)
    mine_out = lax.all_to_all(slots, AXIS, split_axis=0, concat_axis=0)
    return jnp.moveaxis(mine_out, 0, 1).reshape(2 * rows_dev, features)


def local(
    queries,
    cache_keys,
    stored_value_cache,
    lengths,
    residual,
    target,
    gate_weight,
    up_weight,
    down_weight,
):
    devices = lax.axis_size(AXIS)
    nz, nx = grid_of(devices)
    capacity = cache_keys.shape[0]
    columns, features = down_weight.shape
    fits = nz == 4 and nx == 2 and columns % TILE == 0 and features == 16 * BAND
    mixed_rows, *held = attend(
        queries,
        cache_keys,
        stored_value_cache,
        lengths,
        residual,
        (gate_weight, up_weight) if fits else (),
        2 * BAND if fits else 0,
    )
    if not fits:
        return plain(mixed_rows, target, gate_weight, up_weight, down_weight, devices)

    two = lax.ppermute(mixed_rows, AXIS, swap_z(devices, 2))
    held.append(load_rows(mixed_rows, gate_weight, up_weight, 2 * BAND, 2 * BAND))
    a = pack(mixed_rows, two, held[-1])
    b = lax.ppermute(a, AXIS, swap_x(devices))
    c = lax.ppermute(a, AXIS, swap_z(devices, 1))
    held.append(load_rows(a, gate_weight, up_weight, 4 * BAND, 2 * BAND))
    c = hold(c, held[-1])
    d = lax.ppermute(c, AXIS, swap_x(devices))
    held.append(load_rows(c, gate_weight, up_weight, 6 * BAND, 2 * BAND))
    tiles = columns // TILE
    far_cut = 11 * tiles // 13 * TILE
    first = 6 * tiles // 13 * TILE
    cut = 2 * tiles // 13 * TILE, 8 * tiles // 13 * TILE
    part, rows, far_a = gate_up(
        (a, b, c, d), gate_weight, up_weight, down_weight, held, devices, far_cut
    )
    other = lax.ppermute(part, "ffn", [(0, 1), (1, 0)])
    far_b, near_a, chosen = prepare(
        part, target.reshape(1, -1), down_weight, devices, capacity, far_cut, first
    )
    held_far = far_a, far_b

    far, near_b, near_c, hidden = down(
        (part, other),
        held_far,
        down_weight,
        devices,
        True,
        0,
        ((0, first, columns - first), (1, 0, cut[0])),
    )
    arrived = [lax.ppermute(far, AXIS, swap_x(devices))]
    far, near_d = down(
        (hidden,), held_far, down_weight, devices, True, 1, ((1, cut[0], cut[1] - cut[0]),)
    )
    arrived.append(lax.ppermute(far, AXIS, swap_x(devices)))
    keep_a, send_a, near_e = down(
        (hidden, arrived[0], chosen),
        (near_a, near_b),
        down_weight,
        devices,
        False,
        0,
        ((1, cut[1], columns - cut[1]),),
    )
    came_a = lax.ppermute(send_a, AXIS, swap_z(devices, 1))
    keep_b, send_b = down(
        (hidden, arrived[1], chosen), (near_c, near_d, near_e), down_weight, devices, False, 1
    )
    came_b = lax.ppermute(send_b, AXIS, swap_z(devices, 1))
    own, came = [], []
    for keep, arrived in ((keep_a, came_a), (keep_b, came_b)):
        mine, send = add(keep, arrived)
        own.append(mine)
        came.append(lax.ppermute(send, AXIS, swap_z(devices, 2)))
    keep, send = finish(chosen, rows, own, came, devices)
    return join(keep, lax.ppermute(send, AXIS, swap_x(devices)), devices)


def solution(mesh):
    return jax.shard_map(
        local,
        mesh=mesh,
        in_specs=(
            P(("parts", "attn"), "ffn", None),
            P(("parts", "attn"), None, "ffn", None),
            P(("parts", "attn"), None, "ffn", None),
            P(("parts", "attn")),
            P(("parts", "attn"), "ffn"),
            P("parts", None),
            P("ffn", "attn"),
            P("ffn", "attn"),
            P("attn", "ffn"),
        ),
        out_specs=P(("parts", "attn"), "ffn"),
        check_vma=False,
    )
```

```python
import functools
import math

import jax
import jax.numpy as jnp
from jax import lax
from jax.experimental import pallas as pl
from jax.experimental.pallas import tpu as pltpu
from jax.sharding import PartitionSpec as P

AXIS = "attn"
TILE = 256
BAND = 256
GATE_MIB = 11
ORDER = (0, 2, 1, 3)
MIB = 1 << 20
VMEM = pl.BlockSpec(memory_space=pltpu.VMEM)
SMEM = pl.BlockSpec(memory_space=pltpu.SMEM)
ANY = pl.BlockSpec(memory_space=pl.ANY)
HBM = pl.BlockSpec(memory_space=pltpu.HBM)
F32 = jnp.float32
BF16 = jnp.bfloat16


def params(mib):
    return pltpu.CompilerParams(vmem_limit_bytes=mib * MIB)


def in_vmem(array):
    return pltpu.with_memory_space_constraint(array, pltpu.VMEM)


def in_hbm(array):
    return pltpu.with_memory_space_constraint(array, pltpu.HBM)


def cost(flops, moved):
    return pl.CostEstimate(flops=flops, bytes_accessed=moved, transcendentals=0)


def grid_of(devices):
    nx = 1
    while 4 * nx * nx < devices:
        nx *= 2
    if devices % nx:
        nx = 1
    return devices // nx, nx


def swap_z(devices, bits):
    nz, nx = grid_of(devices)
    return [(z * nx + x, (z ^ bits) * nx + x) for z in range(nz) for x in range(nx)]


def swap_x(devices, bits=0):
    nz, nx = grid_of(devices)
    return [(z * nx + x, (z ^ bits) * nx + (x ^ 1)) for z in range(nz) for x in range(nx)]


COST = cost(0, 1024)


def attend_kernel(
    kv, lengths, q_hbm, k_hbm, v_hbm, res_ref, up_hbm, out_ref, att_ref, scores_ref, probs_ref, q_ref, k_ref, v_ref, sems
):
    rows, heads, dim = q_ref.shape
    span = k_ref.shape[1]
    per_group = heads // kv
    loads = [
        pltpu.make_async_copy(source, held, sems.at[i])
        for i, (source, held) in enumerate(((q_hbm, q_ref), (k_hbm, k_ref), (v_hbm, v_ref)))
    ]
    for load in loads:
        load.start()
    column = lax.broadcasted_iota(jnp.int32, (heads, span), 1)
    head = lax.broadcasted_iota(jnp.int32, (heads, span), 0)
    right_group = (column % kv) == (head // per_group)
    position = column // kv

    def at(r):
        return slice(r * heads, (r + 1) * heads)

    loads[0].wait()
    loads[1].wait()
    for r in range(rows):
        scores = lax.dot_general(
            q_ref[r], k_ref[r], (((1,), (1,)), ((), ())), preferred_element_type=F32
        ) * (1.0 / math.sqrt(dim))
        scores_ref[at(r), :] = jnp.where(right_group & (position < lengths[r]), scores, -1e30)
    for r in range(rows):
        scores = scores_ref[at(r), :]
        raw = jnp.exp(scores - jnp.max(scores, axis=-1, keepdims=True))
        probs_ref[at(r), :] = (raw * (1.0 / jnp.sum(raw, axis=-1, keepdims=True))).astype(BF16)
    loads[2].wait()
    for r in range(rows):
        att_ref[at(r), :] = jnp.dot(probs_ref[at(r), :], v_ref[r], preferred_element_type=F32)
    for h in range(heads):
        lanes = slice(h * dim, (h + 1) * dim)
        mine = att_ref[pl.ds(h, rows, stride=heads), :]
        out_ref[:, lanes] = (res_ref[:, lanes].astype(F32) + mine).astype(BF16)


def attend(queries, cache_keys, stored_value_cache, lengths, residual, up):
    rows, heads, dim = queries.shape
    kv = cache_keys.shape[2]
    span = cache_keys.shape[1] * kv
    return pl.pallas_call(
        functools.partial(attend_kernel, kv),
        out_shape=jax.ShapeDtypeStruct((rows, heads * dim), BF16),
        in_specs=[SMEM, HBM, HBM, HBM, VMEM, HBM],
        out_specs=VMEM,
        scratch_shapes=[
            pltpu.VMEM((rows * heads, dim), F32),
            pltpu.VMEM((rows * heads, span), F32),
            pltpu.VMEM((rows * heads, span), BF16),
            pltpu.VMEM(queries.shape, BF16),
            pltpu.VMEM((rows, span, dim), BF16),
            pltpu.VMEM((rows, span, dim), BF16),
            pltpu.SemaphoreType.DMA((3,)),
        ],
        compiler_params=params(8),
        cost_estimate=cost(rows * heads * span * dim * 4, rows * span * dim * 4),
        name="attention",
    )(
        in_hbm(lengths),
        in_hbm(queries),
        in_hbm(cache_keys.reshape(rows, span, dim)),
        in_hbm(stored_value_cache.reshape(rows, span, dim)),
        in_hbm(residual),
        in_hbm(up),
    )


def row_copy(w_hbm, held_ref, sem, first):
    rows = pl.ds(pl.multiple_of(first, BAND), BAND)
    return pltpu.make_async_copy(w_hbm.at[rows], held_ref, sem)


def pack_kernel(*refs):
    *block_refs, out_ref = refs
    for i, ref in enumerate(block_refs):
        out_ref[i] = ref[...]


def pack(*blocks):
    return pl.pallas_call(
        pack_kernel,
        out_shape=jax.ShapeDtypeStruct((len(blocks),) + blocks[0].shape, BF16),
        in_specs=[VMEM] * len(blocks),
        out_specs=VMEM,
        compiler_params=params(4),
        name="pack",
    )(*blocks)


def tile_at(index):
    return pl.ds(pl.multiple_of(index * TILE, TILE), TILE)


def gate_up_kernel(
    devices,
    a_ref,
    c_ref,
    d_ref,
    e_ref,
    u_hbm,
    w_hbm,
    gate_ref,
    part_ref,
    rows_ref,
    far_ref,
    total_ref,
    buf,
    sems,
    far_sems,
):
    nx = grid_of(devices)[1]
    slots = buf.shape[0]
    left = u_hbm.shape[0] // BAND

    def streamed(j):
        slot = lax.rem(j, slots)
        return row_copy(u_hbm, buf.at[slot], sems.at[slot], j * BAND)

    for j in range(min(slots, left)):
        streamed(j).start()
    far_tiles = far_ref.shape[0] // TILE
    per_step = -(-far_tiles // left)
    far_base = half_base(devices, False, far_ref.shape[1])

    def far_copy(i):
        at = tile_at(i)
        return pltpu.make_async_copy(
            w_hbm.at[at, pl.ds(far_base, far_ref.shape[1])], far_ref.at[at], far_sems.at[i]
        )

    me = lax.axis_index(AXIS)
    my_z, my_x = me // nx, me % nx
    per = a_ref.shape[1]
    for bits, near, far in (
        (0, a_ref[0], a_ref[2]),
        (1, c_ref[0], c_ref[2]),
        (2, a_ref[1], d_ref[...]),
        (3, c_ref[1], e_ref[...]),
    ):
        here, there = near.astype(F32), far.astype(F32)
        pair = [jnp.where(my_x == 0, here, there), jnp.where(my_x == 0, there, here)]
        at = pl.ds(pl.multiple_of((my_z ^ bits) * (2 * per), 2 * per), 2 * per)
        rows_ref[at, :] = jnp.concatenate(pair, axis=0).astype(BF16)

    def add(at, weight, kind):
        total_ref[kind] += jnp.dot(rows_ref[:, at], weight, preferred_element_type=F32)

    total_ref[...] = jnp.zeros_like(total_ref)

    def step(j, _):
        at = pl.ds(pl.multiple_of(j * BAND, BAND), BAND)
        add(at, gate_ref[at, :], 0)
        streamed(j).wait()
        add(at, buf[lax.rem(j, slots)], 1)

        @pl.when(j + slots < left)
        def _():
            streamed(j + slots).start()

        for k in range(per_step):

            @pl.when(j * per_step + k < far_tiles)
            def _(k=k):
                far_copy(j * per_step + k).start()

        return 0

    lax.fori_loop(0, left, step, 0)
    part_ref[...] = total_ref[...].astype(BF16)
    for i in range(far_tiles):
        far_copy(i).wait()


def gate_up(blocks, gate_weight, up_weight, down_weight, devices, ahead):
    total = devices * blocks[0].shape[1]
    features, columns = gate_weight.shape
    slots = 4
    return pl.pallas_call(
        functools.partial(gate_up_kernel, devices),
        out_shape=(
            jax.ShapeDtypeStruct((2, total, columns), BF16),
            jax.ShapeDtypeStruct((total, features), BF16),
            pltpu.VMEM((ahead, features // 2), BF16),
        ),
        in_specs=[VMEM] * 4 + [HBM] * 2 + [VMEM],
        out_specs=(VMEM, VMEM, VMEM),
        scratch_shapes=[
            pltpu.VMEM((2, total, columns), F32),
            pltpu.VMEM((slots, BAND, columns), BF16),
            pltpu.SemaphoreType.DMA((slots,)),
            pltpu.SemaphoreType.DMA((ahead // TILE,)),
        ],
        compiler_params=params(GATE_MIB),
        cost_estimate=cost(4 * total * features * columns, 4 * features * columns),
        name="gate_up",
    )(
        *blocks,
        in_hbm(up_weight),
        in_hbm(down_weight),
        in_vmem(gate_weight),
    )


def down_copies(w_hbm, base, held_ref, sems, first):
    rows, wide = held_ref.shape
    return [
        pltpu.make_async_copy(
            w_hbm.at[pl.ds(first + i * TILE, TILE), pl.ds(base, wide)],
            held_ref.at[pl.ds(i * TILE, TILE)],
            sems.at[i],
        )
        for i in range(rows // TILE)
    ]


def half_base(devices, mine, half):
    my_x = lax.axis_index(AXIS) % grid_of(devices)[1]
    return pl.multiple_of((my_x if mine else 1 - my_x) * half, half)


def quarter_base(devices, far, quarter, wide):
    my_x = lax.axis_index(AXIS) % grid_of(devices)[1]
    half = 1 - my_x if far else my_x
    return pl.multiple_of((2 * half + quarter) * wide, wide)


def pick(row_ref, capacity, first_slot, slots):
    row = row_ref[...]
    total = row.shape[1]
    down = lax.broadcasted_iota(jnp.int32, (total, total), 0)
    across = lax.broadcasted_iota(jnp.int32, (total, total), 1)
    diagonal = jnp.where(down == across, row, 0).astype(F32).astype(BF16)
    column = jnp.dot(diagonal, jnp.ones((total, total), BF16), preferred_element_type=F32)
    earlier = (column == row.astype(F32)) & (down < across)
    rank = jnp.sum(earlier.astype(F32), axis=0, keepdims=True).astype(jnp.int32)
    slot = first_slot + lax.broadcasted_iota(jnp.int32, (slots, total), 0)
    return (slot == row * capacity + rank).astype(F32).astype(BF16)


def prepare_kernel(
    devices, capacity, first, after_ref, row_ref, w_hbm, far_ref, near_ref, chosen_ref, far_sems, sems
):
    base = half_base(devices, False, far_ref.shape[1])
    copies = down_copies(w_hbm, base, far_ref, far_sems, first)
    base = quarter_base(devices, False, 0, near_ref.shape[1])
    copies += down_copies(w_hbm, base, near_ref, sems, 0)
    for c in copies:
        c.start()
    nz, nx = grid_of(devices)
    my_z = lax.axis_index(AXIS) // nx
    slots = chosen_ref.shape[0] // nz
    for i, bits in enumerate(ORDER):
        chosen_ref[i * slots : (i + 1) * slots, :] = pick(
            row_ref, capacity, (my_z ^ bits) * slots, slots
        )
    for c in copies:
        c.wait()


def prepare(after, row, down_weight, devices, capacity, first, near_rows):
    columns, features = down_weight.shape
    total = row.shape[1]
    far_rows = columns - first
    return pl.pallas_call(
        functools.partial(prepare_kernel, devices, capacity, first),
        out_shape=(
            pltpu.VMEM((far_rows, features // 2), BF16),
            pltpu.VMEM((near_rows, features // 4), BF16),
            jax.ShapeDtypeStruct((devices * 2 * capacity, total), BF16),
        ),
        in_specs=[ANY, VMEM, HBM],
        out_specs=(VMEM, VMEM, VMEM),
        scratch_shapes=[
            pltpu.SemaphoreType.DMA((far_rows // TILE,)),
            pltpu.SemaphoreType.DMA((near_rows // TILE,)),
        ],
        compiler_params=params(2),
        cost_estimate=cost(0, (2 * far_rows + near_rows) * features // 2),
        name="prepare",
    )(after, row, in_hbm(down_weight))


def down_kernel(devices, far, quarter, held_count, aheads, *refs):
    refs = list(refs)

    def take(count):
        return [refs.pop(0) for _ in range(count)]

    first_call = far and quarter == 0
    sources = take(2 if first_call else 1)
    arrived_ref, chosen_ref = (None, None) if far else take(2)
    held_refs = take(held_count)
    (w_hbm,) = take(1)
    out_refs = take(1 if far else 2)
    next_refs = take(len(aheads))
    (hidden_ref,) = take(1) if first_call else sources
    (total_ref,) = take(1)
    wide = total_ref.shape[1]
    ahead = []
    for (their, start, _), ref, sems in zip(aheads, next_refs, take(len(aheads))):
        ahead += down_copies(w_hbm, quarter_base(devices, False, their, wide), ref, sems, start)
    for c in ahead:
        c.start()
    if first_call:
        own_ref, other_ref = sources

        @pl.when(lax.axis_index(AXIS) >= 0)
        def _():
            gate = own_ref[0].astype(F32) + other_ref[0].astype(F32)
            up = own_ref[1].astype(F32) + other_ref[1].astype(F32)
            hidden_ref[...] = (gate / (1.0 + jnp.exp(-gate)) * up).astype(BF16)

    if far:
        total_ref[...] = jnp.zeros_like(total_ref)
    else:
        total_ref[...] = arrived_ref[...].astype(F32)
    @pl.when(lax.axis_index(AXIS) >= 0)
    def _():
        start = 0
        for held_ref in held_refs:
            stop = start + held_ref.shape[0]
            at = slice(quarter * wide, (quarter + 1) * wide) if far else slice(None)
            total_ref[...] += jnp.dot(
                hidden_ref[:, start:stop], held_ref[:, at], preferred_element_type=F32
            )
            start = stop

    rounded = total_ref[...].astype(BF16)
    if far:
        out_refs[0][...] = rounded
    else:
        slots = out_refs[0].shape[0]
        for i, ref in enumerate(out_refs):
            chosen = chosen_ref[i * slots : (i + 1) * slots]
            ref[...] = jnp.dot(chosen, rounded, preferred_element_type=F32).astype(BF16)
    for c in ahead:
        c.wait()


def down(sources, held, down_weight, devices, far, quarter, aheads=()):
    total = sources[0].shape[-2]
    columns, features = down_weight.shape
    wide = features // 4
    if far:
        out_shape = [jax.ShapeDtypeStruct((total, wide), BF16)]
    else:
        out_shape = [jax.ShapeDtypeStruct((sources[2].shape[0] // 2, wide), BF16)] * 2
    out_shape += [pltpu.VMEM((rows, wide), BF16) for _, _, rows in aheads]
    if far and quarter == 0:
        out_shape.append(jax.ShapeDtypeStruct((total, columns), BF16))
    return pl.pallas_call(
        functools.partial(down_kernel, devices, far, quarter, len(held), aheads),
        out_shape=tuple(out_shape),
        in_specs=[VMEM] * (len(sources) + len(held)) + [HBM],
        out_specs=tuple(VMEM for _ in out_shape),
        scratch_shapes=[pltpu.VMEM((total, wide), F32)]
        + [pltpu.SemaphoreType.DMA((rows // TILE,)) for _, _, rows in aheads],
        compiler_params=params(6),
        cost_estimate=COST,
        name="down_far" if far else "down_near",
    )(*sources, *(in_vmem(h) for h in held), in_hbm(down_weight))


def add_kernel(keep_ref, came_ref, own_ref, send_ref):
    slots = own_ref.shape[0]
    total = keep_ref[...].astype(F32) + came_ref[...].astype(F32)
    own_ref[...] = total[:slots]
    send_ref[...] = total[slots:].astype(BF16)


def add(keep, came):
    slots, wide = keep.shape
    return pl.pallas_call(
        add_kernel,
        out_shape=(
            jax.ShapeDtypeStruct((slots // 2, wide), F32),
            jax.ShapeDtypeStruct((slots // 2, wide), BF16),
        ),
        in_specs=[VMEM, VMEM],
        out_specs=(VMEM, VMEM),
        compiler_params=params(4),
        name="add",
    )(keep, came)


def finish_kernel(devices, chosen_ref, rows_ref, *refs):
    own_refs, came_refs, (keep_ref, send_ref) = refs[:2], refs[2:4], refs[4:]
    my_x = lax.axis_index(AXIS) % grid_of(devices)[1]
    slots, wide = own_refs[0].shape
    half = slots // 2
    for quarter, (own_ref, came_ref) in enumerate(zip(own_refs, came_refs)):
        mixed = rows_ref[:, pl.ds(quarter_base(devices, False, quarter, wide), wide)]
        done = jnp.dot(chosen_ref[:slots], mixed, preferred_element_type=F32)
        done = done + (own_ref[...] + came_ref[...].astype(F32))
        first, second = done[:half], done[half:]
        at = slice(quarter * wide, (quarter + 1) * wide)
        keep_ref[:, at] = jnp.where(my_x == 0, first, second).astype(BF16)
        send_ref[:, at] = jnp.where(my_x == 0, second, first).astype(BF16)


def finish(chosen, rows, own, came, devices):
    slots, wide = own[0].shape
    shape = jax.ShapeDtypeStruct((slots // 2, 2 * wide), BF16)
    return pl.pallas_call(
        functools.partial(finish_kernel, devices),
        out_shape=(shape, shape),
        in_specs=[VMEM] * 6,
        out_specs=(VMEM, VMEM),
        compiler_params=params(6),
        name="finish",
    )(chosen, rows, *own, *came)


def join_kernel(nx, keep_ref, other_ref, out_ref):
    my_x = lax.axis_index(AXIS) % nx
    width = keep_ref.shape[1]
    out_ref[:, :width] = jnp.where(my_x == 0, keep_ref[...], other_ref[...])
    out_ref[:, width:] = jnp.where(my_x == 0, other_ref[...], keep_ref[...])


def join(keep, other, devices):
    slots, width = keep.shape
    return pl.pallas_call(
        functools.partial(join_kernel, grid_of(devices)[1]),
        out_shape=jax.ShapeDtypeStruct((slots, 2 * width), BF16),
        in_specs=[VMEM, VMEM],
        out_specs=VMEM,
        compiler_params=params(8),
        name="join_halves",
    )(keep, other)


def slot_positions(column, destinations, capacity):
    onehot = (column[:, None] == jnp.arange(destinations, dtype=jnp.int32)[None, :]).astype(
        jnp.int32
    )
    before = jnp.cumsum(onehot, axis=0) - onehot
    slot_rank = jnp.sum(before * onehot, axis=1)
    return column * capacity + slot_rank


def plain(mixed_rows, target, gate_weight, up_weight, down_weight, devices):
    rows_dev, features = mixed_rows.shape
    me = lax.axis_index(AXIS)
    gathered = lax.all_gather(mixed_rows, AXIS, axis=0, tiled=True)
    mine = jnp.stack(
        [
            jnp.dot(gathered, gate_weight, preferred_element_type=F32),
            jnp.dot(gathered, up_weight, preferred_element_type=F32),
        ]
    )
    other = lax.ppermute(mine.astype(BF16), "ffn", [(0, 1), (1, 0)])
    gate_sum, up_sum = mine + other.astype(F32)
    hidden = (jax.nn.silu(gate_sum) * up_sum).astype(BF16)
    down = jnp.dot(hidden, down_weight, preferred_element_type=F32)
    share = features // devices
    landed = lax.all_to_all(
        jnp.moveaxis(down.astype(BF16).reshape(-1, devices, share), 1, 0), AXIS, 0, 0
    )
    summed = jnp.sum(landed.astype(F32), axis=0)
    mixed_share = lax.dynamic_slice_in_dim(gathered, me * share, share, axis=1)
    finished = (mixed_share.astype(F32) + summed).astype(BF16)
    slot_count = 2 * devices * rows_dev
    position = slot_positions(target[:, 0], 2 * devices, rows_dev)
    chosen = (jnp.arange(slot_count, dtype=jnp.int32)[:, None] == position[None, :]).astype(BF16)
    slots = jnp.dot(chosen, finished, preferred_element_type=F32).astype(BF16)
    slots = slots.reshape(devices, 2 * rows_dev, share)
    mine_out = lax.all_to_all(slots, AXIS, split_axis=0, concat_axis=0)
    return jnp.moveaxis(mine_out, 0, 1).reshape(2 * rows_dev, features)


def local(
    queries,
    cache_keys,
    stored_value_cache,
    lengths,
    residual,
    target,
    gate_weight,
    up_weight,
    down_weight,
):
    devices = lax.axis_size(AXIS)
    nz, nx = grid_of(devices)
    capacity = cache_keys.shape[0]
    columns, features = down_weight.shape
    fits = nz == 4 and nx == 2 and columns % TILE == 0 and features == 16 * BAND
    mixed_rows = attend(queries, cache_keys, stored_value_cache, lengths, residual, up_weight)
    if not fits:
        return plain(mixed_rows, target, gate_weight, up_weight, down_weight, devices)

    two = lax.ppermute(mixed_rows, AXIS, swap_z(devices, 2))
    side = lax.ppermute(mixed_rows, AXIS, swap_x(devices))
    e = lax.ppermute(mixed_rows, AXIS, swap_x(devices, 3))
    a = pack(mixed_rows, two, side)
    c = lax.ppermute(a, AXIS, swap_z(devices, 1))
    d = lax.ppermute(two, AXIS, swap_x(devices))
    tiles = columns // TILE
    far_cut = 11 * tiles // 13 * TILE
    first = 6 * tiles // 13 * TILE
    cut = 2 * tiles // 13 * TILE, 8 * tiles // 13 * TILE
    part, rows, far_a = gate_up(
        (a, c, d, e), gate_weight, up_weight, down_weight, devices, far_cut
    )
    other = lax.ppermute(part, "ffn", [(0, 1), (1, 0)])
    far_b, near_a, chosen = prepare(
        part, target.reshape(1, -1), down_weight, devices, capacity, far_cut, first
    )
    held_far = far_a, far_b

    far, near_b, near_c, hidden = down(
        (part, other),
        held_far,
        down_weight,
        devices,
        True,
        0,
        ((0, first, columns - first), (1, 0, cut[0])),
    )
    arrived = [lax.ppermute(far, AXIS, swap_x(devices))]
    far, near_d = down(
        (hidden,), held_far, down_weight, devices, True, 1, ((1, cut[0], cut[1] - cut[0]),)
    )
    arrived.append(lax.ppermute(far, AXIS, swap_x(devices)))
    keep_a, send_a, near_e = down(
        (hidden, arrived[0], chosen),
        (near_a, near_b),
        down_weight,
        devices,
        False,
        0,
        ((1, cut[1], columns - cut[1]),),
    )
    came_a = lax.ppermute(send_a, AXIS, swap_z(devices, 1))
    keep_b, send_b = down(
        (hidden, arrived[1], chosen), (near_c, near_d, near_e), down_weight, devices, False, 1
    )
    came_b = lax.ppermute(send_b, AXIS, swap_z(devices, 1))
    own, came = [], []
    for keep, arrived in ((keep_a, came_a), (keep_b, came_b)):
        mine, send = add(keep, arrived)
        own.append(mine)
        came.append(lax.ppermute(send, AXIS, swap_z(devices, 2)))
    keep, send = finish(chosen, rows, own, came, devices)
    return join(keep, lax.ppermute(send, AXIS, swap_x(devices)), devices)


def solution(mesh):
    return jax.shard_map(
        local,
        mesh=mesh,
        in_specs=(
            P(("parts", "attn"), "ffn", None),
            P(("parts", "attn"), None, "ffn", None),
            P(("parts", "attn"), None, "ffn", None),
            P(("parts", "attn")),
            P(("parts", "attn"), "ffn"),
            P("parts", None),
            P("ffn", "attn"),
            P("ffn", "attn"),
            P("attn", "ffn"),
        ),
        out_specs=P(("parts", "attn"), "ffn"),
        check_vma=False,
    )
```

```python
import functools
import math

import jax
import jax.numpy as jnp
from jax import lax
from jax.experimental import pallas as pl
from jax.experimental.pallas import tpu as pltpu
from jax.sharding import PartitionSpec as P

AXIS = "attn"
TILE = 256
BAND = 256
GATE_MIB = 11
ORDER = (0, 2, 1, 3)
MIB = 1 << 20
VMEM = pl.BlockSpec(memory_space=pltpu.VMEM)
SMEM = pl.BlockSpec(memory_space=pltpu.SMEM)
ANY = pl.BlockSpec(memory_space=pl.ANY)
HBM = pl.BlockSpec(memory_space=pltpu.HBM)
F32 = jnp.float32
BF16 = jnp.bfloat16


def params(mib):
    return pltpu.CompilerParams(vmem_limit_bytes=mib * MIB)


def in_vmem(array):
    return pltpu.with_memory_space_constraint(array, pltpu.VMEM)


def in_hbm(array):
    return pltpu.with_memory_space_constraint(array, pltpu.HBM)


def cost(flops, moved):
    return pl.CostEstimate(flops=flops, bytes_accessed=moved, transcendentals=0)


def grid_of(devices):
    nx = 1
    while 4 * nx * nx < devices:
        nx *= 2
    if devices % nx:
        nx = 1
    return devices // nx, nx


def swap_z(devices, bits):
    nz, nx = grid_of(devices)
    return [(z * nx + x, (z ^ bits) * nx + x) for z in range(nz) for x in range(nx)]


def swap_x(devices, bits=0):
    nz, nx = grid_of(devices)
    return [(z * nx + x, (z ^ bits) * nx + (x ^ 1)) for z in range(nz) for x in range(nx)]


COST = cost(0, 1024)


def attend_kernel(
    kv, lengths, q_hbm, k_hbm, v_hbm, res_ref, up_hbm, out_ref, att_ref, scores_ref, probs_ref, q_ref, k_ref, v_ref, sems
):
    rows, heads, dim = q_ref.shape
    span = k_ref.shape[1]
    per_group = heads // kv
    loads = [
        pltpu.make_async_copy(source, held, sems.at[i])
        for i, (source, held) in enumerate(((q_hbm, q_ref), (k_hbm, k_ref), (v_hbm, v_ref)))
    ]
    for load in loads:
        load.start()
    column = lax.broadcasted_iota(jnp.int32, (heads, span), 1)
    head = lax.broadcasted_iota(jnp.int32, (heads, span), 0)
    right_group = (column % kv) == (head // per_group)
    position = column // kv

    def at(r):
        return slice(r * heads, (r + 1) * heads)

    loads[0].wait()
    loads[1].wait()
    for r in range(rows):
        scores = lax.dot_general(
            q_ref[r], k_ref[r], (((1,), (1,)), ((), ())), preferred_element_type=F32
        ) * (1.0 / math.sqrt(dim))
        scores_ref[at(r), :] = jnp.where(right_group & (position < lengths[r]), scores, -1e30)
    for r in range(rows):
        scores = scores_ref[at(r), :]
        raw = jnp.exp(scores - jnp.max(scores, axis=-1, keepdims=True))
        probs_ref[at(r), :] = (raw * (1.0 / jnp.sum(raw, axis=-1, keepdims=True))).astype(BF16)
    loads[2].wait()
    for r in range(rows):
        att_ref[at(r), :] = jnp.dot(probs_ref[at(r), :], v_ref[r], preferred_element_type=F32)
    for h in range(heads):
        lanes = slice(h * dim, (h + 1) * dim)
        mine = att_ref[pl.ds(h, rows, stride=heads), :]
        out_ref[:, lanes] = (res_ref[:, lanes].astype(F32) + mine).astype(BF16)


def attend(queries, cache_keys, stored_value_cache, lengths, residual, up):
    rows, heads, dim = queries.shape
    kv = cache_keys.shape[2]
    span = cache_keys.shape[1] * kv
    return pl.pallas_call(
        functools.partial(attend_kernel, kv),
        out_shape=jax.ShapeDtypeStruct((rows, heads * dim), BF16),
        in_specs=[SMEM, HBM, HBM, HBM, VMEM, HBM],
        out_specs=VMEM,
        scratch_shapes=[
            pltpu.VMEM((rows * heads, dim), F32),
            pltpu.VMEM((rows * heads, span), F32),
            pltpu.VMEM((rows * heads, span), BF16),
            pltpu.VMEM(queries.shape, BF16),
            pltpu.VMEM((rows, span, dim), BF16),
            pltpu.VMEM((rows, span, dim), BF16),
            pltpu.SemaphoreType.DMA((3,)),
        ],
        compiler_params=params(8),
        cost_estimate=cost(rows * heads * span * dim * 4, rows * span * dim * 4),
        name="attention",
    )(
        in_hbm(lengths),
        in_hbm(queries),
        in_hbm(cache_keys.reshape(rows, span, dim)),
        in_hbm(stored_value_cache.reshape(rows, span, dim)),
        in_hbm(residual),
        in_hbm(up),
    )


def row_copy(w_hbm, held_ref, sem, first):
    rows = pl.ds(pl.multiple_of(first, BAND), BAND)
    return pltpu.make_async_copy(w_hbm.at[rows], held_ref, sem)


def pack_kernel(*refs):
    *block_refs, out_ref = refs
    for i, ref in enumerate(block_refs):
        out_ref[i] = ref[...]


def pack(*blocks):
    return pl.pallas_call(
        pack_kernel,
        out_shape=jax.ShapeDtypeStruct((len(blocks),) + blocks[0].shape, BF16),
        in_specs=[VMEM] * len(blocks),
        out_specs=VMEM,
        compiler_params=params(4),
        name="pack",
    )(*blocks)


def tile_at(index):
    return pl.ds(pl.multiple_of(index * TILE, TILE), TILE)


def gate_up_kernel(
    devices,
    a_ref,
    c_ref,
    d_ref,
    e_ref,
    u_hbm,
    w_hbm,
    gate_ref,
    part_ref,
    rows_ref,
    far_ref,
    total_ref,
    buf,
    sems,
    far_sems,
):
    nx = grid_of(devices)[1]
    slots = buf.shape[0]
    left = u_hbm.shape[0] // BAND

    def streamed(j):
        slot = lax.rem(j, slots)
        return row_copy(u_hbm, buf.at[slot], sems.at[slot], j * BAND)

    for j in range(min(slots, left)):
        streamed(j).start()
    far_tiles = far_ref.shape[0] // TILE
    per_step = -(-far_tiles // left)
    far_base = half_base(devices, False, far_ref.shape[1])

    def far_copy(i):
        at = tile_at(i)
        return pltpu.make_async_copy(
            w_hbm.at[at, pl.ds(far_base, far_ref.shape[1])], far_ref.at[at], far_sems.at[i]
        )

    me = lax.axis_index(AXIS)
    my_z, my_x = me // nx, me % nx
    per = a_ref.shape[1]
    for bits, near, far in (
        (0, a_ref[0], a_ref[2]),
        (1, c_ref[0], c_ref[2]),
        (2, a_ref[1], d_ref[...]),
        (3, c_ref[1], e_ref[...]),
    ):
        here, there = near.astype(F32), far.astype(F32)
        pair = [jnp.where(my_x == 0, here, there), jnp.where(my_x == 0, there, here)]
        at = pl.ds(pl.multiple_of((my_z ^ bits) * (2 * per), 2 * per), 2 * per)
        rows_ref[at, :] = jnp.concatenate(pair, axis=0).astype(BF16)

    def add(at, weight, kind):
        total_ref[kind] += jnp.dot(rows_ref[:, at], weight, preferred_element_type=F32)

    total_ref[...] = jnp.zeros_like(total_ref)

    def step(j, _):
        at = pl.ds(pl.multiple_of(j * BAND, BAND), BAND)
        add(at, gate_ref[at, :], 0)
        streamed(j).wait()
        add(at, buf[lax.rem(j, slots)], 1)

        @pl.when(j + slots < left)
        def _():
            streamed(j + slots).start()

        for k in range(per_step):

            @pl.when(j * per_step + k < far_tiles)
            def _(k=k):
                far_copy(j * per_step + k).start()

        return 0

    lax.fori_loop(0, left, step, 0)
    part_ref[...] = total_ref[...].astype(BF16)
    for i in range(far_tiles):
        far_copy(i).wait()


def gate_up(blocks, gate_weight, up_weight, down_weight, devices, ahead):
    total = devices * blocks[0].shape[1]
    features, columns = gate_weight.shape
    slots = 4
    return pl.pallas_call(
        functools.partial(gate_up_kernel, devices),
        out_shape=(
            jax.ShapeDtypeStruct((2, total, columns), BF16),
            jax.ShapeDtypeStruct((total, features), BF16),
            pltpu.VMEM((ahead, features // 2), BF16),
        ),
        in_specs=[VMEM] * 4 + [HBM] * 2 + [VMEM],
        out_specs=(VMEM, VMEM, VMEM),
        scratch_shapes=[
            pltpu.VMEM((2, total, columns), F32),
            pltpu.VMEM((slots, BAND, columns), BF16),
            pltpu.SemaphoreType.DMA((slots,)),
            pltpu.SemaphoreType.DMA((ahead // TILE,)),
        ],
        compiler_params=params(GATE_MIB),
        cost_estimate=cost(4 * total * features * columns, 4 * features * columns),
        name="gate_up",
    )(
        *blocks,
        in_hbm(up_weight),
        in_hbm(down_weight),
        in_vmem(gate_weight),
    )


def down_copies(w_hbm, base, held_ref, sems, first):
    rows, wide = held_ref.shape
    return [
        pltpu.make_async_copy(
            w_hbm.at[pl.ds(first + i * TILE, TILE), pl.ds(base, wide)],
            held_ref.at[pl.ds(i * TILE, TILE)],
            sems.at[i],
        )
        for i in range(rows // TILE)
    ]


def half_base(devices, mine, half):
    my_x = lax.axis_index(AXIS) % grid_of(devices)[1]
    return pl.multiple_of((my_x if mine else 1 - my_x) * half, half)


def quarter_base(devices, far, quarter, wide):
    my_x = lax.axis_index(AXIS) % grid_of(devices)[1]
    half = 1 - my_x if far else my_x
    return pl.multiple_of((2 * half + quarter) * wide, wide)


def pick(row_ref, capacity, first_slot, slots):
    row = row_ref[...]
    total = row.shape[1]
    down = lax.broadcasted_iota(jnp.int32, (total, total), 0)
    across = lax.broadcasted_iota(jnp.int32, (total, total), 1)
    diagonal = jnp.where(down == across, row, 0).astype(F32).astype(BF16)
    column = jnp.dot(diagonal, jnp.ones((total, total), BF16), preferred_element_type=F32)
    earlier = (column == row.astype(F32)) & (down < across)
    rank = jnp.sum(earlier.astype(F32), axis=0, keepdims=True).astype(jnp.int32)
    slot = first_slot + lax.broadcasted_iota(jnp.int32, (slots, total), 0)
    return (slot == row * capacity + rank).astype(F32).astype(BF16)


def prepare_kernel(devices, capacity, first, after_ref, row_ref, w_hbm, far_ref, chosen_ref, sems):
    base = half_base(devices, False, far_ref.shape[1])
    copies = down_copies(w_hbm, base, far_ref, sems, first)
    for c in copies:
        c.start()
    nz, nx = grid_of(devices)
    my_z = lax.axis_index(AXIS) // nx
    slots = chosen_ref.shape[0] // nz
    for i, bits in enumerate(ORDER):
        chosen_ref[i * slots : (i + 1) * slots, :] = pick(
            row_ref, capacity, (my_z ^ bits) * slots, slots
        )
    for c in copies:
        c.wait()


def prepare(after, row, down_weight, devices, capacity, first):
    columns, features = down_weight.shape
    total = row.shape[1]
    rows = columns - first
    return pl.pallas_call(
        functools.partial(prepare_kernel, devices, capacity, first),
        out_shape=(
            pltpu.VMEM((rows, features // 2), BF16),
            jax.ShapeDtypeStruct((devices * 2 * capacity, total), BF16),
        ),
        in_specs=[ANY, VMEM, HBM],
        out_specs=(VMEM, VMEM),
        scratch_shapes=[pltpu.SemaphoreType.DMA((rows // TILE,))],
        compiler_params=params(2),
        cost_estimate=cost(0, rows * features),
        name="prepare",
    )(after, row, in_hbm(down_weight))


def down_kernel(devices, far, quarter, held_count, aheads, *refs):
    refs = list(refs)

    def take(count):
        return [refs.pop(0) for _ in range(count)]

    first_call = far and quarter == 0
    sources = take(2 if first_call else 1)
    arrived_ref, chosen_ref = (None, None) if far else take(2)
    held_refs = take(held_count)
    (w_hbm,) = take(1)
    out_refs = take(1 if far else 2)
    next_refs = take(len(aheads))
    (hidden_ref,) = take(1) if first_call else sources
    (total_ref,) = take(1)
    wide = total_ref.shape[1]
    ahead = []
    for (their, start, _), ref, sems in zip(aheads, next_refs, take(len(aheads))):
        ahead += down_copies(w_hbm, quarter_base(devices, False, their, wide), ref, sems, start)
    for c in ahead:
        c.start()
    if first_call:
        own_ref, other_ref = sources

        @pl.when(lax.axis_index(AXIS) >= 0)
        def _():
            gate = own_ref[0].astype(F32) + other_ref[0].astype(F32)
            up = own_ref[1].astype(F32) + other_ref[1].astype(F32)
            hidden_ref[...] = (gate / (1.0 + jnp.exp(-gate)) * up).astype(BF16)

    if far:
        total_ref[...] = jnp.zeros_like(total_ref)
    else:
        total_ref[...] = arrived_ref[...].astype(F32)
    @pl.when(lax.axis_index(AXIS) >= 0)
    def _():
        start = 0
        for held_ref in held_refs:
            stop = start + held_ref.shape[0]
            at = slice(quarter * wide, (quarter + 1) * wide) if far else slice(None)
            total_ref[...] += jnp.dot(
                hidden_ref[:, start:stop], held_ref[:, at], preferred_element_type=F32
            )
            start = stop

    rounded = total_ref[...].astype(BF16)
    if far:
        out_refs[0][...] = rounded
    else:
        slots = out_refs[0].shape[0]
        for i, ref in enumerate(out_refs):
            chosen = chosen_ref[i * slots : (i + 1) * slots]
            ref[...] = jnp.dot(chosen, rounded, preferred_element_type=F32).astype(BF16)
    for c in ahead:
        c.wait()


def down(sources, held, down_weight, devices, far, quarter, aheads=()):
    total = sources[0].shape[-2]
    columns, features = down_weight.shape
    wide = features // 4
    if far:
        out_shape = [jax.ShapeDtypeStruct((total, wide), BF16)]
    else:
        out_shape = [jax.ShapeDtypeStruct((sources[2].shape[0] // 2, wide), BF16)] * 2
    out_shape += [pltpu.VMEM((rows, wide), BF16) for _, _, rows in aheads]
    if far and quarter == 0:
        out_shape.append(jax.ShapeDtypeStruct((total, columns), BF16))
    return pl.pallas_call(
        functools.partial(down_kernel, devices, far, quarter, len(held), aheads),
        out_shape=tuple(out_shape),
        in_specs=[VMEM] * (len(sources) + len(held)) + [HBM],
        out_specs=tuple(VMEM for _ in out_shape),
        scratch_shapes=[pltpu.VMEM((total, wide), F32)]
        + [pltpu.SemaphoreType.DMA((rows // TILE,)) for _, _, rows in aheads],
        compiler_params=params(6),
        cost_estimate=COST,
        name="down_far" if far else "down_near",
    )(*sources, *(in_vmem(h) for h in held), in_hbm(down_weight))


def add_kernel(keep_ref, came_ref, own_ref, send_ref):
    slots = own_ref.shape[0]
    total = keep_ref[...].astype(F32) + came_ref[...].astype(F32)
    own_ref[...] = total[:slots]
    send_ref[...] = total[slots:].astype(BF16)


def add(keep, came):
    slots, wide = keep.shape
    return pl.pallas_call(
        add_kernel,
        out_shape=(
            jax.ShapeDtypeStruct((slots // 2, wide), F32),
            jax.ShapeDtypeStruct((slots // 2, wide), BF16),
        ),
        in_specs=[VMEM, VMEM],
        out_specs=(VMEM, VMEM),
        compiler_params=params(4),
        name="add",
    )(keep, came)


def finish_kernel(devices, chosen_ref, rows_ref, *refs):
    own_refs, came_refs, (keep_ref, send_ref) = refs[:2], refs[2:4], refs[4:]
    my_x = lax.axis_index(AXIS) % grid_of(devices)[1]
    slots, wide = own_refs[0].shape
    half = slots // 2
    for quarter, (own_ref, came_ref) in enumerate(zip(own_refs, came_refs)):
        mixed = rows_ref[:, pl.ds(quarter_base(devices, False, quarter, wide), wide)]
        done = jnp.dot(chosen_ref[:slots], mixed, preferred_element_type=F32)
        done = done + (own_ref[...] + came_ref[...].astype(F32))
        first, second = done[:half], done[half:]
        at = slice(quarter * wide, (quarter + 1) * wide)
        keep_ref[:, at] = jnp.where(my_x == 0, first, second).astype(BF16)
        send_ref[:, at] = jnp.where(my_x == 0, second, first).astype(BF16)


def finish(chosen, rows, own, came, devices):
    slots, wide = own[0].shape
    shape = jax.ShapeDtypeStruct((slots // 2, 2 * wide), BF16)
    return pl.pallas_call(
        functools.partial(finish_kernel, devices),
        out_shape=(shape, shape),
        in_specs=[VMEM] * 6,
        out_specs=(VMEM, VMEM),
        compiler_params=params(6),
        name="finish",
    )(chosen, rows, *own, *came)


def join_kernel(nx, keep_ref, other_ref, out_ref):
    my_x = lax.axis_index(AXIS) % nx
    width = keep_ref.shape[1]
    out_ref[:, :width] = jnp.where(my_x == 0, keep_ref[...], other_ref[...])
    out_ref[:, width:] = jnp.where(my_x == 0, other_ref[...], keep_ref[...])


def join(keep, other, devices):
    slots, width = keep.shape
    return pl.pallas_call(
        functools.partial(join_kernel, grid_of(devices)[1]),
        out_shape=jax.ShapeDtypeStruct((slots, 2 * width), BF16),
        in_specs=[VMEM, VMEM],
        out_specs=VMEM,
        compiler_params=params(8),
        name="join_halves",
    )(keep, other)


def slot_positions(column, destinations, capacity):
    onehot = (column[:, None] == jnp.arange(destinations, dtype=jnp.int32)[None, :]).astype(
        jnp.int32
    )
    before = jnp.cumsum(onehot, axis=0) - onehot
    slot_rank = jnp.sum(before * onehot, axis=1)
    return column * capacity + slot_rank


def plain(mixed_rows, target, gate_weight, up_weight, down_weight, devices):
    rows_dev, features = mixed_rows.shape
    me = lax.axis_index(AXIS)
    gathered = lax.all_gather(mixed_rows, AXIS, axis=0, tiled=True)
    mine = jnp.stack(
        [
            jnp.dot(gathered, gate_weight, preferred_element_type=F32),
            jnp.dot(gathered, up_weight, preferred_element_type=F32),
        ]
    )
    other = lax.ppermute(mine.astype(BF16), "ffn", [(0, 1), (1, 0)])
    gate_sum, up_sum = mine + other.astype(F32)
    hidden = (jax.nn.silu(gate_sum) * up_sum).astype(BF16)
    down = jnp.dot(hidden, down_weight, preferred_element_type=F32)
    share = features // devices
    landed = lax.all_to_all(
        jnp.moveaxis(down.astype(BF16).reshape(-1, devices, share), 1, 0), AXIS, 0, 0
    )
    summed = jnp.sum(landed.astype(F32), axis=0)
    mixed_share = lax.dynamic_slice_in_dim(gathered, me * share, share, axis=1)
    finished = (mixed_share.astype(F32) + summed).astype(BF16)
    slot_count = 2 * devices * rows_dev
    position = slot_positions(target[:, 0], 2 * devices, rows_dev)
    chosen = (jnp.arange(slot_count, dtype=jnp.int32)[:, None] == position[None, :]).astype(BF16)
    slots = jnp.dot(chosen, finished, preferred_element_type=F32).astype(BF16)
    slots = slots.reshape(devices, 2 * rows_dev, share)
    mine_out = lax.all_to_all(slots, AXIS, split_axis=0, concat_axis=0)
    return jnp.moveaxis(mine_out, 0, 1).reshape(2 * rows_dev, features)


def local(
    queries,
    cache_keys,
    stored_value_cache,
    lengths,
    residual,
    target,
    gate_weight,
    up_weight,
    down_weight,
):
    devices = lax.axis_size(AXIS)
    nz, nx = grid_of(devices)
    capacity = cache_keys.shape[0]
    columns, features = down_weight.shape
    fits = nz == 4 and nx == 2 and columns % TILE == 0 and features == 16 * BAND
    mixed_rows = attend(queries, cache_keys, stored_value_cache, lengths, residual, up_weight)
    if not fits:
        return plain(mixed_rows, target, gate_weight, up_weight, down_weight, devices)

    two = lax.ppermute(mixed_rows, AXIS, swap_z(devices, 2))
    side = lax.ppermute(mixed_rows, AXIS, swap_x(devices))
    e = lax.ppermute(mixed_rows, AXIS, swap_x(devices, 3))
    a = pack(mixed_rows, two, side)
    c = lax.ppermute(a, AXIS, swap_z(devices, 1))
    d = lax.ppermute(two, AXIS, swap_x(devices))
    tiles = columns // TILE
    far_cut = 8 * tiles // 13 * TILE
    cut = 8 * tiles // 13 * TILE, 7 * tiles // 13 * TILE
    part, rows, far_a = gate_up(
        (a, c, d, e), gate_weight, up_weight, down_weight, devices, far_cut
    )
    other = lax.ppermute(part, "ffn", [(0, 1), (1, 0)])
    far_b, chosen = prepare(
        part, target.reshape(1, -1), down_weight, devices, capacity, far_cut
    )
    held_far = far_a, far_b

    far, near_a, hidden = down(
        (part, other), held_far, down_weight, devices, True, 0, ((0, 0, cut[0]),)
    )
    arrived = [lax.ppermute(far, AXIS, swap_x(devices))]
    far, near_b, near_c = down(
        (hidden,),
        held_far,
        down_weight,
        devices,
        True,
        1,
        ((0, cut[0], columns - cut[0]), (1, 0, cut[1])),
    )
    arrived.append(lax.ppermute(far, AXIS, swap_x(devices)))
    keep_a, send_a, near_d = down(
        (hidden, arrived[0], chosen),
        (near_a, near_b),
        down_weight,
        devices,
        False,
        0,
        ((1, cut[1], columns - cut[1]),),
    )
    came_a = lax.ppermute(send_a, AXIS, swap_z(devices, 1))
    keep_b, send_b = down(
        (hidden, arrived[1], chosen), (near_c, near_d), down_weight, devices, False, 1
    )
    came_b = lax.ppermute(send_b, AXIS, swap_z(devices, 1))
    own, came = [], []
    for keep, arrived in ((keep_a, came_a), (keep_b, came_b)):
        mine, send = add(keep, arrived)
        own.append(mine)
        came.append(lax.ppermute(send, AXIS, swap_z(devices, 2)))
    keep, send = finish(chosen, rows, own, came, devices)
    return join(keep, lax.ppermute(send, AXIS, swap_x(devices)), devices)


def solution(mesh):
    return jax.shard_map(
        local,
        mesh=mesh,
        in_specs=(
            P(("parts", "attn"), "ffn", None),
            P(("parts", "attn"), None, "ffn", None),
            P(("parts", "attn"), None, "ffn", None),
            P(("parts", "attn")),
            P(("parts", "attn"), "ffn"),
            P("parts", None),
            P("ffn", "attn"),
            P("ffn", "attn"),
            P("attn", "ffn"),
        ),
        out_specs=P(("parts", "attn"), "ffn"),
        check_vma=False,
    )
```

```python
import functools
import math

import jax
import jax.numpy as jnp
from jax import lax
from jax.experimental import pallas as pl
from jax.experimental.pallas import tpu as pltpu
from jax.sharding import PartitionSpec as P

AXIS = "attn"
TILE = 256
BAND = 512
GATE_MIB = 14
ORDER = (0, 2, 1, 3)
MIB = 1 << 20
VMEM = pl.BlockSpec(memory_space=pltpu.VMEM)
SMEM = pl.BlockSpec(memory_space=pltpu.SMEM)
ANY = pl.BlockSpec(memory_space=pl.ANY)
HBM = pl.BlockSpec(memory_space=pltpu.HBM)
F32 = jnp.float32
BF16 = jnp.bfloat16


def params(mib):
    return pltpu.CompilerParams(vmem_limit_bytes=mib * MIB)


def in_vmem(array):
    return pltpu.with_memory_space_constraint(array, pltpu.VMEM)


def in_hbm(array):
    return pltpu.with_memory_space_constraint(array, pltpu.HBM)


def cost(flops, moved):
    return pl.CostEstimate(flops=flops, bytes_accessed=moved, transcendentals=0)


def grid_of(devices):
    nx = 1
    while 4 * nx * nx < devices:
        nx *= 2
    if devices % nx:
        nx = 1
    return devices // nx, nx


def swap_z(devices, bits):
    nz, nx = grid_of(devices)
    return [(z * nx + x, (z ^ bits) * nx + x) for z in range(nz) for x in range(nx)]


def swap_x(devices, bits=0):
    nz, nx = grid_of(devices)
    return [(z * nx + x, (z ^ bits) * nx + (x ^ 1)) for z in range(nz) for x in range(nx)]


COST = cost(0, 1024)


def attend_kernel(
    kv, lengths, q_hbm, k_hbm, v_hbm, res_ref, up_hbm, out_ref, att_ref, scores_ref, probs_ref, q_ref, k_ref, v_ref, sems
):
    rows, heads, dim = q_ref.shape
    span = k_ref.shape[1]
    per_group = heads // kv
    loads = [
        pltpu.make_async_copy(source, held, sems.at[i])
        for i, (source, held) in enumerate(((q_hbm, q_ref), (k_hbm, k_ref), (v_hbm, v_ref)))
    ]
    for load in loads:
        load.start()
    column = lax.broadcasted_iota(jnp.int32, (heads, span), 1)
    head = lax.broadcasted_iota(jnp.int32, (heads, span), 0)
    right_group = (column % kv) == (head // per_group)
    position = column // kv

    def at(r):
        return slice(r * heads, (r + 1) * heads)

    loads[0].wait()
    loads[1].wait()
    for r in range(rows):
        scores = lax.dot_general(
            q_ref[r], k_ref[r], (((1,), (1,)), ((), ())), preferred_element_type=F32
        ) * (1.0 / math.sqrt(dim))
        scores_ref[at(r), :] = jnp.where(right_group & (position < lengths[r]), scores, -1e30)
    for r in range(rows):
        scores = scores_ref[at(r), :]
        raw = jnp.exp(scores - jnp.max(scores, axis=-1, keepdims=True))
        probs_ref[at(r), :] = (raw * (1.0 / jnp.sum(raw, axis=-1, keepdims=True))).astype(BF16)
    loads[2].wait()
    for r in range(rows):
        att_ref[at(r), :] = jnp.dot(probs_ref[at(r), :], v_ref[r], preferred_element_type=F32)
    for h in range(heads):
        lanes = slice(h * dim, (h + 1) * dim)
        mine = att_ref[pl.ds(h, rows, stride=heads), :]
        out_ref[:, lanes] = (res_ref[:, lanes].astype(F32) + mine).astype(BF16)


def attend(queries, cache_keys, stored_value_cache, lengths, residual, up):
    rows, heads, dim = queries.shape
    kv = cache_keys.shape[2]
    span = cache_keys.shape[1] * kv
    return pl.pallas_call(
        functools.partial(attend_kernel, kv),
        out_shape=jax.ShapeDtypeStruct((rows, heads * dim), BF16),
        in_specs=[SMEM, HBM, HBM, HBM, VMEM, HBM],
        out_specs=VMEM,
        scratch_shapes=[
            pltpu.VMEM((rows * heads, dim), F32),
            pltpu.VMEM((rows * heads, span), F32),
            pltpu.VMEM((rows * heads, span), BF16),
            pltpu.VMEM(queries.shape, BF16),
            pltpu.VMEM((rows, span, dim), BF16),
            pltpu.VMEM((rows, span, dim), BF16),
            pltpu.SemaphoreType.DMA((3,)),
        ],
        compiler_params=params(8),
        cost_estimate=cost(rows * heads * span * dim * 4, rows * span * dim * 4),
        name="attention",
    )(
        in_hbm(lengths),
        in_hbm(queries),
        in_hbm(cache_keys.reshape(rows, span, dim)),
        in_hbm(stored_value_cache.reshape(rows, span, dim)),
        in_hbm(residual),
        in_hbm(up),
    )


def row_copy(w_hbm, held_ref, sem, first):
    rows = pl.ds(pl.multiple_of(first, BAND), BAND)
    return pltpu.make_async_copy(w_hbm.at[rows], held_ref, sem)


def pack_kernel(*refs):
    *block_refs, out_ref = refs
    for i, ref in enumerate(block_refs):
        out_ref[i] = ref[...]


def pack(*blocks):
    return pl.pallas_call(
        pack_kernel,
        out_shape=jax.ShapeDtypeStruct((len(blocks),) + blocks[0].shape, BF16),
        in_specs=[VMEM] * len(blocks),
        out_specs=VMEM,
        compiler_params=params(4),
        name="pack",
    )(*blocks)


def tile_at(index):
    return pl.ds(pl.multiple_of(index * TILE, TILE), TILE)


def gate_up_kernel(
    devices,
    a_ref,
    c_ref,
    d_ref,
    e_ref,
    u_hbm,
    w_hbm,
    gate_ref,
    part_ref,
    rows_ref,
    far_ref,
    total_ref,
    buf,
    sems,
    far_sems,
):
    nx = grid_of(devices)[1]
    slots = buf.shape[0]
    left = u_hbm.shape[0] // BAND

    def streamed(j):
        slot = lax.rem(j, slots)
        return row_copy(u_hbm, buf.at[slot], sems.at[slot], j * BAND)

    for j in range(min(slots, left)):
        streamed(j).start()
    far_tiles = far_ref.shape[0] // TILE
    per_step = -(-far_tiles // (left - 1))
    far_base = half_base(devices, False, far_ref.shape[1])

    def far_copy(i):
        at = tile_at(i)
        return pltpu.make_async_copy(
            w_hbm.at[at, pl.ds(far_base, far_ref.shape[1])], far_ref.at[at], far_sems.at[i]
        )

    me = lax.axis_index(AXIS)
    my_z, my_x = me // nx, me % nx
    per = a_ref.shape[1]
    for bits, near, far in (
        (0, a_ref[0], a_ref[2]),
        (1, c_ref[0], c_ref[2]),
        (2, a_ref[1], d_ref[...]),
        (3, c_ref[1], e_ref[...]),
    ):
        here, there = near.astype(F32), far.astype(F32)
        pair = [jnp.where(my_x == 0, here, there), jnp.where(my_x == 0, there, here)]
        at = pl.ds(pl.multiple_of((my_z ^ bits) * (2 * per), 2 * per), 2 * per)
        rows_ref[at, :] = jnp.concatenate(pair, axis=0).astype(BF16)

    def add(at, weight, kind):
        total_ref[kind] += jnp.dot(rows_ref[:, at], weight, preferred_element_type=F32)

    total_ref[...] = jnp.zeros_like(total_ref)

    def band(j):
        return pl.ds(pl.multiple_of(j * BAND, BAND), BAND)

    @pl.when(me >= 0)
    def _():
        add(band(0), gate_ref[band(0), :], 0)

    def step(j, _):
        streamed(j).wait()
        add(band(j), buf[lax.rem(j, slots)], 1)
        add(band(j + 1), gate_ref[band(j + 1), :], 0)

        @pl.when(j + slots < left)
        def _():
            streamed(j + slots).start()

        for k in range(per_step):

            @pl.when(j * per_step + k < far_tiles)
            def _(k=k):
                far_copy(j * per_step + k).start()

        return 0

    lax.fori_loop(0, left - 1, step, 0)
    streamed(left - 1).wait()
    add(band(left - 1), buf[(left - 1) % slots], 1)
    part_ref[...] = total_ref[...].astype(BF16)
    for i in range(far_tiles):
        far_copy(i).wait()


def gate_up(blocks, gate_weight, up_weight, down_weight, devices, ahead):
    total = devices * blocks[0].shape[1]
    features, columns = gate_weight.shape
    slots = 3
    return pl.pallas_call(
        functools.partial(gate_up_kernel, devices),
        out_shape=(
            jax.ShapeDtypeStruct((2, total, columns), BF16),
            jax.ShapeDtypeStruct((total, features), BF16),
            pltpu.VMEM((ahead, features // 2), BF16),
        ),
        in_specs=[VMEM] * 4 + [HBM] * 2 + [VMEM],
        out_specs=(VMEM, VMEM, VMEM),
        scratch_shapes=[
            pltpu.VMEM((2, total, columns), F32),
            pltpu.VMEM((slots, BAND, columns), BF16),
            pltpu.SemaphoreType.DMA((slots,)),
            pltpu.SemaphoreType.DMA((ahead // TILE,)),
        ],
        compiler_params=params(GATE_MIB),
        cost_estimate=cost(4 * total * features * columns, 4 * features * columns),
        name="gate_up",
    )(
        *blocks,
        in_hbm(up_weight),
        in_hbm(down_weight),
        in_vmem(gate_weight),
    )


def down_copies(w_hbm, base, held_ref, sems, first):
    rows, wide = held_ref.shape
    return [
        pltpu.make_async_copy(
            w_hbm.at[pl.ds(first + i * TILE, TILE), pl.ds(base, wide)],
            held_ref.at[pl.ds(i * TILE, TILE)],
            sems.at[i],
        )
        for i in range(rows // TILE)
    ]


def half_base(devices, mine, half):
    my_x = lax.axis_index(AXIS) % grid_of(devices)[1]
    return pl.multiple_of((my_x if mine else 1 - my_x) * half, half)


def quarter_base(devices, far, quarter, wide):
    my_x = lax.axis_index(AXIS) % grid_of(devices)[1]
    half = 1 - my_x if far else my_x
    return pl.multiple_of((2 * half + quarter) * wide, wide)


def pick(row_ref, capacity, first_slot, slots):
    row = row_ref[...]
    total = row.shape[1]
    down = lax.broadcasted_iota(jnp.int32, (total, total), 0)
    across = lax.broadcasted_iota(jnp.int32, (total, total), 1)
    diagonal = jnp.where(down == across, row, 0).astype(F32).astype(BF16)
    column = jnp.dot(diagonal, jnp.ones((total, total), BF16), preferred_element_type=F32)
    earlier = (column == row.astype(F32)) & (down < across)
    rank = jnp.sum(earlier.astype(F32), axis=0, keepdims=True).astype(jnp.int32)
    slot = first_slot + lax.broadcasted_iota(jnp.int32, (slots, total), 0)
    return (slot == row * capacity + rank).astype(F32).astype(BF16)


def prepare_kernel(devices, capacity, first, after_ref, row_ref, w_hbm, far_ref, chosen_ref, sems):
    base = half_base(devices, False, far_ref.shape[1])
    copies = down_copies(w_hbm, base, far_ref, sems, first)
    for c in copies:
        c.start()
    nz, nx = grid_of(devices)
    my_z = lax.axis_index(AXIS) // nx
    slots = chosen_ref.shape[0] // nz
    for i, bits in enumerate(ORDER):
        chosen_ref[i * slots : (i + 1) * slots, :] = pick(
            row_ref, capacity, (my_z ^ bits) * slots, slots
        )
    for c in copies:
        c.wait()


def prepare(after, row, down_weight, devices, capacity, first):
    columns, features = down_weight.shape
    total = row.shape[1]
    rows = columns - first
    return pl.pallas_call(
        functools.partial(prepare_kernel, devices, capacity, first),
        out_shape=(
            pltpu.VMEM((rows, features // 2), BF16),
            jax.ShapeDtypeStruct((devices * 2 * capacity, total), BF16),
        ),
        in_specs=[ANY, VMEM, HBM],
        out_specs=(VMEM, VMEM),
        scratch_shapes=[pltpu.SemaphoreType.DMA((rows // TILE,))],
        compiler_params=params(2),
        cost_estimate=cost(0, rows * features),
        name="prepare",
    )(after, row, in_hbm(down_weight))


def down_kernel(devices, far, quarter, held_count, aheads, *refs):
    refs = list(refs)

    def take(count):
        return [refs.pop(0) for _ in range(count)]

    first_call = far and quarter == 0
    sources = take(2 if first_call else 1)
    arrived_ref, chosen_ref = (None, None) if far else take(2)
    held_refs = take(held_count)
    (w_hbm,) = take(1)
    out_refs = take(1 if far else 2)
    next_refs = take(len(aheads))
    (hidden_ref,) = take(1) if first_call else sources
    (total_ref,) = take(1)
    wide = total_ref.shape[1]
    ahead = []
    for (their, start, _), ref, sems in zip(aheads, next_refs, take(len(aheads))):
        ahead += down_copies(w_hbm, quarter_base(devices, False, their, wide), ref, sems, start)
    for c in ahead:
        c.start()
    if first_call:
        own_ref, other_ref = sources

        @pl.when(lax.axis_index(AXIS) >= 0)
        def _():
            gate = own_ref[0].astype(F32) + other_ref[0].astype(F32)
            up = own_ref[1].astype(F32) + other_ref[1].astype(F32)
            hidden_ref[...] = (gate / (1.0 + jnp.exp(-gate)) * up).astype(BF16)

    if far:
        total_ref[...] = jnp.zeros_like(total_ref)
    else:
        total_ref[...] = arrived_ref[...].astype(F32)
    @pl.when(lax.axis_index(AXIS) >= 0)
    def _():
        start = 0
        for held_ref in held_refs:
            stop = start + held_ref.shape[0]
            at = slice(quarter * wide, (quarter + 1) * wide) if far else slice(None)
            total_ref[...] += jnp.dot(
                hidden_ref[:, start:stop], held_ref[:, at], preferred_element_type=F32
            )
            start = stop

    rounded = total_ref[...].astype(BF16)
    if far:
        out_refs[0][...] = rounded
    else:
        slots = out_refs[0].shape[0]
        for i, ref in enumerate(out_refs):
            chosen = chosen_ref[i * slots : (i + 1) * slots]
            ref[...] = jnp.dot(chosen, rounded, preferred_element_type=F32).astype(BF16)
    for c in ahead:
        c.wait()


def down(sources, held, down_weight, devices, far, quarter, aheads=()):
    total = sources[0].shape[-2]
    columns, features = down_weight.shape
    wide = features // 4
    if far:
        out_shape = [jax.ShapeDtypeStruct((total, wide), BF16)]
    else:
        out_shape = [jax.ShapeDtypeStruct((sources[2].shape[0] // 2, wide), BF16)] * 2
    out_shape += [pltpu.VMEM((rows, wide), BF16) for _, _, rows in aheads]
    if far and quarter == 0:
        out_shape.append(jax.ShapeDtypeStruct((total, columns), BF16))
    return pl.pallas_call(
        functools.partial(down_kernel, devices, far, quarter, len(held), aheads),
        out_shape=tuple(out_shape),
        in_specs=[VMEM] * (len(sources) + len(held)) + [HBM],
        out_specs=tuple(VMEM for _ in out_shape),
        scratch_shapes=[pltpu.VMEM((total, wide), F32)]
        + [pltpu.SemaphoreType.DMA((rows // TILE,)) for _, _, rows in aheads],
        compiler_params=params(6),
        cost_estimate=COST,
        name="down_far" if far else "down_near",
    )(*sources, *(in_vmem(h) for h in held), in_hbm(down_weight))


def add_kernel(keep_ref, came_ref, own_ref, send_ref):
    slots = own_ref.shape[0]
    total = keep_ref[...].astype(F32) + came_ref[...].astype(F32)
    own_ref[...] = total[:slots]
    send_ref[...] = total[slots:].astype(BF16)


def add(keep, came):
    slots, wide = keep.shape
    return pl.pallas_call(
        add_kernel,
        out_shape=(
            jax.ShapeDtypeStruct((slots // 2, wide), F32),
            jax.ShapeDtypeStruct((slots // 2, wide), BF16),
        ),
        in_specs=[VMEM, VMEM],
        out_specs=(VMEM, VMEM),
        compiler_params=params(4),
        name="add",
    )(keep, came)


def finish_kernel(devices, chosen_ref, rows_ref, *refs):
    own_refs, came_refs, (keep_ref, send_ref) = refs[:2], refs[2:4], refs[4:]
    my_x = lax.axis_index(AXIS) % grid_of(devices)[1]
    slots, wide = own_refs[0].shape
    half = slots // 2
    for quarter, (own_ref, came_ref) in enumerate(zip(own_refs, came_refs)):
        mixed = rows_ref[:, pl.ds(quarter_base(devices, False, quarter, wide), wide)]
        done = jnp.dot(chosen_ref[:slots], mixed, preferred_element_type=F32)
        done = done + (own_ref[...] + came_ref[...].astype(F32))
        first, second = done[:half], done[half:]
        at = slice(quarter * wide, (quarter + 1) * wide)
        keep_ref[:, at] = jnp.where(my_x == 0, first, second).astype(BF16)
        send_ref[:, at] = jnp.where(my_x == 0, second, first).astype(BF16)


def finish(chosen, rows, own, came, devices):
    slots, wide = own[0].shape
    shape = jax.ShapeDtypeStruct((slots // 2, 2 * wide), BF16)
    return pl.pallas_call(
        functools.partial(finish_kernel, devices),
        out_shape=(shape, shape),
        in_specs=[VMEM] * 6,
        out_specs=(VMEM, VMEM),
        compiler_params=params(6),
        name="finish",
    )(chosen, rows, *own, *came)


def join_kernel(nx, keep_ref, other_ref, out_ref):
    my_x = lax.axis_index(AXIS) % nx
    width = keep_ref.shape[1]
    out_ref[:, :width] = jnp.where(my_x == 0, keep_ref[...], other_ref[...])
    out_ref[:, width:] = jnp.where(my_x == 0, other_ref[...], keep_ref[...])


def join(keep, other, devices):
    slots, width = keep.shape
    return pl.pallas_call(
        functools.partial(join_kernel, grid_of(devices)[1]),
        out_shape=jax.ShapeDtypeStruct((slots, 2 * width), BF16),
        in_specs=[VMEM, VMEM],
        out_specs=VMEM,
        compiler_params=params(8),
        name="join_halves",
    )(keep, other)


def slot_positions(column, destinations, capacity):
    onehot = (column[:, None] == jnp.arange(destinations, dtype=jnp.int32)[None, :]).astype(
        jnp.int32
    )
    before = jnp.cumsum(onehot, axis=0) - onehot
    slot_rank = jnp.sum(before * onehot, axis=1)
    return column * capacity + slot_rank


def plain(mixed_rows, target, gate_weight, up_weight, down_weight, devices):
    rows_dev, features = mixed_rows.shape
    me = lax.axis_index(AXIS)
    gathered = lax.all_gather(mixed_rows, AXIS, axis=0, tiled=True)
    mine = jnp.stack(
        [
            jnp.dot(gathered, gate_weight, preferred_element_type=F32),
            jnp.dot(gathered, up_weight, preferred_element_type=F32),
        ]
    )
    other = lax.ppermute(mine.astype(BF16), "ffn", [(0, 1), (1, 0)])
    gate_sum, up_sum = mine + other.astype(F32)
    hidden = (jax.nn.silu(gate_sum) * up_sum).astype(BF16)
    down = jnp.dot(hidden, down_weight, preferred_element_type=F32)
    share = features // devices
    landed = lax.all_to_all(
        jnp.moveaxis(down.astype(BF16).reshape(-1, devices, share), 1, 0), AXIS, 0, 0
    )
    summed = jnp.sum(landed.astype(F32), axis=0)
    mixed_share = lax.dynamic_slice_in_dim(gathered, me * share, share, axis=1)
    finished = (mixed_share.astype(F32) + summed).astype(BF16)
    slot_count = 2 * devices * rows_dev
    position = slot_positions(target[:, 0], 2 * devices, rows_dev)
    chosen = (jnp.arange(slot_count, dtype=jnp.int32)[:, None] == position[None, :]).astype(BF16)
    slots = jnp.dot(chosen, finished, preferred_element_type=F32).astype(BF16)
    slots = slots.reshape(devices, 2 * rows_dev, share)
    mine_out = lax.all_to_all(slots, AXIS, split_axis=0, concat_axis=0)
    return jnp.moveaxis(mine_out, 0, 1).reshape(2 * rows_dev, features)


def local(
    queries,
    cache_keys,
    stored_value_cache,
    lengths,
    residual,
    target,
    gate_weight,
    up_weight,
    down_weight,
):
    devices = lax.axis_size(AXIS)
    nz, nx = grid_of(devices)
    capacity = cache_keys.shape[0]
    columns, features = down_weight.shape
    fits = nz == 4 and nx == 2 and columns % TILE == 0 and features % (8 * BAND) == 0
    mixed_rows = attend(queries, cache_keys, stored_value_cache, lengths, residual, up_weight)
    if not fits:
        return plain(mixed_rows, target, gate_weight, up_weight, down_weight, devices)

    two = lax.ppermute(mixed_rows, AXIS, swap_z(devices, 2))
    side = lax.ppermute(mixed_rows, AXIS, swap_x(devices))
    e = lax.ppermute(mixed_rows, AXIS, swap_x(devices, 3))
    a = pack(mixed_rows, two, side)
    c = lax.ppermute(a, AXIS, swap_z(devices, 1))
    d = lax.ppermute(two, AXIS, swap_x(devices))
    tiles = columns // TILE
    far_cut = 8 * tiles // 13 * TILE
    cut = 8 * tiles // 13 * TILE, 7 * tiles // 13 * TILE
    part, rows, far_a = gate_up(
        (a, c, d, e), gate_weight, up_weight, down_weight, devices, far_cut
    )
    other = lax.ppermute(part, "ffn", [(0, 1), (1, 0)])
    far_b, chosen = prepare(
        part, target.reshape(1, -1), down_weight, devices, capacity, far_cut
    )
    held_far = far_a, far_b

    far, near_a, hidden = down(
        (part, other), held_far, down_weight, devices, True, 0, ((0, 0, cut[0]),)
    )
    arrived = [lax.ppermute(far, AXIS, swap_x(devices))]
    far, near_b, near_c = down(
        (hidden,),
        held_far,
        down_weight,
        devices,
        True,
        1,
        ((0, cut[0], columns - cut[0]), (1, 0, cut[1])),
    )
    arrived.append(lax.ppermute(far, AXIS, swap_x(devices)))
    keep_a, send_a, near_d = down(
        (hidden, arrived[0], chosen),
        (near_a, near_b),
        down_weight,
        devices,
        False,
        0,
        ((1, cut[1], columns - cut[1]),),
    )
    came_a = lax.ppermute(send_a, AXIS, swap_z(devices, 1))
    keep_b, send_b = down(
        (hidden, arrived[1], chosen), (near_c, near_d), down_weight, devices, False, 1
    )
    came_b = lax.ppermute(send_b, AXIS, swap_z(devices, 1))
    own, came = [], []
    for keep, arrived in ((keep_a, came_a), (keep_b, came_b)):
        mine, send = add(keep, arrived)
        own.append(mine)
        came.append(lax.ppermute(send, AXIS, swap_z(devices, 2)))
    keep, send = finish(chosen, rows, own, came, devices)
    return join(keep, lax.ppermute(send, AXIS, swap_x(devices)), devices)


def solution(mesh):
    return jax.shard_map(
        local,
        mesh=mesh,
        in_specs=(
            P(("parts", "attn"), "ffn", None),
            P(("parts", "attn"), None, "ffn", None),
            P(("parts", "attn"), None, "ffn", None),
            P(("parts", "attn")),
            P(("parts", "attn"), "ffn"),
            P("parts", None),
            P("ffn", "attn"),
            P("ffn", "attn"),
            P("attn", "ffn"),
        ),
        out_specs=P(("parts", "attn"), "ffn"),
        check_vma=False,
    )
```

```python
import functools
import math

import jax
import jax.numpy as jnp
from jax import lax
from jax.experimental import pallas as pl
from jax.experimental.pallas import tpu as pltpu
from jax.sharding import PartitionSpec as P

AXIS = "attn"
TILE = 256
BAND = 512
GATE_MIB = 14
ORDER = (0, 2, 1, 3)
MIB = 1 << 20
VMEM = pl.BlockSpec(memory_space=pltpu.VMEM)
SMEM = pl.BlockSpec(memory_space=pltpu.SMEM)
ANY = pl.BlockSpec(memory_space=pl.ANY)
HBM = pl.BlockSpec(memory_space=pltpu.HBM)
F32 = jnp.float32
BF16 = jnp.bfloat16


def params(mib):
    return pltpu.CompilerParams(vmem_limit_bytes=mib * MIB)


def in_vmem(array):
    return pltpu.with_memory_space_constraint(array, pltpu.VMEM)


def in_hbm(array):
    return pltpu.with_memory_space_constraint(array, pltpu.HBM)


def cost(flops, moved):
    return pl.CostEstimate(flops=flops, bytes_accessed=moved, transcendentals=0)


def grid_of(devices):
    nx = 1
    while 4 * nx * nx < devices:
        nx *= 2
    if devices % nx:
        nx = 1
    return devices // nx, nx


def swap_z(devices, bits):
    nz, nx = grid_of(devices)
    return [(z * nx + x, (z ^ bits) * nx + x) for z in range(nz) for x in range(nx)]


def swap_x(devices, bits=0):
    nz, nx = grid_of(devices)
    return [(z * nx + x, (z ^ bits) * nx + (x ^ 1)) for z in range(nz) for x in range(nx)]


COST = cost(0, 1024)


def attend_kernel(
    kv, lengths, q_hbm, k_hbm, v_hbm, res_ref, up_hbm, out_ref, att_ref, scores_ref, probs_ref, q_ref, k_ref, v_ref, sems
):
    rows, heads, dim = q_ref.shape
    span = k_ref.shape[1]
    per_group = heads // kv
    loads = [
        pltpu.make_async_copy(source, held, sems.at[i])
        for i, (source, held) in enumerate(((q_hbm, q_ref), (k_hbm, k_ref), (v_hbm, v_ref)))
    ]
    for load in loads:
        load.start()
    column = lax.broadcasted_iota(jnp.int32, (heads, span), 1)
    head = lax.broadcasted_iota(jnp.int32, (heads, span), 0)
    right_group = (column % kv) == (head // per_group)
    position = column // kv

    def at(r):
        return slice(r * heads, (r + 1) * heads)

    loads[0].wait()
    loads[1].wait()
    for r in range(rows):
        scores = lax.dot_general(
            q_ref[r], k_ref[r], (((1,), (1,)), ((), ())), preferred_element_type=F32
        ) * (1.0 / math.sqrt(dim))
        scores_ref[at(r), :] = jnp.where(right_group & (position < lengths[r]), scores, -1e30)
    for r in range(rows):
        scores = scores_ref[at(r), :]
        raw = jnp.exp(scores - jnp.max(scores, axis=-1, keepdims=True))
        probs_ref[at(r), :] = (raw * (1.0 / jnp.sum(raw, axis=-1, keepdims=True))).astype(BF16)
    loads[2].wait()
    for r in range(rows):
        att_ref[at(r), :] = jnp.dot(probs_ref[at(r), :], v_ref[r], preferred_element_type=F32)
    for h in range(heads):
        lanes = slice(h * dim, (h + 1) * dim)
        mine = att_ref[pl.ds(h, rows, stride=heads), :]
        out_ref[:, lanes] = (res_ref[:, lanes].astype(F32) + mine).astype(BF16)


def attend(queries, cache_keys, stored_value_cache, lengths, residual, up):
    rows, heads, dim = queries.shape
    kv = cache_keys.shape[2]
    span = cache_keys.shape[1] * kv
    return pl.pallas_call(
        functools.partial(attend_kernel, kv),
        out_shape=jax.ShapeDtypeStruct((rows, heads * dim), BF16),
        in_specs=[SMEM, HBM, HBM, HBM, VMEM, HBM],
        out_specs=VMEM,
        scratch_shapes=[
            pltpu.VMEM((rows * heads, dim), F32),
            pltpu.VMEM((rows * heads, span), F32),
            pltpu.VMEM((rows * heads, span), BF16),
            pltpu.VMEM(queries.shape, BF16),
            pltpu.VMEM((rows, span, dim), BF16),
            pltpu.VMEM((rows, span, dim), BF16),
            pltpu.SemaphoreType.DMA((3,)),
        ],
        compiler_params=params(8),
        cost_estimate=cost(rows * heads * span * dim * 4, rows * span * dim * 4),
        name="attention",
    )(
        in_hbm(lengths),
        in_hbm(queries),
        in_hbm(cache_keys.reshape(rows, span, dim)),
        in_hbm(stored_value_cache.reshape(rows, span, dim)),
        in_hbm(residual),
        in_hbm(up),
    )


def row_copy(w_hbm, held_ref, sem, first):
    rows = pl.ds(pl.multiple_of(first, BAND), BAND)
    return pltpu.make_async_copy(w_hbm.at[rows], held_ref, sem)


def pack_kernel(*refs):
    *block_refs, out_ref = refs
    for i, ref in enumerate(block_refs):
        out_ref[i] = ref[...]


def pack(*blocks):
    return pl.pallas_call(
        pack_kernel,
        out_shape=jax.ShapeDtypeStruct((len(blocks),) + blocks[0].shape, BF16),
        in_specs=[VMEM] * len(blocks),
        out_specs=VMEM,
        compiler_params=params(4),
        name="pack",
    )(*blocks)


def tile_at(index):
    return pl.ds(pl.multiple_of(index * TILE, TILE), TILE)


def gate_up_kernel(
    devices,
    a_ref,
    c_ref,
    d_ref,
    e_ref,
    u_hbm,
    w_hbm,
    gate_ref,
    part_ref,
    rows_ref,
    far_ref,
    total_ref,
    buf,
    sems,
    far_sems,
):
    nx = grid_of(devices)[1]
    slots = buf.shape[0]
    left = u_hbm.shape[0] // BAND

    def streamed(j):
        slot = lax.rem(j, slots)
        return row_copy(u_hbm, buf.at[slot], sems.at[slot], j * BAND)

    for j in range(min(slots, left)):
        streamed(j).start()
    far_tiles = far_ref.shape[0] // TILE
    per_step = -(-far_tiles // (left - 1))
    far_base = half_base(devices, False, far_ref.shape[1])

    def far_copy(i):
        at = tile_at(i)
        return pltpu.make_async_copy(
            w_hbm.at[at, pl.ds(far_base, far_ref.shape[1])], far_ref.at[at], far_sems.at[i]
        )

    me = lax.axis_index(AXIS)
    my_z, my_x = me // nx, me % nx
    per = a_ref.shape[1]
    for bits, near, far in (
        (0, a_ref[0], a_ref[2]),
        (1, c_ref[0], c_ref[2]),
        (2, a_ref[1], d_ref[...]),
        (3, c_ref[1], e_ref[...]),
    ):
        here, there = near.astype(F32), far.astype(F32)
        pair = [jnp.where(my_x == 0, here, there), jnp.where(my_x == 0, there, here)]
        at = pl.ds(pl.multiple_of((my_z ^ bits) * (2 * per), 2 * per), 2 * per)
        rows_ref[at, :] = jnp.concatenate(pair, axis=0).astype(BF16)

    def add(at, weight, kind):
        total_ref[kind] += jnp.dot(rows_ref[:, at], weight, preferred_element_type=F32)

    total_ref[...] = jnp.zeros_like(total_ref)

    def band(j):
        return pl.ds(pl.multiple_of(j * BAND, BAND), BAND)

    @pl.when(me >= 0)
    def _():
        add(band(0), gate_ref[band(0), :], 0)

    def step(j, _):
        streamed(j).wait()
        add(band(j), buf[lax.rem(j, slots)], 1)
        add(band(j + 1), gate_ref[band(j + 1), :], 0)

        @pl.when(j + slots < left)
        def _():
            streamed(j + slots).start()

        for k in range(per_step):

            @pl.when(j * per_step + k < far_tiles)
            def _(k=k):
                far_copy(j * per_step + k).start()

        return 0

    lax.fori_loop(0, left - 1, step, 0)
    streamed(left - 1).wait()
    add(band(left - 1), buf[(left - 1) % slots], 1)
    part_ref[...] = total_ref[...].astype(BF16)
    for i in range(far_tiles):
        far_copy(i).wait()


def gate_up(blocks, gate_weight, up_weight, down_weight, devices, ahead):
    total = devices * blocks[0].shape[1]
    features, columns = gate_weight.shape
    slots = 3
    return pl.pallas_call(
        functools.partial(gate_up_kernel, devices),
        out_shape=(
            jax.ShapeDtypeStruct((2, total, columns), BF16),
            jax.ShapeDtypeStruct((total, features), BF16),
            pltpu.VMEM((ahead, features // 2), BF16),
        ),
        in_specs=[VMEM] * 4 + [HBM] * 2 + [VMEM],
        out_specs=(VMEM, VMEM, VMEM),
        scratch_shapes=[
            pltpu.VMEM((2, total, columns), F32),
            pltpu.VMEM((slots, BAND, columns), BF16),
            pltpu.SemaphoreType.DMA((slots,)),
            pltpu.SemaphoreType.DMA((ahead // TILE,)),
        ],
        compiler_params=params(GATE_MIB),
        cost_estimate=cost(4 * total * features * columns, 4 * features * columns),
        name="gate_up",
    )(
        *blocks,
        in_hbm(up_weight),
        in_hbm(down_weight),
        in_vmem(gate_weight),
    )


def down_copies(w_hbm, base, held_ref, sems, first):
    rows, wide = held_ref.shape
    return [
        pltpu.make_async_copy(
            w_hbm.at[pl.ds(first + i * TILE, TILE), pl.ds(base, wide)],
            held_ref.at[pl.ds(i * TILE, TILE)],
            sems.at[i],
        )
        for i in range(rows // TILE)
    ]


def half_base(devices, mine, half):
    my_x = lax.axis_index(AXIS) % grid_of(devices)[1]
    return pl.multiple_of((my_x if mine else 1 - my_x) * half, half)


def quarter_base(devices, far, quarter, wide):
    my_x = lax.axis_index(AXIS) % grid_of(devices)[1]
    half = 1 - my_x if far else my_x
    return pl.multiple_of((2 * half + quarter) * wide, wide)


def pick(row_ref, capacity, first_slot, slots):
    row = row_ref[...]
    total = row.shape[1]
    down = lax.broadcasted_iota(jnp.int32, (total, total), 0)
    across = lax.broadcasted_iota(jnp.int32, (total, total), 1)
    diagonal = jnp.where(down == across, row, 0).astype(F32).astype(BF16)
    column = jnp.dot(diagonal, jnp.ones((total, total), BF16), preferred_element_type=F32)
    earlier = (column == row.astype(F32)) & (down < across)
    rank = jnp.sum(earlier.astype(F32), axis=0, keepdims=True).astype(jnp.int32)
    slot = first_slot + lax.broadcasted_iota(jnp.int32, (slots, total), 0)
    return (slot == row * capacity + rank).astype(F32).astype(BF16)


def prepare_kernel(devices, capacity, first, after_ref, row_ref, w_hbm, far_ref, chosen_ref, sems):
    base = half_base(devices, False, far_ref.shape[1])
    copies = down_copies(w_hbm, base, far_ref, sems, first)
    for c in copies:
        c.start()
    nz, nx = grid_of(devices)
    my_z = lax.axis_index(AXIS) // nx
    slots = chosen_ref.shape[0] // nz
    for i, bits in enumerate(ORDER):
        chosen_ref[i * slots : (i + 1) * slots, :] = pick(
            row_ref, capacity, (my_z ^ bits) * slots, slots
        )
    for c in copies:
        c.wait()


def prepare(after, row, down_weight, devices, capacity, first):
    columns, features = down_weight.shape
    total = row.shape[1]
    rows = columns - first
    return pl.pallas_call(
        functools.partial(prepare_kernel, devices, capacity, first),
        out_shape=(
            pltpu.VMEM((rows, features // 2), BF16),
            jax.ShapeDtypeStruct((devices * 2 * capacity, total), BF16),
        ),
        in_specs=[ANY, VMEM, HBM],
        out_specs=(VMEM, VMEM),
        scratch_shapes=[pltpu.SemaphoreType.DMA((rows // TILE,))],
        compiler_params=params(2),
        cost_estimate=cost(0, rows * features),
        name="prepare",
    )(after, row, in_hbm(down_weight))


def down_kernel(devices, far, quarter, held_count, aheads, *refs):
    refs = list(refs)

    def take(count):
        return [refs.pop(0) for _ in range(count)]

    first_call = far and quarter == 0
    sources = take(2 if first_call else 1)
    arrived_ref, chosen_ref = (None, None) if far else take(2)
    held_refs = take(held_count)
    (w_hbm,) = take(1)
    out_refs = take(1 if far else 2)
    next_refs = take(len(aheads))
    (hidden_ref,) = take(1) if first_call else sources
    (total_ref,) = take(1)
    wide = total_ref.shape[1]
    ahead = []
    for (their, start, _), ref, sems in zip(aheads, next_refs, take(len(aheads))):
        ahead += down_copies(w_hbm, quarter_base(devices, False, their, wide), ref, sems, start)
    for c in ahead:
        c.start()
    if first_call:
        own_ref, other_ref = sources

        @pl.when(lax.axis_index(AXIS) >= 0)
        def _():
            gate = own_ref[0].astype(F32) + other_ref[0].astype(F32)
            up = own_ref[1].astype(F32) + other_ref[1].astype(F32)
            hidden_ref[...] = (gate / (1.0 + jnp.exp(-gate)) * up).astype(BF16)

    if far:
        total_ref[...] = jnp.zeros_like(total_ref)
    else:
        total_ref[...] = arrived_ref[...].astype(F32)
    @pl.when(lax.axis_index(AXIS) >= 0)
    def _():
        start = 0
        for held_ref in held_refs:
            stop = start + held_ref.shape[0]
            at = slice(quarter * wide, (quarter + 1) * wide) if far else slice(None)
            total_ref[...] += jnp.dot(
                hidden_ref[:, start:stop], held_ref[:, at], preferred_element_type=F32
            )
            start = stop

    rounded = total_ref[...].astype(BF16)
    if far:
        out_refs[0][...] = rounded
    else:
        slots = out_refs[0].shape[0]
        for i, ref in enumerate(out_refs):
            chosen = chosen_ref[i * slots : (i + 1) * slots]
            ref[...] = jnp.dot(chosen, rounded, preferred_element_type=F32).astype(BF16)
    for c in ahead:
        c.wait()


def down(sources, held, down_weight, devices, far, quarter, aheads=()):
    total = sources[0].shape[-2]
    columns, features = down_weight.shape
    wide = features // 4
    if far:
        out_shape = [jax.ShapeDtypeStruct((total, wide), BF16)]
    else:
        out_shape = [jax.ShapeDtypeStruct((sources[2].shape[0] // 2, wide), BF16)] * 2
    out_shape += [pltpu.VMEM((rows, wide), BF16) for _, _, rows in aheads]
    if far and quarter == 0:
        out_shape.append(jax.ShapeDtypeStruct((total, columns), BF16))
    return pl.pallas_call(
        functools.partial(down_kernel, devices, far, quarter, len(held), aheads),
        out_shape=tuple(out_shape),
        in_specs=[VMEM] * (len(sources) + len(held)) + [HBM],
        out_specs=tuple(VMEM for _ in out_shape),
        scratch_shapes=[pltpu.VMEM((total, wide), F32)]
        + [pltpu.SemaphoreType.DMA((rows // TILE,)) for _, _, rows in aheads],
        compiler_params=params(6),
        cost_estimate=COST,
        name="down_far" if far else "down_near",
    )(*sources, *(in_vmem(h) for h in held), in_hbm(down_weight))


def add_kernel(keep_ref, came_ref, own_ref, send_ref):
    slots = own_ref.shape[0]
    total = keep_ref[...].astype(F32) + came_ref[...].astype(F32)
    own_ref[...] = total[:slots]
    send_ref[...] = total[slots:].astype(BF16)


def add(keep, came):
    slots, wide = keep.shape
    return pl.pallas_call(
        add_kernel,
        out_shape=(
            jax.ShapeDtypeStruct((slots // 2, wide), F32),
            jax.ShapeDtypeStruct((slots // 2, wide), BF16),
        ),
        in_specs=[VMEM, VMEM],
        out_specs=(VMEM, VMEM),
        compiler_params=params(4),
        name="add",
    )(keep, came)


def finish_kernel(devices, chosen_ref, rows_ref, *refs):
    own_refs, came_refs, (keep_ref, send_ref) = refs[:2], refs[2:4], refs[4:]
    my_x = lax.axis_index(AXIS) % grid_of(devices)[1]
    slots, wide = own_refs[0].shape
    half = slots // 2
    for quarter, (own_ref, came_ref) in enumerate(zip(own_refs, came_refs)):
        mixed = rows_ref[:, pl.ds(quarter_base(devices, False, quarter, wide), wide)]
        done = jnp.dot(chosen_ref[:slots], mixed, preferred_element_type=F32)
        done = done + (own_ref[...] + came_ref[...].astype(F32))
        first, second = done[:half], done[half:]
        at = slice(quarter * wide, (quarter + 1) * wide)
        keep_ref[:, at] = jnp.where(my_x == 0, first, second).astype(BF16)
        send_ref[:, at] = jnp.where(my_x == 0, second, first).astype(BF16)


def finish(chosen, rows, own, came, devices):
    slots, wide = own[0].shape
    shape = jax.ShapeDtypeStruct((slots // 2, 2 * wide), BF16)
    return pl.pallas_call(
        functools.partial(finish_kernel, devices),
        out_shape=(shape, shape),
        in_specs=[VMEM] * 6,
        out_specs=(VMEM, VMEM),
        compiler_params=params(6),
        name="finish",
    )(chosen, rows, *own, *came)


def join_kernel(nx, keep_ref, other_ref, out_ref):
    my_x = lax.axis_index(AXIS) % nx
    width = keep_ref.shape[1]
    out_ref[:, :width] = jnp.where(my_x == 0, keep_ref[...], other_ref[...])
    out_ref[:, width:] = jnp.where(my_x == 0, other_ref[...], keep_ref[...])


def join(keep, other, devices):
    slots, width = keep.shape
    return pl.pallas_call(
        functools.partial(join_kernel, grid_of(devices)[1]),
        out_shape=jax.ShapeDtypeStruct((slots, 2 * width), BF16),
        in_specs=[VMEM, VMEM],
        out_specs=VMEM,
        compiler_params=params(8),
        name="join_halves",
    )(keep, other)


def slot_positions(column, destinations, capacity):
    onehot = (column[:, None] == jnp.arange(destinations, dtype=jnp.int32)[None, :]).astype(
        jnp.int32
    )
    before = jnp.cumsum(onehot, axis=0) - onehot
    slot_rank = jnp.sum(before * onehot, axis=1)
    return column * capacity + slot_rank


def plain(mixed_rows, target, gate_weight, up_weight, down_weight, devices):
    rows_dev, features = mixed_rows.shape
    me = lax.axis_index(AXIS)
    gathered = lax.all_gather(mixed_rows, AXIS, axis=0, tiled=True)
    mine = jnp.stack(
        [
            jnp.dot(gathered, gate_weight, preferred_element_type=F32),
            jnp.dot(gathered, up_weight, preferred_element_type=F32),
        ]
    )
    other = lax.ppermute(mine.astype(BF16), "ffn", [(0, 1), (1, 0)])
    gate_sum, up_sum = mine + other.astype(F32)
    hidden = (jax.nn.silu(gate_sum) * up_sum).astype(BF16)
    down = jnp.dot(hidden, down_weight, preferred_element_type=F32)
    share = features // devices
    landed = lax.all_to_all(
        jnp.moveaxis(down.astype(BF16).reshape(-1, devices, share), 1, 0), AXIS, 0, 0
    )
    summed = jnp.sum(landed.astype(F32), axis=0)
    mixed_share = lax.dynamic_slice_in_dim(gathered, me * share, share, axis=1)
    finished = (mixed_share.astype(F32) + summed).astype(BF16)
    slot_count = 2 * devices * rows_dev
    position = slot_positions(target[:, 0], 2 * devices, rows_dev)
    chosen = (jnp.arange(slot_count, dtype=jnp.int32)[:, None] == position[None, :]).astype(BF16)
    slots = jnp.dot(chosen, finished, preferred_element_type=F32).astype(BF16)
    slots = slots.reshape(devices, 2 * rows_dev, share)
    mine_out = lax.all_to_all(slots, AXIS, split_axis=0, concat_axis=0)
    return jnp.moveaxis(mine_out, 0, 1).reshape(2 * rows_dev, features)


def local(
    queries,
    cache_keys,
    stored_value_cache,
    lengths,
    residual,
    target,
    gate_weight,
    up_weight,
    down_weight,
):
    devices = lax.axis_size(AXIS)
    nz, nx = grid_of(devices)
    capacity = cache_keys.shape[0]
    columns, features = down_weight.shape
    fits = nz == 4 and nx == 2 and columns % TILE == 0 and features % (8 * BAND) == 0
    mixed_rows = attend(queries, cache_keys, stored_value_cache, lengths, residual, up_weight)
    if not fits:
        return plain(mixed_rows, target, gate_weight, up_weight, down_weight, devices)

    two = lax.ppermute(mixed_rows, AXIS, swap_z(devices, 2))
    side = lax.ppermute(mixed_rows, AXIS, swap_x(devices))
    e = lax.ppermute(mixed_rows, AXIS, swap_x(devices, 3))
    a = pack(mixed_rows, two, side)
    c = lax.ppermute(a, AXIS, swap_z(devices, 1))
    d = lax.ppermute(two, AXIS, swap_x(devices))
    tiles = columns // TILE
    far_cut = 10 * tiles // 13 * TILE
    cut = 8 * tiles // 13 * TILE, 7 * tiles // 13 * TILE
    part, rows, far_a = gate_up(
        (a, c, d, e), gate_weight, up_weight, down_weight, devices, far_cut
    )
    other = lax.ppermute(part, "ffn", [(0, 1), (1, 0)])
    far_b, chosen = prepare(
        part, target.reshape(1, -1), down_weight, devices, capacity, far_cut
    )
    held_far = far_a, far_b

    far, near_a, hidden = down(
        (part, other), held_far, down_weight, devices, True, 0, ((0, 0, cut[0]),)
    )
    arrived = [lax.ppermute(far, AXIS, swap_x(devices))]
    far, near_b, near_c = down(
        (hidden,),
        held_far,
        down_weight,
        devices,
        True,
        1,
        ((0, cut[0], columns - cut[0]), (1, 0, cut[1])),
    )
    arrived.append(lax.ppermute(far, AXIS, swap_x(devices)))
    keep_a, send_a, near_d = down(
        (hidden, arrived[0], chosen),
        (near_a, near_b),
        down_weight,
        devices,
        False,
        0,
        ((1, cut[1], columns - cut[1]),),
    )
    came_a = lax.ppermute(send_a, AXIS, swap_z(devices, 1))
    keep_b, send_b = down(
        (hidden, arrived[1], chosen), (near_c, near_d), down_weight, devices, False, 1
    )
    came_b = lax.ppermute(send_b, AXIS, swap_z(devices, 1))
    own, came = [], []
    for keep, arrived in ((keep_a, came_a), (keep_b, came_b)):
        mine, send = add(keep, arrived)
        own.append(mine)
        came.append(lax.ppermute(send, AXIS, swap_z(devices, 2)))
    keep, send = finish(chosen, rows, own, came, devices)
    return join(keep, lax.ppermute(send, AXIS, swap_x(devices)), devices)


def solution(mesh):
    return jax.shard_map(
        local,
        mesh=mesh,
        in_specs=(
            P(("parts", "attn"), "ffn", None),
            P(("parts", "attn"), None, "ffn", None),
            P(("parts", "attn"), None, "ffn", None),
            P(("parts", "attn")),
            P(("parts", "attn"), "ffn"),
            P("parts", None),
            P("ffn", "attn"),
            P("ffn", "attn"),
            P("attn", "ffn"),
        ),
        out_specs=P(("parts", "attn"), "ffn"),
        check_vma=False,
    )
```
